32 devices in a mesh: dp: 4 (over z), loop: 8 (over y, x, core).
Axes of the slice: x: 2, y: 2, z: 4, core: 2. Of those that a mesh axis runs over, the one named last changes fastest.
Arguments:
- tokens: bfloat16 [8192, 2048], P('loop', 'dp'), may hold values from -6 to 6
- cotangent: bfloat16 [8192, 2048], P('loop', 'dp'), may hold values from -6 to 6
- up_first: bfloat16 [128, 16, 128], P('loop'), may hold values from -0.5 to 0.5
- up_second: bfloat16 [16, 128, 128], P('loop'), may hold values from -0.5 to 0.5
- down_first: bfloat16 [16, 128, 128], P('loop'), may hold values from -0.5 to 0.5
- down_second: bfloat16 [128, 16, 128], P('loop'), may hold values from -1 to 1
- perm_up: int32 [128], replicated, may hold values from 0 to 127, each once
- perm_down: int32 [128], replicated, may hold values from 0 to 127, each once
Outputs:
- mixed: bfloat16 [8192, 2048], P('loop', 'dp')
- grad_tokens: bfloat16 [8192, 2048], P('loop', 'dp')
- grad_up_first: float32 [128, 16, 128], P('loop')
- grad_up_second: float32 [16, 128, 128], P('loop')
- grad_down_first: float32 [16, 128, 128], P('loop')
- grad_down_second: float32 [128, 16, 128], P('loop')
The draws below stay inside these ranges and needn't reach their ends.
Inputs may be any that keep to these rules, and one draw needn't show every extreme that they name: perm_up holds each of 0 to 127 once. perm_down holds each of 0 to 127 once.
All inputs are finite; a program needn't handle non-finite values.
Results may differ from the reference program's by a relative error of at most 0.01.
Values may be sent and summed in bfloat16 or wider, within the bound.
No kernel may reach another device: no remote copies, remote signals or barrier semaphores. Data moves between devices by JAX's collectives and lax.ppermute only.
A program may use at most 64 MiB of HBM per device.

```python
import math
import jax
import jax.numpy as jnp
from jax import lax

D = 8192
BLK = 128
TOKENS = 2048
BD = 16
GRP = 2
PB = 16
N_LOOP = 8


def levels(rng, dims, shards, least, largest):
    level = 1.0
    for axis_at, parts in shards:
        steps = jax.random.uniform(jax.random.fold_in(jax.random.fold_in(rng, 6), axis_at), (parts,), jnp.float32, least / len(shards), largest / len(shards))
        level = level * jnp.repeat(jnp.exp(steps), dims[axis_at] // parts).reshape((-1,) + (1,) * (len(dims) - 1 - axis_at))
    return level


def gaussian(own_key, extent, scale, limit, shards=(), held_as=jnp.bfloat16):
    loudness = levels(own_key, extent, shards, -0.22, 0.18) if shards else 1.0
    entries = jax.random.normal(own_key, extent, jnp.float32) * scale * loudness
    return jnp.minimum(jnp.maximum(entries, -limit), limit).astype(held_as)


def setup_inputs(seed: int = 0) -> dict:
    splits = jax.random.split(jax.random.key(seed), 9)
    return {
        "tokens": gaussian(splits[0], (D, TOKENS), 1.0, 6.0, ((0, 8), (1, 4))),
        "cotangent": gaussian(splits[1], (D, TOKENS), 1.0, 6.0, ((0, 8), (1, 4))),
        "up_first": gaussian(splits[2], (BLK, BD, BLK), BLK ** -0.5, 0.5, ((0, 8),)),
        "up_second": gaussian(splits[3], (BD, BLK, BLK), BLK ** -0.5, 0.5, ((0, 8),)),
        "down_first": gaussian(splits[4], (BD, BLK, BLK), BLK ** -0.5, 0.5, ((0, 8),)),
        "down_second": gaussian(splits[5], (BLK, BD, BLK), (GRP * BD) ** -0.5, 1.0, ((0, 8),)),
        "perm_up": jax.random.permutation(splits[6], BLK).astype(jnp.int32),
        "perm_down": jax.random.permutation(splits[7], BLK).astype(jnp.int32),
    }


def gelu_parts(pre_act):
    cumul = 0.5 * (1.0 + jax.scipy.special.erf(pre_act * (1.0 / math.sqrt(2.0))))
    slope = cumul + pre_act * jnp.exp(-0.5 * pre_act * pre_act) * (1.0 / math.sqrt(2.0 * math.pi))
    return (pre_act * cumul, slope)

def inverse_of(permute):
    return jnp.zeros(permute.shape, jnp.int32).at[permute].set(jnp.arange(permute.shape[0], dtype=jnp.int32))

def to_blocks(field):
    width = field.shape[1]
    shaped = field.reshape(N_LOOP // 2, 2, PB, BLK // 2, width).transpose(0, 2, 1, 3, 4)
    return shaped.reshape(D // BLK, BLK, width)

def from_blocks(field):
    width = field.shape[2]
    shaped = field.reshape(N_LOOP // 2, PB, 2, BLK // 2, width).transpose(0, 2, 1, 3, 4)
    return shaped.reshape(D, width)

def reference(tokens, cotangent, up_first, up_second, down_first, down_second, perm_up, perm_down):
    wide = jnp.float32
    narrow = jnp.bfloat16
    blocks = D // BLK
    width = min(1024, TOKENS)
    pieces_count = TOKENS // width
    first_up = up_first.astype(wide).reshape(blocks, GRP, BD, BLK)
    second_up = up_second.astype(wide)
    first_down = down_first.astype(wide)
    last_down = down_second.astype(wide).reshape(blocks, GRP, BD, BLK)
    inverse_up = inverse_of(perm_up)
    inverse_down = inverse_of(perm_down)

    def one_block(carry, pieces):
        x_block, d_block = pieces
        x_wide = to_blocks(x_block.astype(wide))
        d_wide = to_blocks(d_block.astype(wide))
        hidden_one = jnp.einsum('egbi,eit->egbt', first_up, x_wide).reshape(BLK, BD, width).astype(narrow)
        permuted = jnp.take(hidden_one, perm_up, axis=0)
        pre_act = jnp.einsum('boa,abt->bot', second_up, permuted.astype(wide))
        gelu_val, slope = gelu_parts(pre_act)
        activated = gelu_val.astype(narrow)
        mixed_cols = jnp.einsum('bpo,bot->pbt', first_down, activated.astype(wide)).astype(narrow)
        back_rows = jnp.take(mixed_cols, perm_down, axis=0)
        rows_wide = back_rows.astype(wide).reshape(blocks, GRP, BD, width)
        branch_out = from_blocks(jnp.einsum('egbo,egbt->eot', last_down, rows_wide))
        mixed = (x_block.astype(wide) + branch_out).astype(narrow)
        grad_rows = jnp.einsum('egbo,eot->egbt', last_down, d_wide).reshape(BLK, BD, width).astype(narrow)
        g_down_second = jnp.einsum('egbt,eot->egbo', rows_wide, d_wide).reshape(BLK, BD, BLK)
        grad_mixed = jnp.take(grad_rows, inverse_down, axis=0).astype(wide)
        grad_act = jnp.einsum('bpo,pbt->bot', first_down, grad_mixed)
        g_down_first = jnp.einsum('pbt,bot->bpo', grad_mixed, activated.astype(wide))
        grad_pre = (grad_act * slope).astype(narrow).astype(wide)
        g_up_second = jnp.einsum('bot,abt->boa', grad_pre, permuted.astype(wide))
        grad_perm = jnp.einsum('boa,bot->abt', second_up, grad_pre).astype(narrow)
        grad_hidden = jnp.take(grad_perm, inverse_up, axis=0).astype(wide).reshape(blocks, GRP, BD, width)
        g_up_first = jnp.einsum('egbt,eit->egbi', grad_hidden, x_wide).reshape(BLK, BD, BLK)
        grad_branch = from_blocks(jnp.einsum('egbi,egbt->eit', first_up, grad_hidden))
        grad_tokens = (d_block.astype(wide) + grad_branch).astype(narrow)
        carry = (carry[0] + g_up_first, carry[1] + g_up_second, carry[2] + g_down_first, carry[3] + g_down_second)
        return (carry, (mixed, grad_tokens))
    start = (jnp.zeros((BLK, BD, BLK), wide), jnp.zeros((BD, BLK, BLK), wide), jnp.zeros((BD, BLK, BLK), wide), jnp.zeros((BLK, BD, BLK), wide))
    x_stack = tokens.reshape(D, pieces_count, width).transpose(1, 0, 2)
    d_stack = cotangent.reshape(D, pieces_count, width).transpose(1, 0, 2)
    totals, outputs = lax.scan(one_block, start, (x_stack, d_stack))
    scale = 1.0 / math.sqrt(TOKENS)
    mixed = outputs[0].transpose(1, 0, 2).reshape(D, TOKENS)
    grad_tokens = outputs[1].transpose(1, 0, 2).reshape(D, TOKENS)
    return (mixed, grad_tokens, totals[0] * scale, totals[1] * scale, totals[2] * scale, totals[3] * scale)
```

```python
import math

import jax
import jax.numpy as jnp
from jax import lax
from jax.experimental import pallas as pl
from jax.experimental.pallas import tpu as pltpu
from jax.sharding import PartitionSpec as P


def from_partner(value, axis, apart):
    mask = 2**apart
    pairs = [(source, source ^ mask) for source in range(lax.axis_size(axis))]
    return lax.ppermute(value, axis, pairs)


def gelu_parts(pre_act):
    cumul = 0.5 * (1.0 + jax.scipy.special.erf(pre_act * (1.0 / math.sqrt(2.0))))
    slope = cumul + pre_act * jnp.exp(-0.5 * pre_act * pre_act) * (1.0 / math.sqrt(2.0 * math.pi))
    return (pre_act * cumul, slope)


def inverse_of(permute):
    return (
        jnp.zeros(permute.shape, jnp.int32)
        .at[permute]
        .set(jnp.arange(permute.shape[0], dtype=jnp.int32))
    )


def pair_total(contrib, half_width, parity):
    pair_blocks = contrib.shape[0]
    tok_count = contrib.shape[2]
    leaving = lax.dynamic_slice_in_dim(contrib, (1 - parity) * half_width, half_width, 1)
    other = from_partner(leaving.astype(jnp.bfloat16), "loop", 0).astype(leaving.dtype)
    mine = lax.dynamic_slice_in_dim(contrib, parity * half_width, half_width, 1) + other
    return mine.reshape(pair_blocks * half_width, tok_count)


def plain_shards(tokens, cotangent, up_first, up_second, down_first, down_second, perm_up, perm_down):
    wide = jnp.float32
    narrow = jnp.bfloat16
    feature_rows = tokens.shape[0]
    tok_count = tokens.shape[1]
    local_rows = up_first.shape[0]
    block = up_first.shape[2]
    half_width = block // 2
    pair_blocks = 2 * feature_rows // block
    group = 2 * local_rows // pair_blocks
    parity = lax.axis_index("loop") % 2
    other_x, other_d = from_partner((tokens, cotangent), "loop", 0)
    low_x = jnp.where(parity == 0, tokens, other_x)
    high_x = jnp.where(parity == 0, other_x, tokens)
    low_d = jnp.where(parity == 0, cotangent, other_d)
    high_d = jnp.where(parity == 0, other_d, cotangent)
    x_blocks = jnp.concatenate(
        [
            low_x.reshape(pair_blocks, half_width, tok_count),
            high_x.reshape(pair_blocks, half_width, tok_count),
        ],
        1,
    )
    d_blocks = jnp.concatenate(
        [
            low_d.reshape(pair_blocks, half_width, tok_count),
            high_d.reshape(pair_blocks, half_width, tok_count),
        ],
        1,
    )
    row_block = (parity * local_rows + jnp.arange(local_rows, dtype=jnp.int32)) // group
    picker = row_block[:, None] == jnp.arange(pair_blocks, dtype=jnp.int32)[None, :]
    picker_narrow = picker.astype(narrow)
    picker_wide = picker.astype(wide)
    x_rows = jnp.einsum("am,mit->ait", picker_narrow, x_blocks, preferred_element_type=wide).astype(
        narrow
    )
    d_rows = jnp.einsum("am,mit->ait", picker_narrow, d_blocks, preferred_element_type=wide).astype(
        narrow
    )
    inverse_up = inverse_of(perm_up)
    inverse_down = inverse_of(perm_down)
    hidden_one = jnp.einsum("abi,ait->abt", up_first, x_rows, preferred_element_type=wide).astype(
        narrow
    )
    permuted = jnp.take(
        lax.all_to_all(hidden_one, "loop", split_axis=1, concat_axis=0, tiled=True), perm_up, axis=0
    )
    pre_act = jnp.einsum("boa,abt->bot", up_second, permuted, preferred_element_type=wide)
    gelu_val, slope = gelu_parts(pre_act)
    activated = gelu_val.astype(narrow)
    mixed_cols = jnp.einsum(
        "bpo,bot->pbt", down_first, activated, preferred_element_type=wide
    ).astype(narrow)
    leaving = jnp.take(mixed_cols, perm_down, axis=0)
    back_rows = lax.all_to_all(leaving, "loop", split_axis=0, concat_axis=1, tiled=True)
    back_rows, permuted, activated, slope = (back_rows, permuted, activated, slope)
    out_rows = jnp.einsum("abo,abt->aot", down_second, back_rows, preferred_element_type=wide)
    out_contrib = jnp.einsum("am,aot->mot", picker_wide, out_rows, precision=lax.Precision.HIGHEST)
    branch_out = pair_total(out_contrib, half_width, parity)
    mixed = (tokens.astype(wide) + branch_out).astype(narrow)
    scale = 1.0 / math.sqrt(lax.axis_size("dp") * tok_count)
    grad_rows = jnp.einsum("abo,aot->abt", down_second, d_rows, preferred_element_type=wide).astype(
        narrow
    )
    g_down_second = jnp.einsum("abt,aot->abo", back_rows, d_rows, preferred_element_type=wide)
    grad_cols = lax.all_to_all(grad_rows, "loop", split_axis=1, concat_axis=0, tiled=True)
    grad_mixed = jnp.take(grad_cols, inverse_down, axis=0)
    grad_act = jnp.einsum("bpo,pbt->bot", down_first, grad_mixed, preferred_element_type=wide)
    g_down_first = jnp.einsum("pbt,bot->bpo", grad_mixed, activated, preferred_element_type=wide)
    grad_pre = (grad_act * slope).astype(narrow)
    g_up_second = jnp.einsum("bot,abt->boa", grad_pre, permuted, preferred_element_type=wide)
    grad_perm = jnp.einsum("boa,bot->abt", up_second, grad_pre, preferred_element_type=wide).astype(
        narrow
    )
    grad_recv = jnp.take(grad_perm, inverse_up, axis=0)
    grad_hidden = lax.all_to_all(grad_recv, "loop", split_axis=0, concat_axis=1, tiled=True)
    g_up_first = jnp.einsum("abt,ait->abi", grad_hidden, x_rows, preferred_element_type=wide)
    g_up_first, g_up_second, g_down_first, g_down_second = (
        lax.psum(g_up_first.astype(jnp.bfloat16), "dp").astype(jnp.float32),
        lax.psum(g_up_second.astype(jnp.bfloat16), "dp").astype(jnp.float32),
        lax.psum(g_down_first.astype(jnp.bfloat16), "dp").astype(jnp.float32),
        lax.psum(g_down_second.astype(jnp.bfloat16), "dp").astype(jnp.float32),
    )
    grad_rows_in = jnp.einsum("abi,abt->ait", up_first, grad_hidden, preferred_element_type=wide)
    grad_contrib = jnp.einsum(
        "am,ait->mit", picker_wide, grad_rows_in, precision=lax.Precision.HIGHEST
    )
    grad_branch = pair_total(grad_contrib, half_width, parity)
    grad_tokens = (cotangent.astype(wide) + grad_branch).astype(narrow)
    return (
        mixed,
        grad_tokens,
        g_up_first * scale,
        g_up_second * scale,
        g_down_first * scale,
        g_down_second * scale,
    )


VMEM_LIMIT = 48 * 2**20


def dot(left, right, left_dim=1, right_dim=0):
    return lax.dot_general(
        left, right, (((left_dim,), (right_dim,)), ((), ())), preferred_element_type=jnp.float32
    )


def call(body, outs, *args):
    whole = pl.BlockSpec(memory_space=pltpu.VMEM)
    return pl.pallas_call(
        body,
        out_shape=outs,
        in_specs=[whole] * len(args),
        out_specs=jax.tree.map(lambda _: whole, outs),
        compiler_params=pltpu.CompilerParams(vmem_limit_bytes=VMEM_LIMIT),
    )(*args)


def own_first(weights, parity):
    wide = weights.astype(jnp.float32)
    half = wide.shape[1] // 2
    turned = pltpu.roll(wide, half, 1)
    return jnp.where(parity == 0, wide, turned)


def block_rows(own_ref, other_ref, block, half, parity, count):
    start = pl.multiple_of(parity * (count * half) + block * half, half)
    return jnp.concatenate(
        [own_ref[pl.ds(start, half), :], other_ref[block * half : (block + 1) * half, :]], 0
    )


def grid_order(me, loops, rows, cols, sent_dim):
    size = loops * rows * cols
    sent = lax.broadcasted_iota(jnp.int32, (size, size), sent_dim)
    kept = lax.broadcasted_iota(jnp.int32, (size, size), 1 - sent_dim)
    device = (sent // (rows * cols)) ^ me
    col = device * cols + (sent // rows) % cols
    return (kept == (sent % rows) * (loops * cols) + col).astype(jnp.bfloat16)


def first_rows(loops, rows, cols, half):
    narrow = jnp.bfloat16

    def body(tok_ref, x_ref, cot_ref, d_ref, up_ref, down_ref, *rest):
        outs, (hid_ref, grad_ref) = rest[:loops], rest[loops:]
        me = lax.axis_index("loop")
        parity = me % 2
        count = x_ref.shape[0] // half
        high = up_ref.shape[0] // count
        up = own_first(up_ref[...], parity).astype(narrow)
        down = own_first(down_ref[...], parity).astype(narrow)
        for e in range(count):
            part = slice(e * high, (e + 1) * high)
            x_rows = block_rows(tok_ref, x_ref, e, half, parity, count)
            d_rows = block_rows(cot_ref, d_ref, e, half, parity, count)
            hid_ref[part, :] = dot(up[part], x_rows).astype(narrow)
            grad_ref[part, :] = dot(down[part], d_rows).astype(narrow)
        order = grid_order(me, loops, rows, cols, 0)
        unit = rows * cols
        for q, ref in enumerate((hid_ref, grad_ref)):
            sent = dot(order, ref[...]).astype(narrow)
            for k in range(loops):
                outs[k][q * unit : (q + 1) * unit, :] = sent[k * unit : (k + 1) * unit]

    return body


def columns(loops, rows, cols):
    narrow = jnp.bfloat16

    def body(*refs):
        bufs, rest = refs[:loops], refs[loops:]
        up_ref, down_ref, perm_up_ref, perm_down_ref = rest[:4]
        outs, grads_ref = rest[4 : 4 + loops], rest[4 + loops]
        me = lax.axis_index("loop")
        size = loops * rows
        unit = rows * cols
        lead = lax.broadcasted_iota(jnp.int32, (size, size), 0)
        lane = lax.broadcasted_iota(jnp.int32, (size, size), 1)
        row = ((lead // rows) ^ me) * rows + lead % rows
        take_up = (perm_up_ref[...] == row).astype(narrow)
        take_down = dot(
            (lane == row).astype(narrow), (perm_down_ref[...] == lead).astype(narrow), 1, 1
        ).astype(narrow)
        for b in range(cols):
            span = slice(b * size, (b + 1) * size)
            hid = jnp.concatenate([r[b * rows : (b + 1) * rows, :] for r in bufs], 0)
            grad = jnp.concatenate([r[unit + b * rows : unit + (b + 1) * rows, :] for r in bufs], 0)
            up = dot(up_ref[span, :], take_up, 1, 1).astype(narrow)
            down = dot(take_down, down_ref[span, :]).astype(narrow)
            gelu_val, slope = gelu_parts(dot(up, hid))
            activated = gelu_val.astype(narrow)
            back = dot(down, activated).astype(narrow)
            grad_pre = (dot(down, grad, 0, 0) * slope).astype(narrow)
            grad_back = dot(up, grad_pre, 0, 0).astype(narrow)
            for k in range(loops):
                part = slice(k * rows, (k + 1) * rows)
                outs[k][b * rows : (b + 1) * rows, :] = back[part]
                outs[k][unit + b * rows : unit + (b + 1) * rows, :] = grad_back[part]
            g_up = dot(grad_pre, hid, 1, 1).astype(narrow)
            g_down = dot(grad, activated, 1, 1).astype(narrow)
            grads_ref[span, :] = dot(g_up, take_up).astype(narrow)
            grads_ref[cols * size + b * size : cols * size + (b + 1) * size, :] = dot(
                take_down, g_down, 0, 0
            ).astype(narrow)

    return body


def row_grads(loops, rows, cols, half):
    narrow = jnp.bfloat16

    def body(*refs):
        bufs, rest = refs[:loops], refs[loops:]
        tok_ref, x_ref, cot_ref, d_ref, grads_ref, back_ref, grad_ref = rest
        me = lax.axis_index("loop")
        parity = me % 2
        unit = rows * cols
        count = x_ref.shape[0] // half
        size = loops * unit
        high = size // count
        order = grid_order(me, loops, rows, cols, 1)
        for q, ref in enumerate((back_ref, grad_ref)):
            sent = jnp.concatenate([r[q * unit : (q + 1) * unit, :] for r in bufs], 0)
            ref[...] = dot(order, sent).astype(narrow)
        g_up, g_down = [], []
        for e in range(count):
            part = slice(e * high, (e + 1) * high)
            x_rows = block_rows(tok_ref, x_ref, e, half, parity, count)
            d_rows = block_rows(cot_ref, d_ref, e, half, parity, count)
            g_up.append(dot(grad_ref[part, :], x_rows, 1, 1))
            g_down.append(dot(back_ref[part, :], d_rows, 1, 1))
        grads_ref[:size, :] = own_first(jnp.concatenate(g_up, 0), parity).astype(narrow)
        grads_ref[size:, :] = own_first(jnp.concatenate(g_down, 0), parity).astype(narrow)

    return body


def row_outputs(half):
    narrow = jnp.bfloat16

    def body(back_ref, grad_ref, tok_ref, x_ref, cot_ref, d_ref, up_ref, down_ref, *outs):
        mixed_ref, mixed_send_ref, grads_ref, grads_send_ref = outs
        parity = lax.axis_index("loop") % 2
        count = x_ref.shape[0] // half
        high = up_ref.shape[0] // count
        up = own_first(up_ref[...], parity).astype(narrow)
        down = own_first(down_ref[...], parity).astype(narrow)
        jobs = (
            (down, back_ref, tok_ref, x_ref, mixed_ref, mixed_send_ref),
            (up, grad_ref, cot_ref, d_ref, grads_ref, grads_send_ref),
        )
        for weights, rows_ref, own_ref, other_ref, kept_ref, sent_ref in jobs:
            for e in range(count):
                part = slice(e * high, (e + 1) * high)
                start = pl.multiple_of(parity * (count * half) + e * half, half)
                near = slice(e * half, (e + 1) * half)
                branch = dot(weights[part], rows_ref[part, :], 0, 0)
                own = own_ref[pl.ds(start, half), :].astype(jnp.float32)
                kept_ref[pl.ds(start, half), :] = (own + branch[:half]).astype(narrow)
                other = other_ref[near, :].astype(jnp.float32)
                sent_ref[near, :] = (other + branch[half:]).astype(narrow)

    return body


def add_shards(scale):
    def body(*refs):
        parts, outs = refs[:-2], refs[-2:]
        size = outs[0].shape[0]
        for at, out in enumerate(outs):
            span = slice(at * size, (at + 1) * size)
            total = parts[0][span, :].astype(jnp.float32)
            for part in parts[1:]:
                total = total + part[span, :].astype(jnp.float32)
            out[...] = total * scale

    return body


def exchange(bufs, axis):
    count = len(bufs)
    got = {
        k: lax.ppermute(bufs[k], axis, [(s, s ^ k) for s in range(count)])
        for k in range(count - 1, 0, -1)
    }
    return [bufs[0]] + [got[k] for k in range(1, count)]


def shards(tokens, cotangent, up_first, up_second, down_first, down_second, perm_up, perm_down):
    narrow = jnp.bfloat16
    loops, dps = lax.axis_size("loop"), lax.axis_size("dp")
    feature_rows, toks = tokens.shape
    rows, all_cols, block = up_first.shape
    cols = up_second.shape[0]
    half = block // 2
    group = 2 * rows // (2 * feature_rows // block)
    if loops > 8 or rows % 16 or rows % group or dps & (dps - 1):
        return plain_shards(
            tokens, cotangent, up_first, up_second, down_first, down_second, perm_up, perm_down
        )
    parity = lax.axis_index("loop") % 2
    kept = feature_rows // 2

    def partner_half(value):
        leaving = lax.dynamic_slice_in_dim(value, (1 - parity) * kept, kept, 0)
        return from_partner(leaving, "loop", 0)

    other_x, other_d = partner_half(tokens), partner_half(cotangent)
    up_rows = up_first.reshape(rows * all_cols, block)
    down_rows = down_second.reshape(rows * all_cols, block)
    buf = jax.ShapeDtypeStruct((2 * rows * cols, toks), narrow)
    whole = jax.ShapeDtypeStruct((rows * all_cols, toks), narrow)
    grads = jax.ShapeDtypeStruct((2 * rows * all_cols, block), narrow)
    unit = rows * cols

    def rows_call(body, outs, args, scratch):
        spec = pl.BlockSpec(memory_space=pltpu.VMEM)
        return pl.pallas_call(
            body,
            out_shape=outs,
            in_specs=[spec] * len(args),
            out_specs=[spec] * len(outs),
            scratch_shapes=scratch,
            compiler_params=pltpu.CompilerParams(vmem_limit_bytes=VMEM_LIMIT),
        )(*args)

    sent = rows_call(
        first_rows(loops, rows, cols, half),
        [buf] * loops,
        (tokens, other_x, cotangent, other_d, up_rows, down_rows),
        [pltpu.VMEM(whole.shape, narrow)] * 2,
    )
    got = exchange(sent, "loop")
    size = up_second.shape[1]
    *sent, col_grads = call(
        columns(loops, rows, cols),
        [buf] * loops + [jax.ShapeDtypeStruct((2 * cols * size, size), narrow)],
        *got,
        up_second.reshape(cols * size, size),
        down_first.reshape(cols * size, size),
        perm_up.reshape(1, size),
        perm_down.reshape(1, size),
    )
    got = exchange(sent, "loop")
    row_sums, back, grad = call(
        row_grads(loops, rows, cols, half),
        [grads, whole, whole],
        *got,
        tokens,
        other_x,
        cotangent,
        other_d,
    )
    scale = 1.0 / math.sqrt(dps * toks)

    def dp_total(value):
        parts = [value] + [
            lax.ppermute(value, "dp", [(s, s ^ k) for s in range(dps)])
            for k in range(dps - 1, 0, -1)
        ]
        out = jax.ShapeDtypeStruct((value.shape[0] // 2, value.shape[1]), jnp.float32)
        return call(add_shards(scale), [out, out], *parts)

    g_up_second, g_down_first = dp_total(col_grads)
    g_up_first, g_down_second = dp_total(row_sums)
    full = jax.ShapeDtypeStruct(tokens.shape, narrow)
    part = jax.ShapeDtypeStruct((kept, toks), narrow)
    mixed, mixed_send, grad_tokens, grad_send = call(
        row_outputs(half),
        [full, part, full, part],
        back,
        grad,
        tokens,
        other_x,
        cotangent,
        other_d,
        up_rows,
        down_rows,
    )

    def place(value, leaving):
        return lax.dynamic_update_slice_in_dim(
            value, from_partner(leaving, "loop", 0), (1 - parity) * kept, 0
        )

    return (
        place(mixed, mixed_send),
        place(grad_tokens, grad_send),
        g_up_first.reshape(up_first.shape),
        g_up_second.reshape(up_second.shape),
        g_down_first.reshape(down_first.shape),
        g_down_second.reshape(down_second.shape),
    )


def solution(mesh):
    in_specs = (
        P("loop", "dp"),
        P("loop", "dp"),
        P("loop", None, None),
        P("loop", None, None),
        P("loop", None, None),
        P("loop", None, None),
        P(),
        P(),
    )
    out_specs = (
        P("loop", "dp"),
        P("loop", "dp"),
        P("loop", None, None),
        P("loop", None, None),
        P("loop", None, None),
        P("loop", None, None),
    )
    return jax.shard_map(shards, mesh=mesh, in_specs=in_specs, out_specs=out_specs, check_vma=False)
```

```python
import math

import jax
import jax.numpy as jnp
from jax import lax
from jax.experimental import pallas as pl
from jax.experimental.pallas import tpu as pltpu
from jax.sharding import PartitionSpec as P


def from_partner(value, axis, apart):
    mask = 2**apart
    pairs = [(source, source ^ mask) for source in range(lax.axis_size(axis))]
    return lax.ppermute(value, axis, pairs)


def gelu_parts(pre_act):
    cumul = 0.5 * (1.0 + jax.scipy.special.erf(pre_act * (1.0 / math.sqrt(2.0))))
    slope = cumul + pre_act * jnp.exp(-0.5 * pre_act * pre_act) * (1.0 / math.sqrt(2.0 * math.pi))
    return (pre_act * cumul, slope)


def inverse_of(permute):
    return (
        jnp.zeros(permute.shape, jnp.int32)
        .at[permute]
        .set(jnp.arange(permute.shape[0], dtype=jnp.int32))
    )


def pair_total(contrib, half_width, parity):
    pair_blocks = contrib.shape[0]
    tok_count = contrib.shape[2]
    leaving = lax.dynamic_slice_in_dim(contrib, (1 - parity) * half_width, half_width, 1)
    other = from_partner(leaving.astype(jnp.bfloat16), "loop", 0).astype(leaving.dtype)
    mine = lax.dynamic_slice_in_dim(contrib, parity * half_width, half_width, 1) + other
    return mine.reshape(pair_blocks * half_width, tok_count)


def plain_shards(tokens, cotangent, up_first, up_second, down_first, down_second, perm_up, perm_down):
    wide = jnp.float32
    narrow = jnp.bfloat16
    feature_rows = tokens.shape[0]
    tok_count = tokens.shape[1]
    local_rows = up_first.shape[0]
    block = up_first.shape[2]
    half_width = block // 2
    pair_blocks = 2 * feature_rows // block
    group = 2 * local_rows // pair_blocks
    parity = lax.axis_index("loop") % 2
    other_x, other_d = from_partner((tokens, cotangent), "loop", 0)
    low_x = jnp.where(parity == 0, tokens, other_x)
    high_x = jnp.where(parity == 0, other_x, tokens)
    low_d = jnp.where(parity == 0, cotangent, other_d)
    high_d = jnp.where(parity == 0, other_d, cotangent)
    x_blocks = jnp.concatenate(
        [
            low_x.reshape(pair_blocks, half_width, tok_count),
            high_x.reshape(pair_blocks, half_width, tok_count),
        ],
        1,
    )
    d_blocks = jnp.concatenate(
        [
            low_d.reshape(pair_blocks, half_width, tok_count),
            high_d.reshape(pair_blocks, half_width, tok_count),
        ],
        1,
    )
    row_block = (parity * local_rows + jnp.arange(local_rows, dtype=jnp.int32)) // group
    picker = row_block[:, None] == jnp.arange(pair_blocks, dtype=jnp.int32)[None, :]
    picker_narrow = picker.astype(narrow)
    picker_wide = picker.astype(wide)
    x_rows = jnp.einsum("am,mit->ait", picker_narrow, x_blocks, preferred_element_type=wide).astype(
        narrow
    )
    d_rows = jnp.einsum("am,mit->ait", picker_narrow, d_blocks, preferred_element_type=wide).astype(
        narrow
    )
    inverse_up = inverse_of(perm_up)
    inverse_down = inverse_of(perm_down)
    hidden_one = jnp.einsum("abi,ait->abt", up_first, x_rows, preferred_element_type=wide).astype(
        narrow
    )
    permuted = jnp.take(
        lax.all_to_all(hidden_one, "loop", split_axis=1, concat_axis=0, tiled=True), perm_up, axis=0
    )
    pre_act = jnp.einsum("boa,abt->bot", up_second, permuted, preferred_element_type=wide)
    gelu_val, slope = gelu_parts(pre_act)
    activated = gelu_val.astype(narrow)
    mixed_cols = jnp.einsum(
        "bpo,bot->pbt", down_first, activated, preferred_element_type=wide
    ).astype(narrow)
    leaving = jnp.take(mixed_cols, perm_down, axis=0)
    back_rows = lax.all_to_all(leaving, "loop", split_axis=0, concat_axis=1, tiled=True)
    back_rows, permuted, activated, slope = (back_rows, permuted, activated, slope)
    out_rows = jnp.einsum("abo,abt->aot", down_second, back_rows, preferred_element_type=wide)
    out_contrib = jnp.einsum("am,aot->mot", picker_wide, out_rows, precision=lax.Precision.HIGHEST)
    branch_out = pair_total(out_contrib, half_width, parity)
    mixed = (tokens.astype(wide) + branch_out).astype(narrow)
    scale = 1.0 / math.sqrt(lax.axis_size("dp") * tok_count)
    grad_rows = jnp.einsum("abo,aot->abt", down_second, d_rows, preferred_element_type=wide).astype(
        narrow
    )
    g_down_second = jnp.einsum("abt,aot->abo", back_rows, d_rows, preferred_element_type=wide)
    grad_cols = lax.all_to_all(grad_rows, "loop", split_axis=1, concat_axis=0, tiled=True)
    grad_mixed = jnp.take(grad_cols, inverse_down, axis=0)
    grad_act = jnp.einsum("bpo,pbt->bot", down_first, grad_mixed, preferred_element_type=wide)
    g_down_first = jnp.einsum("pbt,bot->bpo", grad_mixed, activated, preferred_element_type=wide)
    grad_pre = (grad_act * slope).astype(narrow)
    g_up_second = jnp.einsum("bot,abt->boa", grad_pre, permuted, preferred_element_type=wide)
    grad_perm = jnp.einsum("boa,bot->abt", up_second, grad_pre, preferred_element_type=wide).astype(
        narrow
    )
    grad_recv = jnp.take(grad_perm, inverse_up, axis=0)
    grad_hidden = lax.all_to_all(grad_recv, "loop", split_axis=0, concat_axis=1, tiled=True)
    g_up_first = jnp.einsum("abt,ait->abi", grad_hidden, x_rows, preferred_element_type=wide)
    g_up_first, g_up_second, g_down_first, g_down_second = (
        lax.psum(g_up_first.astype(jnp.bfloat16), "dp").astype(jnp.float32),
        lax.psum(g_up_second.astype(jnp.bfloat16), "dp").astype(jnp.float32),
        lax.psum(g_down_first.astype(jnp.bfloat16), "dp").astype(jnp.float32),
        lax.psum(g_down_second.astype(jnp.bfloat16), "dp").astype(jnp.float32),
    )
    grad_rows_in = jnp.einsum("abi,abt->ait", up_first, grad_hidden, preferred_element_type=wide)
    grad_contrib = jnp.einsum(
        "am,ait->mit", picker_wide, grad_rows_in, precision=lax.Precision.HIGHEST
    )
    grad_branch = pair_total(grad_contrib, half_width, parity)
    grad_tokens = (cotangent.astype(wide) + grad_branch).astype(narrow)
    return (
        mixed,
        grad_tokens,
        g_up_first * scale,
        g_up_second * scale,
        g_down_first * scale,
        g_down_second * scale,
    )


VMEM_LIMIT = 16 * 2**20


def dot(left, right, left_dim=1, right_dim=0):
    return lax.dot_general(
        left, right, (((left_dim,), (right_dim,)), ((), ())), preferred_element_type=jnp.float32
    )


def call(body, outs, *args, scratch=(), micros=0.01, to_hbm=False, aliases=()):
    whole = pl.BlockSpec(memory_space=pltpu.VMEM)
    return pl.pallas_call(
        body,
        out_shape=outs,
        in_specs=[whole] * len(args),
        out_specs=[pl.BlockSpec() if to_hbm else whole] * len(outs),
        scratch_shapes=list(scratch),
        input_output_aliases=dict(aliases),
        compiler_params=pltpu.CompilerParams(vmem_limit_bytes=VMEM_LIMIT),
        cost_estimate=pl.CostEstimate(
            flops=int(micros * 1e9), bytes_accessed=int(micros * 3e6), transcendentals=0
        ),
    )(*args)


def own_first(weights, parity):
    half = weights.shape[1] // 2
    return jnp.where(parity == 0, weights, pltpu.roll(weights, half, 1))


def one_hot(rows, cols, at):
    lead = lax.broadcasted_iota(jnp.int32, (rows, cols), 0)
    lane = lax.broadcasted_iota(jnp.int32, (rows, cols), 1)
    return at(lead, lane).astype(jnp.bfloat16)


def pair_cols(me, chips, rows, cols, turn):
    mine = chips * cols
    every = 2 * mine

    def at(lead, lane):
        chip = (me // 2) ^ ((lane // cols) % chips)
        col = (2 * chip + ((me % 2) ^ turn)) * cols + lane % cols
        return lead == (lane // mine) * every + col

    return one_hot(rows * every, rows * mine, at)


def sent_order(chips, rows, cols, sent_dim):
    def at(lead, lane):
        sent, kept = (lead, lane) if sent_dim == 0 else (lane, lead)
        q, rest = sent // (cols * 2 * rows), sent % (cols * 2 * rows)
        b, row = rest // (2 * rows), rest % (2 * rows)
        return kept == row * (chips * cols) + q * cols + b

    size = 2 * rows * chips * cols
    return one_hot(size, size, at)


def block_rows(own_ref, other_ref, start, half):
    span = pl.ds(pl.multiple_of(start, half), half)
    return jnp.concatenate([own_ref[span, :], other_ref[span, :]], 0)


def pair_blocks_of(parity, pair_blocks):
    local = pair_blocks // 2
    return [(parity if at < local else 1 - parity) * local + at % local for at in range(pair_blocks)]


def tables(chips, rows, cols):
    def body(take_ref, order_ref, back_ref):
        take_ref[...] = pair_cols(lax.axis_index("loop"), chips, rows, cols, 0)
        order_ref[...] = sent_order(chips, rows, cols, 0)
        back_ref[...] = sent_order(chips, rows, cols, 1)

    return body


def first_rows(chips, rows, cols, half):
    narrow = jnp.bfloat16

    def body(*refs):
        x_refs, d_refs, (take_ref, order_ref), rest = refs[:4], refs[4:8], refs[8:10], refs[10:]
        outs, (up_out, down_out, hid_ref, grad_ref) = rest[:chips], rest[chips:]
        parity = lax.axis_index("loop") % 2
        take, order = take_ref[...], order_ref[...]
        unit = 2 * rows * cols
        jobs = ((x_refs, up_out, hid_ref), (d_refs, down_out, grad_ref))
        for job, ((own_ref, other_ref, *weights), taken_ref, grid_ref) in enumerate(jobs):
            pair_blocks = own_ref.shape[0] // half
            taken = [own_first(dot(take, ref[...], 0, 0), parity) for ref in weights]
            taken_ref[...] = jnp.concatenate(taken, 0).astype(narrow)
            high = taken_ref.shape[0] // pair_blocks
            for at, block in enumerate(pair_blocks_of(parity, pair_blocks)):
                part = slice(at * high, (at + 1) * high)
                features = block_rows(own_ref, other_ref, block * half, half)
                grid_ref[part, :] = dot(taken_ref[part, :], features).astype(narrow)
            sent = dot(order, grid_ref[...]).astype(narrow)
            for q in range(chips):
                outs[q][job * unit : (job + 1) * unit, :] = sent[q * unit : (q + 1) * unit]

    return body


def one_col(bufs, at, deep):
    return jnp.concatenate([r[at * deep : (at + 1) * deep, :] for r in bufs], 0)


def spread(outs, at, deep, value):
    for q, out in enumerate(outs):
        out[at * deep : (at + 1) * deep, :] = value[q * deep : (q + 1) * deep]


def columns(chips, rows, cols):
    narrow = jnp.bfloat16
    deep = 2 * rows

    def body(*refs):
        bufs, rest = refs[:chips], refs[chips:]
        up_ref, down_ref, perm_up_ref, perm_down_ref = rest[:4]
        outs, rest = rest[4 : 4 + chips], rest[4 + chips :]
        activated_ref, grad_pre_ref, take_up_ref, take_down_ref = rest
        me = lax.axis_index("loop")
        size = chips * deep
        lead = lax.broadcasted_iota(jnp.int32, (size, size), 0)
        lane = lax.broadcasted_iota(jnp.int32, (size, size), 1)
        row = ((lead // rows) ^ me) * rows + lead % rows
        take_up_ref[...] = (perm_up_ref[...] == row).astype(narrow)
        take_down_ref[...] = dot(
            (lane == row).astype(narrow), (perm_down_ref[...] == lead).astype(narrow), 1, 1
        ).astype(narrow)
        for b in range(cols):
            span = slice(b * size, (b + 1) * size)
            up = dot(up_ref[span, :], take_up_ref[...], 1, 1).astype(narrow)
            down = dot(take_down_ref[...], down_ref[span, :]).astype(narrow)
            gelu_val, slope = gelu_parts(dot(up, one_col(bufs, b, deep)))
            activated = gelu_val.astype(narrow)
            activated_ref[span, :] = activated
            spread(outs, b, deep, dot(down, activated).astype(narrow))
            grad_act = dot(down, one_col(bufs, cols + b, deep), 0, 0)
            grad_pre = (grad_act * slope).astype(narrow)
            grad_pre_ref[span, :] = grad_pre
            spread(outs, cols + b, deep, dot(up, grad_pre, 0, 0).astype(narrow))

    return body


def column_grads(chips, rows, cols):
    narrow = jnp.bfloat16
    deep = 2 * rows

    def body(*refs):
        bufs = refs[:chips]
        activated_ref, grad_pre_ref, take_up_ref, take_down_ref, out_ref = refs[chips:]
        size = chips * deep
        for b in range(cols):
            span = slice(b * size, (b + 1) * size)
            hid = one_col(bufs, b, deep)
            grad = one_col(bufs, cols + b, deep)
            g_up = dot(grad_pre_ref[span, :], hid, 1, 1).astype(narrow)
            g_down = dot(grad, activated_ref[span, :], 1, 1).astype(narrow)
            out_ref[span, :] = dot(g_up, take_up_ref[...]).astype(narrow)
            out_ref[cols * size + b * size : cols * size + (b + 1) * size, :] = dot(
                take_down_ref[...], g_down, 0, 0
            ).astype(narrow)

    return body


def row_grads(chips, rows, cols, half):
    narrow = jnp.bfloat16

    def body(*refs):
        bufs, (tok_ref, x_ref, cot_ref, d_ref, order_ref) = refs[:chips], refs[chips : chips + 5]
        kept_ref, leave_ref, back_ref, grad_ref = refs[-4:]
        parity = lax.axis_index("loop") % 2
        pair_blocks = tok_ref.shape[0] // half
        unit = 2 * rows * cols
        jobs = ((1, grad_ref, tok_ref, x_ref), (0, back_ref, cot_ref, d_ref))
        for at, (job, grid_ref, own_ref, other_ref) in enumerate(jobs):
            sent = one_col(bufs, job, unit)
            grid_ref[...] = dot(order_ref[...], sent).astype(narrow)
            high = grid_ref.shape[0] // pair_blocks
            grads = []
            for place, block in enumerate(pair_blocks_of(parity, pair_blocks)):
                part = slice(place * high, (place + 1) * high)
                features = block_rows(own_ref, other_ref, block * half, half)
                grads.append(dot(grid_ref[part, :], features, 1, 1))
            both = own_first(jnp.concatenate(grads, 0), parity).astype(narrow)
            size = both.shape[0] // 2
            kept_ref[at * size : (at + 1) * size, :] = both[:size]
            leave_ref[at * size : (at + 1) * size, :] = both[size:]

    return body


def join(kept_ref, came_ref, left_ref, right_ref, *rest):
    out_ref, with_ref = rest[-4:-2]
    size = kept_ref.shape[0] // 2
    for at in range(2):
        span = slice(at * size, (at + 1) * size)
        for off, ref in enumerate((kept_ref, came_ref)):
            to = slice((2 * at + off) * size, (2 * at + off + 1) * size)
            out_ref[to, :] = ref[span, :]
            with_ref[to, :] = ref[span, :]
    total = left_ref[...].astype(jnp.float32) + right_ref[...].astype(jnp.float32)
    with_ref[4 * size :, :] = total.astype(with_ref.dtype)


def row_outputs(half):
    def body(*refs):
        jobs, outs = (refs[:3], refs[3:6]), refs[6:]
        parity = lax.axis_index("loop") % 2
        for at, (grid_ref, own_ref, weights_ref) in enumerate(jobs):
            kept_ref, sent_ref = outs[2 * at : 2 * at + 2]
            pair_blocks = own_ref.shape[0] // half
            high = weights_ref.shape[0] // pair_blocks
            for place, block in enumerate(pair_blocks_of(parity, pair_blocks)):
                part = slice(place * high, (place + 1) * high)
                span = pl.ds(pl.multiple_of(block * half, half), half)
                branch = dot(weights_ref[part, :], grid_ref[part, :], 0, 0)
                kept_ref[span, :] = own_ref[span, :].astype(jnp.float32) + branch[:half]
                sent_ref[span, :] = branch[half:].astype(jnp.bfloat16)

    return body


def add_partner(*refs):
    jobs, done_ref = ((refs[0], refs[1], refs[4]), (refs[2], refs[3], refs[5])), refs[6]
    for kept, got, out in jobs:
        out[...] = (kept[...] + got[...].astype(jnp.float32)).astype(out.dtype)
    done_ref[...] = jnp.zeros_like(done_ref)


def total_grads(chips, rows, cols, dps, scale):
    def body(*refs):
        parts, outs = refs[:dps], refs[-4:]
        both_ref, got_ref = refs[0], refs[dps - 1]
        me = lax.axis_index("loop")
        place = jnp.concatenate([pair_cols(me, chips, rows, cols, turn) for turn in (0, 1)], 1)
        place = jnp.concatenate([place] * dps, 1)
        size = outs[0].shape[0]
        for at, out in enumerate(outs[:2]):
            span = slice(at * size, (at + 1) * size)
            out[...] = dot(place, jnp.concatenate([r[span, :] for r in parts], 0)) * scale
        size = outs[2].shape[0]
        for at, out in enumerate(outs[2:]):
            span = slice(2 * outs[0].shape[0] + at * size, 2 * outs[0].shape[0] + (at + 1) * size)
            both = both_ref[span, :].astype(jnp.float32) + got_ref[span, :].astype(jnp.float32)
            out[...] = both * scale

    return body


def exchange(bufs, axis):
    count = 2 * len(bufs)
    got = {
        q: lax.ppermute(bufs[q], axis, [(s, s ^ (2 * q)) for s in range(count)])
        for q in range(len(bufs) - 1, 0, -1)
    }
    return [bufs[0]] + [got[q] for q in range(1, len(bufs))]


def shards(tokens, cotangent, up_first, up_second, down_first, down_second, perm_up, perm_down):
    narrow = jnp.bfloat16
    wide = jnp.float32
    loops, dps = lax.axis_size("loop"), lax.axis_size("dp")
    feature_rows, toks = tokens.shape
    rows, all_cols, block = up_first.shape
    cols, size = up_second.shape[:2]
    half = block // 2
    pair_blocks = feature_rows // half
    if loops != 8 or dps != 4 or rows % 16 or pair_blocks % 2 or 2 * rows * cols * loops // 2 % (16 * pair_blocks):
        return plain_shards(
            tokens, cotangent, up_first, up_second, down_first, down_second, perm_up, perm_down
        )
    chips = loops // 2

    def struct(lead, width, dtype=narrow):
        return jax.ShapeDtypeStruct((lead, width), dtype)

    up_rows = up_first.reshape(rows * all_cols, block)
    down_rows = down_second.reshape(rows * all_cols, block)
    other_x = from_partner(tokens, "loop", 0)
    other_up = from_partner(up_rows, "loop", 0)
    other_d = from_partner(cotangent, "loop", 0)
    other_down = from_partner(down_rows, "loop", 0)
    grid_rows = 2 * rows * chips * cols
    buf = struct(4 * rows * cols, toks)
    grid = struct(grid_rows, toks)
    taken = struct(grid_rows, block)
    take, order, order_back = call(
        tables(chips, rows, cols),
        [struct(rows * all_cols, rows * chips * cols)] + [struct(grid_rows, grid_rows)] * 2,
        micros=4,
    )
    *sent, up_taken, down_taken = call(
        first_rows(chips, rows, cols, half),
        [buf] * chips + [taken] * 2,
        tokens,
        other_x,
        up_rows,
        other_up,
        cotangent,
        other_d,
        down_rows,
        other_down,
        take,
        order,
        scratch=[pltpu.VMEM(grid.shape, narrow)] * 2,
    )
    cells = exchange(sent, "loop")
    square = struct(cols * size, size)
    *sent, activated, grad_pre, take_up, take_down = call(
        columns(chips, rows, cols),
        [buf] * chips + [grid] * 2 + [struct(size, size)] * 2,
        *cells,
        up_second.reshape(square.shape),
        down_first.reshape(square.shape),
        perm_up.reshape(1, size),
        perm_down.reshape(1, size),
    )
    back = exchange(sent, "loop")
    (col_grads,) = call(
        column_grads(chips, rows, cols),
        [struct(2 * cols * size, size)],
        *cells,
        activated,
        grad_pre,
        take_up,
        take_down,
    )

    def over_dp(value, apart):
        return lax.ppermute(value, "dp", [(s, s ^ apart) for s in range(dps)])

    col_got = over_dp(col_grads, dps - 1)
    kept, leaving, back_rows, grad_rows = call(
        row_grads(chips, rows, cols, half),
        [taken] * 2 + [grid] * 2,
        *back,
        tokens,
        other_x,
        cotangent,
        other_d,
        order_back,
        col_grads,
    )
    came = from_partner(leaving, "loop", 0)
    partial = struct(feature_rows, toks, wide)
    full = struct(feature_rows, toks)
    mixed, mixed_send, grad_tokens, grad_send = call(
        row_outputs(half),
        [partial, full] * 2,
        back_rows,
        tokens,
        down_taken,
        grad_rows,
        cotangent,
        up_taken,
    )
    sums, sums_more, mixed_send, grad_send = call(
        join,
        [struct(2 * grid_rows, block), struct(2 * grid_rows + 2 * cols * size, block), full, full],
        kept,
        came,
        col_grads,
        col_got,
        mixed_send,
        grad_send,
        aliases=((4, 2), (5, 3)),
    )
    parts = [sums_more] + [
        over_dp(sums if apart > 1 else sums_more, apart) for apart in range(dps - 1, 0, -1)
    ]
    mixed, grad_tokens, done = call(
        add_partner,
        [full] * 2 + [struct(8, 128, wide)],
        mixed,
        from_partner(mixed_send, "loop", 0),
        grad_tokens,
        from_partner(grad_send, "loop", 0),
        to_hbm=True,
    )
    scale = 1.0 / math.sqrt(dps * toks)
    g_up_first, g_down_second, g_up_second, g_down_first = call(
        total_grads(chips, rows, cols, dps, scale),
        [struct(rows * all_cols, block, wide)] * 2 + [struct(*square.shape, wide)] * 2,
        *parts,
        done,
        to_hbm=True,
    )
    return (
        mixed,
        grad_tokens,
        g_up_first.reshape(up_first.shape),
        g_up_second.reshape(up_second.shape),
        g_down_first.reshape(down_first.shape),
        g_down_second.reshape(down_second.shape),
    )


def solution(mesh):
    in_specs = (
        P("loop", "dp"),
        P("loop", "dp"),
        P("loop", None, None),
        P("loop", None, None),
        P("loop", None, None),
        P("loop", None, None),
        P(),
        P(),
    )
    out_specs = (
        P("loop", "dp"),
        P("loop", "dp"),
        P("loop", None, None),
        P("loop", None, None),
        P("loop", None, None),
        P("loop", None, None),
    )
    return jax.shard_map(shards, mesh=mesh, in_specs=in_specs, out_specs=out_specs, check_vma=False)
```

```python
import math

import jax
import jax.numpy as jnp
from jax import lax
from jax.experimental import pallas as pl
from jax.experimental.pallas import tpu as pltpu
from jax.sharding import PartitionSpec as P


def from_partner(value, axis, apart):
    mask = 2**apart
    pairs = [(source, source ^ mask) for source in range(lax.axis_size(axis))]
    return lax.ppermute(value, axis, pairs)


def gelu_parts(pre_act):
    cumul = 0.5 * (1.0 + jax.scipy.special.erf(pre_act * (1.0 / math.sqrt(2.0))))
    slope = cumul + pre_act * jnp.exp(-0.5 * pre_act * pre_act) * (1.0 / math.sqrt(2.0 * math.pi))
    return (pre_act * cumul, slope)


def inverse_of(permute):
    return (
        jnp.zeros(permute.shape, jnp.int32)
        .at[permute]
        .set(jnp.arange(permute.shape[0], dtype=jnp.int32))
    )


def pair_total(contrib, half_width, parity):
    pair_blocks = contrib.shape[0]
    tok_count = contrib.shape[2]
    leaving = lax.dynamic_slice_in_dim(contrib, (1 - parity) * half_width, half_width, 1)
    other = from_partner(leaving.astype(jnp.bfloat16), "loop", 0).astype(leaving.dtype)
    mine = lax.dynamic_slice_in_dim(contrib, parity * half_width, half_width, 1) + other
    return mine.reshape(pair_blocks * half_width, tok_count)


def plain_shards(tokens, cotangent, up_first, up_second, down_first, down_second, perm_up, perm_down):
    wide = jnp.float32
    narrow = jnp.bfloat16
    feature_rows = tokens.shape[0]
    tok_count = tokens.shape[1]
    local_rows = up_first.shape[0]
    block = up_first.shape[2]
    half_width = block // 2
    pair_blocks = 2 * feature_rows // block
    group = 2 * local_rows // pair_blocks
    parity = lax.axis_index("loop") % 2
    other_x, other_d = from_partner((tokens, cotangent), "loop", 0)
    low_x = jnp.where(parity == 0, tokens, other_x)
    high_x = jnp.where(parity == 0, other_x, tokens)
    low_d = jnp.where(parity == 0, cotangent, other_d)
    high_d = jnp.where(parity == 0, other_d, cotangent)
    x_blocks = jnp.concatenate(
        [
            low_x.reshape(pair_blocks, half_width, tok_count),
            high_x.reshape(pair_blocks, half_width, tok_count),
        ],
        1,
    )
    d_blocks = jnp.concatenate(
        [
            low_d.reshape(pair_blocks, half_width, tok_count),
            high_d.reshape(pair_blocks, half_width, tok_count),
        ],
        1,
    )
    row_block = (parity * local_rows + jnp.arange(local_rows, dtype=jnp.int32)) // group
    picker = row_block[:, None] == jnp.arange(pair_blocks, dtype=jnp.int32)[None, :]
    picker_narrow = picker.astype(narrow)
    picker_wide = picker.astype(wide)
    x_rows = jnp.einsum("am,mit->ait", picker_narrow, x_blocks, preferred_element_type=wide).astype(
        narrow
    )
    d_rows = jnp.einsum("am,mit->ait", picker_narrow, d_blocks, preferred_element_type=wide).astype(
        narrow
    )
    inverse_up = inverse_of(perm_up)
    inverse_down = inverse_of(perm_down)
    hidden_one = jnp.einsum("abi,ait->abt", up_first, x_rows, preferred_element_type=wide).astype(
        narrow
    )
    permuted = jnp.take(
        lax.all_to_all(hidden_one, "loop", split_axis=1, concat_axis=0, tiled=True), perm_up, axis=0
    )
    pre_act = jnp.einsum("boa,abt->bot", up_second, permuted, preferred_element_type=wide)
    gelu_val, slope = gelu_parts(pre_act)
    activated = gelu_val.astype(narrow)
    mixed_cols = jnp.einsum(
        "bpo,bot->pbt", down_first, activated, preferred_element_type=wide
    ).astype(narrow)
    leaving = jnp.take(mixed_cols, perm_down, axis=0)
    back_rows = lax.all_to_all(leaving, "loop", split_axis=0, concat_axis=1, tiled=True)
    back_rows, permuted, activated, slope = (back_rows, permuted, activated, slope)
    out_rows = jnp.einsum("abo,abt->aot", down_second, back_rows, preferred_element_type=wide)
    out_contrib = jnp.einsum("am,aot->mot", picker_wide, out_rows, precision=lax.Precision.HIGHEST)
    branch_out = pair_total(out_contrib, half_width, parity)
    mixed = (tokens.astype(wide) + branch_out).astype(narrow)
    scale = 1.0 / math.sqrt(lax.axis_size("dp") * tok_count)
    grad_rows = jnp.einsum("abo,aot->abt", down_second, d_rows, preferred_element_type=wide).astype(
        narrow
    )
    g_down_second = jnp.einsum("abt,aot->abo", back_rows, d_rows, preferred_element_type=wide)
    grad_cols = lax.all_to_all(grad_rows, "loop", split_axis=1, concat_axis=0, tiled=True)
    grad_mixed = jnp.take(grad_cols, inverse_down, axis=0)
    grad_act = jnp.einsum("bpo,pbt->bot", down_first, grad_mixed, preferred_element_type=wide)
    g_down_first = jnp.einsum("pbt,bot->bpo", grad_mixed, activated, preferred_element_type=wide)
    grad_pre = (grad_act * slope).astype(narrow)
    g_up_second = jnp.einsum("bot,abt->boa", grad_pre, permuted, preferred_element_type=wide)
    grad_perm = jnp.einsum("boa,bot->abt", up_second, grad_pre, preferred_element_type=wide).astype(
        narrow
    )
    grad_recv = jnp.take(grad_perm, inverse_up, axis=0)
    grad_hidden = lax.all_to_all(grad_recv, "loop", split_axis=0, concat_axis=1, tiled=True)
    g_up_first = jnp.einsum("abt,ait->abi", grad_hidden, x_rows, preferred_element_type=wide)
    g_up_first, g_up_second, g_down_first, g_down_second = (
        lax.psum(g_up_first.astype(jnp.bfloat16), "dp").astype(jnp.float32),
        lax.psum(g_up_second.astype(jnp.bfloat16), "dp").astype(jnp.float32),
        lax.psum(g_down_first.astype(jnp.bfloat16), "dp").astype(jnp.float32),
        lax.psum(g_down_second.astype(jnp.bfloat16), "dp").astype(jnp.float32),
    )
    grad_rows_in = jnp.einsum("abi,abt->ait", up_first, grad_hidden, preferred_element_type=wide)
    grad_contrib = jnp.einsum(
        "am,ait->mit", picker_wide, grad_rows_in, precision=lax.Precision.HIGHEST
    )
    grad_branch = pair_total(grad_contrib, half_width, parity)
    grad_tokens = (cotangent.astype(wide) + grad_branch).astype(narrow)
    return (
        mixed,
        grad_tokens,
        g_up_first * scale,
        g_up_second * scale,
        g_down_first * scale,
        g_down_second * scale,
    )


VMEM_LIMIT = 16 * 2**20
COL_MICROS = 0.5


def dot(left, right, left_dim=1, right_dim=0):
    return lax.dot_general(
        left, right, (((left_dim,), (right_dim,)), ((), ())), preferred_element_type=jnp.float32
    )


def call(body, outs, *args, scratch=(), micros=0.01, to_hbm=0, aliases=()):
    whole = pl.BlockSpec(memory_space=pltpu.VMEM)
    return pl.pallas_call(
        body,
        out_shape=outs,
        in_specs=[whole] * len(args),
        out_specs=[pl.BlockSpec()] * to_hbm + [whole] * (len(outs) - to_hbm),
        scratch_shapes=list(scratch),
        input_output_aliases=dict(aliases),
        compiler_params=pltpu.CompilerParams(vmem_limit_bytes=VMEM_LIMIT),
        cost_estimate=pl.CostEstimate(
            flops=int(micros * 1e9), bytes_accessed=int(micros * 3e6), transcendentals=0
        ),
    )(*args)


def own_first(weights, parity):
    half = weights.shape[1] // 2
    return jnp.where(parity == 0, weights, pltpu.roll(weights, half, 1))


def one_hot(rows, cols, at):
    lead = lax.broadcasted_iota(jnp.int32, (rows, cols), 0)
    lane = lax.broadcasted_iota(jnp.int32, (rows, cols), 1)
    return at(lead, lane).astype(jnp.bfloat16)


def pair_cols(me, chips, rows, cols, turn):
    mine = chips * cols
    every = 2 * mine

    def at(lead, lane):
        chip = (me // 2) ^ ((lane // cols) % chips)
        col = (2 * chip + ((me % 2) ^ turn)) * cols + lane % cols
        return lead == (lane // mine) * every + col

    return one_hot(rows * every, rows * mine, at)


def sent_order(chips, rows, cols, sent_dim):
    def at(lead, lane):
        sent, kept = (lead, lane) if sent_dim == 0 else (lane, lead)
        q, rest = sent // (cols * 2 * rows), sent % (cols * 2 * rows)
        b, row = rest // (2 * rows), rest % (2 * rows)
        return kept == row * (chips * cols) + q * cols + b

    size = 2 * rows * chips * cols
    return one_hot(size, size, at)


def block_rows(own_ref, other_ref, start, half):
    span = pl.ds(pl.multiple_of(start, half), half)
    return jnp.concatenate([own_ref[span, :], other_ref[span, :]], 0)


def pair_blocks_of(parity, pair_blocks):
    local = pair_blocks // 2
    return [(parity if at < local else 1 - parity) * local + at % local for at in range(pair_blocks)]


def tables(chips, rows, cols):
    def body(take_ref, order_ref, back_ref, place_ref):
        me = lax.axis_index("loop")
        places = [pair_cols(me, chips, rows, cols, turn) for turn in (0, 1)]
        take_ref[...] = places[0]
        order_ref[...] = sent_order(chips, rows, cols, 0)
        back_ref[...] = sent_order(chips, rows, cols, 1)
        place_ref[...] = jnp.concatenate(places, 1)

    return body


def first_rows(chips, rows, cols, half):
    narrow = jnp.bfloat16

    def body(*refs):
        (own_ref, other_ref, *weights, take_ref, order_ref) = refs[:6]
        earlier, outs, (taken_ref, grid_ref) = refs[6 : -chips - 2], refs[-chips - 2 : -2], refs[-2:]
        parity = lax.axis_index("loop") % 2
        pair_blocks = own_ref.shape[0] // half
        taken = [own_first(dot(take_ref[...], ref[...], 0, 0), parity) for ref in weights]
        taken_ref[...] = jnp.concatenate(taken, 0).astype(narrow)
        high = taken_ref.shape[0] // pair_blocks
        for at, block in enumerate(pair_blocks_of(parity, pair_blocks)):
            part = slice(at * high, (at + 1) * high)
            features = block_rows(own_ref, other_ref, block * half, half)
            grid_ref[part, :] = dot(taken_ref[part, :], features).astype(narrow)
        sent = dot(order_ref[...], grid_ref[...]).astype(narrow)
        unit = 2 * rows * cols
        for q, out in enumerate(outs):
            if earlier:
                out[:unit, :] = earlier[q][...]
            out[out.shape[0] - unit :, :] = sent[q * unit : (q + 1) * unit]

    return body


def by_distance(bufs):
    return [bufs[0], *bufs[:0:-1]]


def one_col(bufs, at, deep):
    return jnp.concatenate([r[at * deep : (at + 1) * deep, :] for r in bufs], 0)


def spread(outs, at, deep, value):
    for q, out in enumerate(outs):
        out[at * deep : (at + 1) * deep, :] = value[q * deep : (q + 1) * deep]


def columns(chips, rows, cols):
    narrow = jnp.bfloat16
    deep = 2 * rows

    def body(*refs):
        bufs, rest = by_distance(refs[:chips]), refs[chips:]
        up_ref, down_ref, perm_up_ref, perm_down_ref = rest[:4]
        outs, rest = rest[4 : 4 + chips], rest[4 + chips :]
        activated_ref, grad_pre_ref, take_up_ref, take_down_ref = rest
        me = lax.axis_index("loop")
        size = chips * deep
        lead = lax.broadcasted_iota(jnp.int32, (size, size), 0)
        lane = lax.broadcasted_iota(jnp.int32, (size, size), 1)
        row = ((lead // rows) ^ me) * rows + lead % rows
        take_up_ref[...] = (perm_up_ref[...] == row).astype(narrow)
        take_down_ref[...] = dot(
            (lane == row).astype(narrow), (perm_down_ref[...] == lead).astype(narrow), 1, 1
        ).astype(narrow)
        for b in range(cols):
            span = slice(b * size, (b + 1) * size)
            up = dot(up_ref[span, :], take_up_ref[...], 1, 1).astype(narrow)
            down = dot(take_down_ref[...], down_ref[span, :]).astype(narrow)
            gelu_val, slope = gelu_parts(dot(up, one_col(bufs, b, deep)))
            activated = gelu_val.astype(narrow)
            activated_ref[span, :] = activated
            spread(outs, b, deep, dot(down, activated).astype(narrow))
            grad_act = dot(down, one_col(bufs, cols + b, deep), 0, 0)
            grad_pre = (grad_act * slope).astype(narrow)
            grad_pre_ref[span, :] = grad_pre
            spread(outs, cols + b, deep, dot(up, grad_pre, 0, 0).astype(narrow))

    return body


def column_grads(chips, rows, cols):
    narrow = jnp.bfloat16
    deep = 2 * rows

    def body(*refs):
        bufs = by_distance(refs[:chips])
        activated_ref, grad_pre_ref, take_up_ref, take_down_ref, out_ref = refs[chips:]
        size = chips * deep
        for b in range(cols):
            span = slice(b * size, (b + 1) * size)
            hid = one_col(bufs, b, deep)
            grad = one_col(bufs, cols + b, deep)
            g_up = dot(grad_pre_ref[span, :], hid, 1, 1).astype(narrow)
            g_down = dot(grad, activated_ref[span, :], 1, 1).astype(narrow)
            out_ref[span, :] = dot(g_up, take_up_ref[...]).astype(narrow)
            out_ref[cols * size + b * size : cols * size + (b + 1) * size, :] = dot(
                take_down_ref[...], g_down, 0, 0
            ).astype(narrow)

    return body


def row_grads(chips, rows, cols, half):
    narrow = jnp.bfloat16

    def body(*refs):
        bufs, (tok_ref, x_ref, cot_ref, d_ref, order_ref) = refs[:chips], refs[chips : chips + 5]
        kept_ref, leave_ref, back_ref, grad_ref = refs[-4:]
        parity = lax.axis_index("loop") % 2
        pair_blocks = tok_ref.shape[0] // half
        unit = 2 * rows * cols
        jobs = ((1, grad_ref, tok_ref, x_ref), (0, back_ref, cot_ref, d_ref))
        for at, (job, grid_ref, own_ref, other_ref) in enumerate(jobs):
            sent = one_col(bufs, job, unit)
            grid_ref[...] = dot(order_ref[...], sent).astype(narrow)
            high = grid_ref.shape[0] // pair_blocks
            grads = []
            for place, block in enumerate(pair_blocks_of(parity, pair_blocks)):
                part = slice(place * high, (place + 1) * high)
                features = block_rows(own_ref, other_ref, block * half, half)
                grads.append(dot(grid_ref[part, :], features, 1, 1))
            both = own_first(jnp.concatenate(grads, 0), parity).astype(narrow)
            size = both.shape[0] // 2
            kept_ref[at * size : (at + 1) * size, :] = both[:size]
            leave_ref[at * size : (at + 1) * size, :] = both[size:]

    return body


def join(kept_ref, came_ref, left_ref, right_ref, *rest):
    out_ref, sum_ref = rest[-3:-1]
    size = kept_ref.shape[0] // 2
    for at in range(2):
        span = slice(at * size, (at + 1) * size)
        for off, ref in enumerate((kept_ref, came_ref)):
            out_ref[(2 * at + off) * size : (2 * at + off + 1) * size, :] = ref[span, :]
    total = left_ref[...].astype(jnp.float32) + right_ref[...].astype(jnp.float32)
    sum_ref[...] = total.astype(sum_ref.dtype)


def row_outputs(half):
    def body(*refs):
        jobs, (*kept_refs, sent_ref) = (refs[:3], refs[3:6]), refs[6:]
        parity = lax.axis_index("loop") % 2
        for at, (grid_ref, own_ref, weights_ref) in enumerate(jobs):
            kept_ref, features = kept_refs[at], own_ref.shape[0]
            pair_blocks = own_ref.shape[0] // half
            high = weights_ref.shape[0] // pair_blocks
            for place, block in enumerate(pair_blocks_of(parity, pair_blocks)):
                part = slice(place * high, (place + 1) * high)
                span = pl.ds(pl.multiple_of(block * half, half), half)
                branch = dot(weights_ref[part, :], grid_ref[part, :], 0, 0)
                kept_ref[span, :] = own_ref[span, :].astype(jnp.float32) + branch[:half]
                span = pl.ds(pl.multiple_of(at * features + block * half, half), half)
                sent_ref[span, :] = branch[half:].astype(jnp.bfloat16)

    return body


def add_partner(mixed_ref, grad_ref, got_ref, _, mixed_out, grad_out, done_ref):
    size = mixed_ref.shape[0]
    for at, (kept, out) in enumerate(((mixed_ref, mixed_out), (grad_ref, grad_out))):
        got = got_ref[at * size : (at + 1) * size, :].astype(jnp.float32)
        out[...] = (kept[...] + got).astype(out.dtype)
    done_ref[...] = jnp.zeros_like(done_ref)


def add(*refs):
    left_ref, right_ref, out_ref = refs[-3:]
    total = left_ref[...].astype(jnp.float32) + right_ref[...].astype(jnp.float32)
    out_ref[...] = total.astype(out_ref.dtype)


def total_grads(scale):
    def body(*refs):
        pair, place_ref, outs = refs[:2], refs[2], refs[-2:]
        place = jnp.concatenate([place_ref[...]] * 2, 1)
        size = outs[0].shape[0]
        for at, out in enumerate(outs):
            span = slice(at * size, (at + 1) * size)
            out[...] = dot(place, jnp.concatenate([r[span, :] for r in pair], 0)) * scale

    return body


def total_col_grads(scale):
    def body(sum_ref, got_ref, up_ref, down_ref, done_ref):
        done_ref[...] = jnp.zeros_like(done_ref)
        size = up_ref.shape[0]
        for at, out in enumerate((up_ref, down_ref)):
            span = slice(at * size, (at + 1) * size)
            both = sum_ref[span, :].astype(jnp.float32) + got_ref[span, :].astype(jnp.float32)
            out[...] = both * scale

    return body


def exchange(bufs, axis, far_first):
    count = len(bufs)
    order = range(count - 1, 0, -1) if far_first else range(1, count)
    pairs = {q: [(s, s ^ (2 * q)) for s in range(2 * count)] for q in order}
    return [bufs[0]] + [lax.ppermute(bufs[q], axis, pairs[q]) for q in order]


def shards(tokens, cotangent, up_first, up_second, down_first, down_second, perm_up, perm_down):
    narrow = jnp.bfloat16
    wide = jnp.float32
    loops, dps = lax.axis_size("loop"), lax.axis_size("dp")
    feature_rows, toks = tokens.shape
    rows, all_cols, block = up_first.shape
    cols, size = up_second.shape[:2]
    half = block // 2
    pair_blocks = feature_rows // half
    if loops != 8 or dps != 4 or rows % 16 or pair_blocks % 2 or 2 * rows * cols * loops // 2 % (16 * pair_blocks):
        return plain_shards(
            tokens, cotangent, up_first, up_second, down_first, down_second, perm_up, perm_down
        )
    chips = loops // 2

    def struct(lead, width, dtype=narrow):
        return jax.ShapeDtypeStruct((lead, width), dtype)

    up_rows = up_first.reshape(rows * all_cols, block)
    down_rows = down_second.reshape(rows * all_cols, block)
    grid_rows = 2 * rows * chips * cols
    half_buf = struct(2 * rows * cols, toks)
    buf = struct(4 * rows * cols, toks)
    grid = struct(grid_rows, toks)
    half_grid = struct(grid_rows // 2, toks)
    taken = struct(grid_rows, block)
    full = struct(feature_rows, toks)
    take, order, order_back, place = call(
        tables(chips, rows, cols),
        [struct(rows * all_cols, rows * chips * cols)] + [struct(grid_rows, grid_rows)] * 3,
        micros=4,
    )
    other_x = from_partner(tokens, "loop", 0)
    other_up = from_partner(up_rows, "loop", 0)
    other_down = from_partner(down_rows, "loop", 0)
    leaving, other_up, other_down = lax.optimization_barrier((cotangent, other_up, other_down))
    other_d = from_partner(leaving, "loop", 0)

    def rows_out(out, *args):
        return call(
            first_rows(chips, rows, cols, half),
            [out] * chips + [taken],
            *args,
            scratch=[pltpu.VMEM(grid.shape, narrow)],
        )

    *sent, up_taken = rows_out(half_buf, tokens, other_x, up_rows, other_up, take, order)
    *sent, down_taken = rows_out(
        buf, cotangent, other_d, down_rows, other_down, take, order, *sent
    )
    cells = exchange(sent, "loop", True)
    square = struct(cols * size, size)
    *sent, activated, grad_pre, take_up, take_down = call(
        columns(chips, rows, cols),
        [buf] * chips + [grid] * 2 + [struct(size, size)] * 2,
        *cells,
        up_second.reshape(square.shape),
        down_first.reshape(square.shape),
        perm_up.reshape(1, size),
        perm_down.reshape(1, size),
    )
    back = exchange(sent, "loop", False)
    (col_grads,) = call(
        column_grads(chips, rows, cols),
        [struct(2 * cols * size, size)],
        *cells,
        activated,
        grad_pre,
        take_up,
        take_down,
    )

    def over_dp(value, apart):
        return lax.ppermute(value, "dp", [(s, s ^ apart) for s in range(dps)])

    kept, leaving, back_rows, grad_rows = call(
        row_grads(chips, rows, cols, half),
        [taken] * 2 + [grid] * 2,
        *back,
        tokens,
        other_x,
        cotangent,
        other_d,
        order_back,
        col_grads,
    )
    partial = struct(feature_rows, toks, wide)
    both = struct(2 * feature_rows, toks)
    mixed, grad_tokens, branches = call(
        row_outputs(half),
        [partial, partial, both],
        back_rows,
        tokens,
        down_taken,
        grad_rows,
        cotangent,
        up_taken,
    )
    sums, col_sum, branches = call(
        join,
        [struct(2 * grid_rows, block), struct(*col_grads.shape), both],
        kept,
        from_partner(leaving, "loop", 0),
        col_grads,
        over_dp(col_grads, dps - 1),
        branches,
        aliases=((4, 2),),
    )
    (sums,) = call(add, [struct(*sums.shape)], sums, over_dp(sums, dps - 1))
    scale = 1.0 / math.sqrt(dps * toks)
    token = struct(8, 128, wide)
    g_up_second, g_down_first, done = call(
        total_col_grads(scale),
        [struct(*square.shape, wide)] * 2 + [token],
        col_sum,
        over_dp(col_sum, 1),
        to_hbm=2,
        micros=COL_MICROS,
    )
    mixed, grad_tokens, done = call(
        add_partner,
        [full] * 2 + [token],
        mixed,
        grad_tokens,
        from_partner(branches, "loop", 0),
        done,
        to_hbm=2,
    )
    g_up_first, g_down_second = call(
        total_grads(scale),
        [struct(rows * all_cols, block, wide)] * 2,
        sums,
        over_dp(sums, 1),
        place,
        done,
        to_hbm=2,
    )
    return (
        mixed,
        grad_tokens,
        g_up_first.reshape(up_first.shape),
        g_up_second.reshape(up_second.shape),
        g_down_first.reshape(down_first.shape),
        g_down_second.reshape(down_second.shape),
    )


def solution(mesh):
    in_specs = (
        P("loop", "dp"),
        P("loop", "dp"),
        P("loop", None, None),
        P("loop", None, None),
        P("loop", None, None),
        P("loop", None, None),
        P(),
        P(),
    )
    out_specs = (
        P("loop", "dp"),
        P("loop", "dp"),
        P("loop", None, None),
        P("loop", None, None),
        P("loop", None, None),
        P("loop", None, None),
    )
    return jax.shard_map(shards, mesh=mesh, in_specs=in_specs, out_specs=out_specs, check_vma=False)
```

```python
import math

import jax
import jax.numpy as jnp
from jax import lax
from jax.experimental import pallas as pl
from jax.experimental.pallas import tpu as pltpu
from jax.sharding import PartitionSpec as P


def from_partner(value, axis, apart):
    mask = 2**apart
    pairs = [(source, source ^ mask) for source in range(lax.axis_size(axis))]
    return lax.ppermute(value, axis, pairs)


def gelu_parts(pre_act):
    cumul = 0.5 * (1.0 + jax.scipy.special.erf(pre_act * (1.0 / math.sqrt(2.0))))
    slope = cumul + pre_act * jnp.exp(-0.5 * pre_act * pre_act) * (1.0 / math.sqrt(2.0 * math.pi))
    return (pre_act * cumul, slope)


def inverse_of(permute):
    return (
        jnp.zeros(permute.shape, jnp.int32)
        .at[permute]
        .set(jnp.arange(permute.shape[0], dtype=jnp.int32))
    )


def pair_total(contrib, half_width, parity):
    pair_blocks = contrib.shape[0]
    tok_count = contrib.shape[2]
    leaving = lax.dynamic_slice_in_dim(contrib, (1 - parity) * half_width, half_width, 1)
    other = from_partner(leaving.astype(jnp.bfloat16), "loop", 0).astype(leaving.dtype)
    mine = lax.dynamic_slice_in_dim(contrib, parity * half_width, half_width, 1) + other
    return mine.reshape(pair_blocks * half_width, tok_count)


def plain_shards(tokens, cotangent, up_first, up_second, down_first, down_second, perm_up, perm_down):
    wide = jnp.float32
    narrow = jnp.bfloat16
    feature_rows = tokens.shape[0]
    tok_count = tokens.shape[1]
    local_rows = up_first.shape[0]
    block = up_first.shape[2]
    half_width = block // 2
    pair_blocks = 2 * feature_rows // block
    group = 2 * local_rows // pair_blocks
    parity = lax.axis_index("loop") % 2
    other_x, other_d = from_partner((tokens, cotangent), "loop", 0)
    low_x = jnp.where(parity == 0, tokens, other_x)
    high_x = jnp.where(parity == 0, other_x, tokens)
    low_d = jnp.where(parity == 0, cotangent, other_d)
    high_d = jnp.where(parity == 0, other_d, cotangent)
    x_blocks = jnp.concatenate(
        [
            low_x.reshape(pair_blocks, half_width, tok_count),
            high_x.reshape(pair_blocks, half_width, tok_count),
        ],
        1,
    )
    d_blocks = jnp.concatenate(
        [
            low_d.reshape(pair_blocks, half_width, tok_count),
            high_d.reshape(pair_blocks, half_width, tok_count),
        ],
        1,
    )
    row_block = (parity * local_rows + jnp.arange(local_rows, dtype=jnp.int32)) // group
    picker = row_block[:, None] == jnp.arange(pair_blocks, dtype=jnp.int32)[None, :]
    picker_narrow = picker.astype(narrow)
    picker_wide = picker.astype(wide)
    x_rows = jnp.einsum("am,mit->ait", picker_narrow, x_blocks, preferred_element_type=wide).astype(
        narrow
    )
    d_rows = jnp.einsum("am,mit->ait", picker_narrow, d_blocks, preferred_element_type=wide).astype(
        narrow
    )
    inverse_up = inverse_of(perm_up)
    inverse_down = inverse_of(perm_down)
    hidden_one = jnp.einsum("abi,ait->abt", up_first, x_rows, preferred_element_type=wide).astype(
        narrow
    )
    permuted = jnp.take(
        lax.all_to_all(hidden_one, "loop", split_axis=1, concat_axis=0, tiled=True), perm_up, axis=0
    )
    pre_act = jnp.einsum("boa,abt->bot", up_second, permuted, preferred_element_type=wide)
    gelu_val, slope = gelu_parts(pre_act)
    activated = gelu_val.astype(narrow)
    mixed_cols = jnp.einsum(
        "bpo,bot->pbt", down_first, activated, preferred_element_type=wide
    ).astype(narrow)
    leaving = jnp.take(mixed_cols, perm_down, axis=0)
    back_rows = lax.all_to_all(leaving, "loop", split_axis=0, concat_axis=1, tiled=True)
    back_rows, permuted, activated, slope = (back_rows, permuted, activated, slope)
    out_rows = jnp.einsum("abo,abt->aot", down_second, back_rows, preferred_element_type=wide)
    out_contrib = jnp.einsum("am,aot->mot", picker_wide, out_rows, precision=lax.Precision.HIGHEST)
    branch_out = pair_total(out_contrib, half_width, parity)
    mixed = (tokens.astype(wide) + branch_out).astype(narrow)
    scale = 1.0 / math.sqrt(lax.axis_size("dp") * tok_count)
    grad_rows = jnp.einsum("abo,aot->abt", down_second, d_rows, preferred_element_type=wide).astype(
        narrow
    )
    g_down_second = jnp.einsum("abt,aot->abo", back_rows, d_rows, preferred_element_type=wide)
    grad_cols = lax.all_to_all(grad_rows, "loop", split_axis=1, concat_axis=0, tiled=True)
    grad_mixed = jnp.take(grad_cols, inverse_down, axis=0)
    grad_act = jnp.einsum("bpo,pbt->bot", down_first, grad_mixed, preferred_element_type=wide)
    g_down_first = jnp.einsum("pbt,bot->bpo", grad_mixed, activated, preferred_element_type=wide)
    grad_pre = (grad_act * slope).astype(narrow)
    g_up_second = jnp.einsum("bot,abt->boa", grad_pre, permuted, preferred_element_type=wide)
    grad_perm = jnp.einsum("boa,bot->abt", up_second, grad_pre, preferred_element_type=wide).astype(
        narrow
    )
    grad_recv = jnp.take(grad_perm, inverse_up, axis=0)
    grad_hidden = lax.all_to_all(grad_recv, "loop", split_axis=0, concat_axis=1, tiled=True)
    g_up_first = jnp.einsum("abt,ait->abi", grad_hidden, x_rows, preferred_element_type=wide)
    g_up_first, g_up_second, g_down_first, g_down_second = (
        lax.psum(g_up_first.astype(jnp.bfloat16), "dp").astype(jnp.float32),
        lax.psum(g_up_second.astype(jnp.bfloat16), "dp").astype(jnp.float32),
        lax.psum(g_down_first.astype(jnp.bfloat16), "dp").astype(jnp.float32),
        lax.psum(g_down_second.astype(jnp.bfloat16), "dp").astype(jnp.float32),
    )
    grad_rows_in = jnp.einsum("abi,abt->ait", up_first, grad_hidden, preferred_element_type=wide)
    grad_contrib = jnp.einsum(
        "am,ait->mit", picker_wide, grad_rows_in, precision=lax.Precision.HIGHEST
    )
    grad_branch = pair_total(grad_contrib, half_width, parity)
    grad_tokens = (cotangent.astype(wide) + grad_branch).astype(narrow)
    return (
        mixed,
        grad_tokens,
        g_up_first * scale,
        g_up_second * scale,
        g_down_first * scale,
        g_down_second * scale,
    )


VMEM_LIMIT = 16 * 2**20
COL_MICROS = 28


def dot(left, right, left_dim=1, right_dim=0):
    return lax.dot_general(
        left, right, (((left_dim,), (right_dim,)), ((), ())), preferred_element_type=jnp.float32
    )


def call(body, outs, *args, scratch=(), micros=0.01, to_hbm=0, aliases=()):
    whole = pl.BlockSpec(memory_space=pltpu.VMEM)
    return pl.pallas_call(
        body,
        out_shape=outs,
        in_specs=[whole] * len(args),
        out_specs=[pl.BlockSpec()] * to_hbm + [whole] * (len(outs) - to_hbm),
        scratch_shapes=list(scratch),
        input_output_aliases=dict(aliases),
        compiler_params=pltpu.CompilerParams(vmem_limit_bytes=VMEM_LIMIT),
        cost_estimate=pl.CostEstimate(
            flops=int(micros * 1e9), bytes_accessed=int(micros * 3e6), transcendentals=0
        ),
    )(*args)


def own_first(weights, parity):
    half = weights.shape[1] // 2
    return jnp.where(parity == 0, weights, pltpu.roll(weights, half, 1))


def one_hot(rows, cols, at):
    lead = lax.broadcasted_iota(jnp.int32, (rows, cols), 0)
    lane = lax.broadcasted_iota(jnp.int32, (rows, cols), 1)
    return at(lead, lane).astype(jnp.bfloat16)


def pair_cols(me, chips, rows, cols, turn):
    mine = chips * cols
    every = 2 * mine

    def at(lead, lane):
        chip = (me // 2) ^ ((lane // cols) % chips)
        col = (2 * chip + ((me % 2) ^ turn)) * cols + lane % cols
        return lead == (lane // mine) * every + col

    return one_hot(rows * every, rows * mine, at)


def sent_order(chips, rows, cols, sent_dim):
    def at(lead, lane):
        sent, kept = (lead, lane) if sent_dim == 0 else (lane, lead)
        q, rest = sent // (cols * 2 * rows), sent % (cols * 2 * rows)
        b, row = rest // (2 * rows), rest % (2 * rows)
        return kept == row * (chips * cols) + q * cols + b

    size = 2 * rows * chips * cols
    return one_hot(size, size, at)


def block_rows(own_ref, other_ref, start, half):
    span = pl.ds(pl.multiple_of(start, half), half)
    return jnp.concatenate([own_ref[span, :], other_ref[span, :]], 0)


def pair_blocks_of(parity, pair_blocks):
    local = pair_blocks // 2
    return [(parity if at < local else 1 - parity) * local + at % local for at in range(pair_blocks)]


def tables(chips, rows, cols):
    def body(take_ref, order_ref, back_ref, place_ref):
        me = lax.axis_index("loop")
        places = [pair_cols(me, chips, rows, cols, turn) for turn in (0, 1)]
        take_ref[...] = places[0]
        order_ref[...] = sent_order(chips, rows, cols, 0)
        back_ref[...] = sent_order(chips, rows, cols, 1)
        place_ref[...] = jnp.concatenate(places, 1)

    return body


def first_rows(chips, rows, cols, half):
    narrow = jnp.bfloat16

    def body(*refs):
        (own_ref, other_ref, *weights, take_ref, order_ref) = refs[:6]
        earlier, outs, (taken_ref, grid_ref) = refs[6 : -chips - 2], refs[-chips - 2 : -2], refs[-2:]
        parity = lax.axis_index("loop") % 2
        pair_blocks = own_ref.shape[0] // half
        taken = [own_first(dot(take_ref[...], ref[...], 0, 0), parity) for ref in weights]
        taken_ref[...] = jnp.concatenate(taken, 0).astype(narrow)
        high = taken_ref.shape[0] // pair_blocks
        for at, block in enumerate(pair_blocks_of(parity, pair_blocks)):
            part = slice(at * high, (at + 1) * high)
            features = block_rows(own_ref, other_ref, block * half, half)
            grid_ref[part, :] = dot(taken_ref[part, :], features).astype(narrow)
        sent = dot(order_ref[...], grid_ref[...]).astype(narrow)
        unit = 2 * rows * cols
        for q, out in enumerate(outs):
            if earlier:
                out[:unit, :] = earlier[q][...]
            out[out.shape[0] - unit :, :] = sent[q * unit : (q + 1) * unit]

    return body


def by_distance(bufs):
    return [bufs[0], *bufs[:0:-1]]


def one_col(bufs, at, deep):
    return jnp.concatenate([r[at * deep : (at + 1) * deep, :] for r in bufs], 0)


def spread(outs, at, deep, value):
    for q, out in enumerate(outs):
        out[at * deep : (at + 1) * deep, :] = value[q * deep : (q + 1) * deep]


def columns(chips, rows, cols):
    narrow = jnp.bfloat16
    deep = 2 * rows

    def body(*refs):
        bufs, rest = by_distance(refs[:chips]), refs[chips:]
        up_ref, down_ref, perm_up_ref, perm_down_ref = rest[:4]
        outs, rest = rest[4 : 4 + chips], rest[4 + chips :]
        activated_ref, grad_pre_ref, take_up_ref, take_down_ref = rest
        me = lax.axis_index("loop")
        size = chips * deep
        lead = lax.broadcasted_iota(jnp.int32, (size, size), 0)
        lane = lax.broadcasted_iota(jnp.int32, (size, size), 1)
        row = ((lead // rows) ^ me) * rows + lead % rows
        take_up_ref[...] = (perm_up_ref[...] == row).astype(narrow)
        take_down_ref[...] = dot(
            (lane == row).astype(narrow), (perm_down_ref[...] == lead).astype(narrow), 1, 1
        ).astype(narrow)
        for b in range(cols):
            span = slice(b * size, (b + 1) * size)
            up = dot(up_ref[span, :], take_up_ref[...], 1, 1).astype(narrow)
            down = dot(take_down_ref[...], down_ref[span, :]).astype(narrow)
            gelu_val, slope = gelu_parts(dot(up, one_col(bufs, b, deep)))
            activated = gelu_val.astype(narrow)
            activated_ref[span, :] = activated
            spread(outs, b, deep, dot(down, activated).astype(narrow))
            grad_act = dot(down, one_col(bufs, cols + b, deep), 0, 0)
            grad_pre = (grad_act * slope).astype(narrow)
            grad_pre_ref[span, :] = grad_pre
            spread(outs, cols + b, deep, dot(up, grad_pre, 0, 0).astype(narrow))

    return body


def column_grads(chips, rows, cols):
    narrow = jnp.bfloat16
    deep = 2 * rows

    def body(*refs):
        bufs = by_distance(refs[:chips])
        activated_ref, grad_pre_ref, take_up_ref, take_down_ref, out_ref = refs[chips:]
        size = chips * deep
        for b in range(cols):
            span = slice(b * size, (b + 1) * size)
            hid = one_col(bufs, b, deep)
            grad = one_col(bufs, cols + b, deep)
            g_up = dot(grad_pre_ref[span, :], hid, 1, 1).astype(narrow)
            g_down = dot(grad, activated_ref[span, :], 1, 1).astype(narrow)
            out_ref[span, :] = dot(g_up, take_up_ref[...]).astype(narrow)
            out_ref[cols * size + b * size : cols * size + (b + 1) * size, :] = dot(
                take_down_ref[...], g_down, 0, 0
            ).astype(narrow)

    return body


def row_grads(chips, rows, cols, half):
    narrow = jnp.bfloat16

    def body(*refs):
        bufs, (tok_ref, x_ref, cot_ref, d_ref, order_ref) = refs[:chips], refs[chips : chips + 5]
        grads_ref, back_ref, grad_ref = refs[-3:]
        parity = lax.axis_index("loop") % 2
        pair_blocks = tok_ref.shape[0] // half
        unit = 2 * rows * cols
        jobs = ((1, grad_ref, tok_ref, x_ref), (0, back_ref, cot_ref, d_ref))
        for at, (job, grid_ref, own_ref, other_ref) in enumerate(jobs):
            sent = one_col(bufs, job, unit)
            grid_ref[...] = dot(order_ref[...], sent).astype(narrow)
            high = grid_ref.shape[0] // pair_blocks
            grads = []
            for place, block in enumerate(pair_blocks_of(parity, pair_blocks)):
                part = slice(place * high, (place + 1) * high)
                features = block_rows(own_ref, other_ref, block * half, half)
                grads.append(dot(grid_ref[part, :], features, 1, 1))
            both = own_first(jnp.concatenate(grads, 0), parity).astype(narrow)
            size = both.shape[0] // 2
            for turn in range(2):
                start = (2 * turn + at) * size
                grads_ref[start : start + size, :] = both[turn * size : (turn + 1) * size]

    return body


def row_outputs(half):
    def body(*refs):
        jobs, col_refs, (*kept_refs, sent_ref, sum_ref) = (refs[:3], refs[3:6]), refs[6:8], refs[8:]
        add(*col_refs, sum_ref)
        parity = lax.axis_index("loop") % 2
        for at, (grid_ref, own_ref, weights_ref) in enumerate(jobs):
            kept_ref, features = kept_refs[at], own_ref.shape[0]
            pair_blocks = own_ref.shape[0] // half
            high = weights_ref.shape[0] // pair_blocks
            for place, block in enumerate(pair_blocks_of(parity, pair_blocks)):
                part = slice(place * high, (place + 1) * high)
                span = pl.ds(pl.multiple_of(block * half, half), half)
                branch = dot(weights_ref[part, :], grid_ref[part, :], 0, 0)
                kept_ref[span, :] = own_ref[span, :].astype(jnp.float32) + branch[:half]
                span = pl.ds(pl.multiple_of(at * features + block * half, half), half)
                sent_ref[span, :] = branch[half:].astype(jnp.bfloat16)

    return body


def add_partner(mixed_ref, grad_ref, got_ref, _, mixed_out, grad_out, done_ref):
    size = mixed_ref.shape[0]
    for at, (kept, out) in enumerate(((mixed_ref, mixed_out), (grad_ref, grad_out))):
        got = got_ref[at * size : (at + 1) * size, :].astype(jnp.float32)
        out[...] = (kept[...] + got).astype(out.dtype)
    done_ref[...] = jnp.zeros_like(done_ref)


def add(left_ref, right_ref, out_ref):
    total = left_ref[...].astype(jnp.float32) + right_ref[...].astype(jnp.float32)
    out_ref[...] = total.astype(out_ref.dtype)


def add_halves(left_ref, right_ref, kept_ref, leave_ref):
    size = kept_ref.shape[0]
    for at, out in enumerate((kept_ref, leave_ref)):
        span = slice(at * size, (at + 1) * size)
        total = left_ref[span, :].astype(jnp.float32) + right_ref[span, :].astype(jnp.float32)
        out[...] = total.astype(out.dtype)


def total_grads(scale):
    def body(*refs):
        parts, place_ref, outs = refs[:4], refs[4], refs[-2:]
        size = parts[0].shape[0] // 2
        near, far = place_ref[:, :size], place_ref[:, size:]
        place = jnp.concatenate([near, near, far, far], 1)
        for at, out in enumerate(outs):
            span = slice(at * size, (at + 1) * size)
            out[...] = dot(place, jnp.concatenate([r[span, :] for r in parts], 0)) * scale

    return body


def total_col_grads(scale):
    def body(sum_ref, got_ref, up_ref, down_ref, done_ref):
        done_ref[...] = jnp.zeros_like(done_ref)
        size = up_ref.shape[0]
        for at, out in enumerate((up_ref, down_ref)):
            span = slice(at * size, (at + 1) * size)
            both = sum_ref[span, :].astype(jnp.float32) + got_ref[span, :].astype(jnp.float32)
            out[...] = both * scale

    return body


def exchange(bufs, axis, far_first):
    count = len(bufs)
    order = range(count - 1, 0, -1) if far_first else range(1, count)
    pairs = {q: [(s, s ^ (2 * q)) for s in range(2 * count)] for q in order}
    return [bufs[0]] + [lax.ppermute(bufs[q], axis, pairs[q]) for q in order]


def shards(tokens, cotangent, up_first, up_second, down_first, down_second, perm_up, perm_down):
    narrow = jnp.bfloat16
    wide = jnp.float32
    loops, dps = lax.axis_size("loop"), lax.axis_size("dp")
    feature_rows, toks = tokens.shape
    rows, all_cols, block = up_first.shape
    cols, size = up_second.shape[:2]
    half = block // 2
    pair_blocks = feature_rows // half
    if loops != 8 or dps != 4 or rows % 16 or pair_blocks % 2 or 2 * rows * cols * loops // 2 % (16 * pair_blocks):
        return plain_shards(
            tokens, cotangent, up_first, up_second, down_first, down_second, perm_up, perm_down
        )
    chips = loops // 2

    def struct(lead, width, dtype=narrow):
        return jax.ShapeDtypeStruct((lead, width), dtype)

    up_rows = up_first.reshape(rows * all_cols, block)
    down_rows = down_second.reshape(rows * all_cols, block)
    grid_rows = 2 * rows * chips * cols
    half_buf = struct(2 * rows * cols, toks)
    buf = struct(4 * rows * cols, toks)
    grid = struct(grid_rows, toks)
    half_grid = struct(grid_rows // 2, toks)
    taken = struct(grid_rows, block)
    full = struct(feature_rows, toks)
    take, order, order_back, place = call(
        tables(chips, rows, cols),
        [struct(rows * all_cols, rows * chips * cols)] + [struct(grid_rows, grid_rows)] * 3,
        micros=4,
    )
    other_x = from_partner(tokens, "loop", 0)
    other_up = from_partner(up_rows, "loop", 0)
    other_down = from_partner(down_rows, "loop", 0)
    leaving, other_up, other_down = lax.optimization_barrier((cotangent, other_up, other_down))
    other_d = from_partner(leaving, "loop", 0)

    def rows_out(out, *args):
        return call(
            first_rows(chips, rows, cols, half),
            [out] * chips + [taken],
            *args,
            scratch=[pltpu.VMEM(grid.shape, narrow)],
        )

    *sent, up_taken = rows_out(half_buf, tokens, other_x, up_rows, other_up, take, order)
    *sent, down_taken = rows_out(
        buf, cotangent, other_d, down_rows, other_down, take, order, *sent
    )
    cells = exchange(sent, "loop", True)
    square = struct(cols * size, size)
    *sent, activated, grad_pre, take_up, take_down = call(
        columns(chips, rows, cols),
        [buf] * chips + [grid] * 2 + [struct(size, size)] * 2,
        *cells,
        up_second.reshape(square.shape),
        down_first.reshape(square.shape),
        perm_up.reshape(1, size),
        perm_down.reshape(1, size),
    )
    back = exchange(sent, "loop", False)
    (col_grads,) = call(
        column_grads(chips, rows, cols),
        [struct(2 * cols * size, size)],
        *cells,
        activated,
        grad_pre,
        take_up,
        take_down,
    )

    def over_dp(value, apart):
        return lax.ppermute(value, "dp", [(s, s ^ apart) for s in range(dps)])

    sums, back_rows, grad_rows = call(
        row_grads(chips, rows, cols, half),
        [struct(2 * grid_rows, block), grid, grid],
        *back,
        tokens,
        other_x,
        cotangent,
        other_d,
        order_back,
        col_grads,
    )
    sums_got = over_dp(sums, dps - 1)
    partial = struct(feature_rows, toks, wide)
    both = struct(2 * feature_rows, toks)
    mixed, grad_tokens, branches, col_sum = call(
        row_outputs(half),
        [partial, partial, both, struct(*col_grads.shape)],
        back_rows,
        tokens,
        down_taken,
        grad_rows,
        cotangent,
        up_taken,
        col_grads,
        over_dp(col_grads, dps - 1),
    )
    kept, leaving = call(add_halves, [taken, taken], sums, sums_got)

    def to_partner(value, apart):
        pairs = [(s, s ^ (apart * loops + 1)) for s in range(dps * loops)]
        return lax.ppermute(value, ("dp", "loop"), pairs)

    parts = (kept, over_dp(kept, 1), to_partner(leaving, 1), from_partner(leaving, "loop", 0))
    scale = 1.0 / math.sqrt(dps * toks)
    token = struct(8, 128, wide)
    g_up_second, g_down_first, done = call(
        total_col_grads(scale),
        [struct(*square.shape, wide)] * 2 + [token],
        col_sum,
        over_dp(col_sum, 1),
        to_hbm=2,
        micros=COL_MICROS,
    )
    mixed, grad_tokens, done = call(
        add_partner,
        [full] * 2 + [token],
        mixed,
        grad_tokens,
        from_partner(branches, "loop", 0),
        done,
        to_hbm=2,
    )
    g_up_first, g_down_second = call(
        total_grads(scale),
        [struct(rows * all_cols, block, wide)] * 2,
        *parts,
        place,
        done,
        to_hbm=2,
    )
    return (
        mixed,
        grad_tokens,
        g_up_first.reshape(up_first.shape),
        g_up_second.reshape(up_second.shape),
        g_down_first.reshape(down_first.shape),
        g_down_second.reshape(down_second.shape),
    )


def solution(mesh):
    in_specs = (
        P("loop", "dp"),
        P("loop", "dp"),
        P("loop", None, None),
        P("loop", None, None),
        P("loop", None, None),
        P("loop", None, None),
        P(),
        P(),
    )
    out_specs = (
        P("loop", "dp"),
        P("loop", "dp"),
        P("loop", None, None),
        P("loop", None, None),
        P("loop", None, None),
        P("loop", None, None),
    )
    return jax.shard_map(shards, mesh=mesh, in_specs=in_specs, out_specs=out_specs, check_vma=False)
```

```python
import math

import jax
import jax.numpy as jnp
from jax import lax
from jax.experimental import pallas as pl
from jax.experimental.pallas import tpu as pltpu
from jax.sharding import PartitionSpec as P


def from_partner(value, axis, apart):
    mask = 2**apart
    pairs = [(source, source ^ mask) for source in range(lax.axis_size(axis))]
    return lax.ppermute(value, axis, pairs)


def gelu_parts(pre_act):
    cumul = 0.5 * (1.0 + jax.scipy.special.erf(pre_act * (1.0 / math.sqrt(2.0))))
    slope = cumul + pre_act * jnp.exp(-0.5 * pre_act * pre_act) * (1.0 / math.sqrt(2.0 * math.pi))
    return (pre_act * cumul, slope)


def inverse_of(permute):
    return (
        jnp.zeros(permute.shape, jnp.int32)
        .at[permute]
        .set(jnp.arange(permute.shape[0], dtype=jnp.int32))
    )


def pair_total(contrib, half_width, parity):
    pair_blocks = contrib.shape[0]
    tok_count = contrib.shape[2]
    leaving = lax.dynamic_slice_in_dim(contrib, (1 - parity) * half_width, half_width, 1)
    other = from_partner(leaving.astype(jnp.bfloat16), "loop", 0).astype(leaving.dtype)
    mine = lax.dynamic_slice_in_dim(contrib, parity * half_width, half_width, 1) + other
    return mine.reshape(pair_blocks * half_width, tok_count)


def plain_shards(tokens, cotangent, up_first, up_second, down_first, down_second, perm_up, perm_down):
    wide = jnp.float32
    narrow = jnp.bfloat16
    feature_rows = tokens.shape[0]
    tok_count = tokens.shape[1]
    local_rows = up_first.shape[0]
    block = up_first.shape[2]
    half_width = block // 2
    pair_blocks = 2 * feature_rows // block
    group = 2 * local_rows // pair_blocks
    parity = lax.axis_index("loop") % 2
    other_x, other_d = from_partner((tokens, cotangent), "loop", 0)
    low_x = jnp.where(parity == 0, tokens, other_x)
    high_x = jnp.where(parity == 0, other_x, tokens)
    low_d = jnp.where(parity == 0, cotangent, other_d)
    high_d = jnp.where(parity == 0, other_d, cotangent)
    x_blocks = jnp.concatenate(
        [
            low_x.reshape(pair_blocks, half_width, tok_count),
            high_x.reshape(pair_blocks, half_width, tok_count),
        ],
        1,
    )
    d_blocks = jnp.concatenate(
        [
            low_d.reshape(pair_blocks, half_width, tok_count),
            high_d.reshape(pair_blocks, half_width, tok_count),
        ],
        1,
    )
    row_block = (parity * local_rows + jnp.arange(local_rows, dtype=jnp.int32)) // group
    picker = row_block[:, None] == jnp.arange(pair_blocks, dtype=jnp.int32)[None, :]
    picker_narrow = picker.astype(narrow)
    picker_wide = picker.astype(wide)
    x_rows = jnp.einsum("am,mit->ait", picker_narrow, x_blocks, preferred_element_type=wide).astype(
        narrow
    )
    d_rows = jnp.einsum("am,mit->ait", picker_narrow, d_blocks, preferred_element_type=wide).astype(
        narrow
    )
    inverse_up = inverse_of(perm_up)
    inverse_down = inverse_of(perm_down)
    hidden_one = jnp.einsum("abi,ait->abt", up_first, x_rows, preferred_element_type=wide).astype(
        narrow
    )
    permuted = jnp.take(
        lax.all_to_all(hidden_one, "loop", split_axis=1, concat_axis=0, tiled=True), perm_up, axis=0
    )
    pre_act = jnp.einsum("boa,abt->bot", up_second, permuted, preferred_element_type=wide)
    gelu_val, slope = gelu_parts(pre_act)
    activated = gelu_val.astype(narrow)
    mixed_cols = jnp.einsum(
        "bpo,bot->pbt", down_first, activated, preferred_element_type=wide
    ).astype(narrow)
    leaving = jnp.take(mixed_cols, perm_down, axis=0)
    back_rows = lax.all_to_all(leaving, "loop", split_axis=0, concat_axis=1, tiled=True)
    back_rows, permuted, activated, slope = (back_rows, permuted, activated, slope)
    out_rows = jnp.einsum("abo,abt->aot", down_second, back_rows, preferred_element_type=wide)
    out_contrib = jnp.einsum("am,aot->mot", picker_wide, out_rows, precision=lax.Precision.HIGHEST)
    branch_out = pair_total(out_contrib, half_width, parity)
    mixed = (tokens.astype(wide) + branch_out).astype(narrow)
    scale = 1.0 / math.sqrt(lax.axis_size("dp") * tok_count)
    grad_rows = jnp.einsum("abo,aot->abt", down_second, d_rows, preferred_element_type=wide).astype(
        narrow
    )
    g_down_second = jnp.einsum("abt,aot->abo", back_rows, d_rows, preferred_element_type=wide)
    grad_cols = lax.all_to_all(grad_rows, "loop", split_axis=1, concat_axis=0, tiled=True)
    grad_mixed = jnp.take(grad_cols, inverse_down, axis=0)
    grad_act = jnp.einsum("bpo,pbt->bot", down_first, grad_mixed, preferred_element_type=wide)
    g_down_first = jnp.einsum("pbt,bot->bpo", grad_mixed, activated, preferred_element_type=wide)
    grad_pre = (grad_act * slope).astype(narrow)
    g_up_second = jnp.einsum("bot,abt->boa", grad_pre, permuted, preferred_element_type=wide)
    grad_perm = jnp.einsum("boa,bot->abt", up_second, grad_pre, preferred_element_type=wide).astype(
        narrow
    )
    grad_recv = jnp.take(grad_perm, inverse_up, axis=0)
    grad_hidden = lax.all_to_all(grad_recv, "loop", split_axis=0, concat_axis=1, tiled=True)
    g_up_first = jnp.einsum("abt,ait->abi", grad_hidden, x_rows, preferred_element_type=wide)
    g_up_first, g_up_second, g_down_first, g_down_second = (
        lax.psum(g_up_first.astype(jnp.bfloat16), "dp").astype(jnp.float32),
        lax.psum(g_up_second.astype(jnp.bfloat16), "dp").astype(jnp.float32),
        lax.psum(g_down_first.astype(jnp.bfloat16), "dp").astype(jnp.float32),
        lax.psum(g_down_second.astype(jnp.bfloat16), "dp").astype(jnp.float32),
    )
    grad_rows_in = jnp.einsum("abi,abt->ait", up_first, grad_hidden, preferred_element_type=wide)
    grad_contrib = jnp.einsum(
        "am,ait->mit", picker_wide, grad_rows_in, precision=lax.Precision.HIGHEST
    )
    grad_branch = pair_total(grad_contrib, half_width, parity)
    grad_tokens = (cotangent.astype(wide) + grad_branch).astype(narrow)
    return (
        mixed,
        grad_tokens,
        g_up_first * scale,
        g_up_second * scale,
        g_down_first * scale,
        g_down_second * scale,
    )


VMEM_LIMIT = 16 * 2**20
COL_MICROS = 28
FIRST_ORDER = (1, 2, 3)
BACK_ORDER = (2, 1, 3)
COL_APART = (2, 1)
ROW_APART = (2, 1)


def dot(left, right, left_dim=1, right_dim=0):
    return lax.dot_general(
        left, right, (((left_dim,), (right_dim,)), ((), ())), preferred_element_type=jnp.float32
    )


def call(body, outs, *args, scratch=(), micros=0.01, to_hbm=0, aliases=()):
    whole = pl.BlockSpec(memory_space=pltpu.VMEM)
    return pl.pallas_call(
        body,
        out_shape=outs,
        in_specs=[whole] * len(args),
        out_specs=[pl.BlockSpec()] * to_hbm + [whole] * (len(outs) - to_hbm),
        scratch_shapes=list(scratch),
        input_output_aliases=dict(aliases),
        compiler_params=pltpu.CompilerParams(vmem_limit_bytes=VMEM_LIMIT),
        cost_estimate=pl.CostEstimate(
            flops=int(micros * 1e9), bytes_accessed=int(micros * 3e6), transcendentals=0
        ),
    )(*args)


def own_first(weights, parity):
    half = weights.shape[1] // 2
    return jnp.where(parity == 0, weights, pltpu.roll(weights, half, 1))


def one_hot(rows, cols, at):
    lead = lax.broadcasted_iota(jnp.int32, (rows, cols), 0)
    lane = lax.broadcasted_iota(jnp.int32, (rows, cols), 1)
    return at(lead, lane).astype(jnp.bfloat16)


def pair_cols(me, chips, rows, cols, turn):
    mine = chips * cols
    every = 2 * mine

    def at(lead, lane):
        chip = (me // 2) ^ ((lane // cols) % chips)
        col = (2 * chip + ((me % 2) ^ turn)) * cols + lane % cols
        return lead == (lane // mine) * every + col

    return one_hot(rows * every, rows * mine, at)


def sent_order(chips, rows, cols, sent_dim):
    def at(lead, lane):
        sent, kept = (lead, lane) if sent_dim == 0 else (lane, lead)
        q, rest = sent // (cols * 2 * rows), sent % (cols * 2 * rows)
        b, row = rest // (2 * rows), rest % (2 * rows)
        return kept == row * (chips * cols) + q * cols + b

    size = 2 * rows * chips * cols
    return one_hot(size, size, at)


def block_rows(own_ref, other_ref, start, half):
    span = pl.ds(pl.multiple_of(start, half), half)
    return jnp.concatenate([own_ref[span, :], other_ref[span, :]], 0)


def pair_blocks_of(parity, pair_blocks):
    local = pair_blocks // 2
    return [(parity if at < local else 1 - parity) * local + at % local for at in range(pair_blocks)]


def tables(chips, rows, cols):
    def body(take_ref, order_ref, back_ref, place_ref):
        me = lax.axis_index("loop")
        places = [pair_cols(me, chips, rows, cols, turn) for turn in (0, 1)]
        take_ref[...] = places[0]
        order_ref[...] = sent_order(chips, rows, cols, 0)
        back_ref[...] = sent_order(chips, rows, cols, 1)
        place_ref[...] = jnp.concatenate(places, 1)

    return body


def first_rows(chips, rows, cols, half):
    narrow = jnp.bfloat16

    def body(*refs):
        (own_ref, other_ref, *weights, take_ref, order_ref) = refs[:6]
        earlier, outs, (taken_ref, grid_ref) = refs[6 : -chips - 2], refs[-chips - 2 : -2], refs[-2:]
        parity = lax.axis_index("loop") % 2
        pair_blocks = own_ref.shape[0] // half
        taken = [own_first(dot(take_ref[...], ref[...], 0, 0), parity) for ref in weights]
        taken_ref[...] = jnp.concatenate(taken, 0).astype(narrow)
        high = taken_ref.shape[0] // pair_blocks
        for at, block in enumerate(pair_blocks_of(parity, pair_blocks)):
            part = slice(at * high, (at + 1) * high)
            features = block_rows(own_ref, other_ref, block * half, half)
            grid_ref[part, :] = dot(taken_ref[part, :], features).astype(narrow)
        sent = dot(order_ref[...], grid_ref[...]).astype(narrow)
        unit = 2 * rows * cols
        for q, out in enumerate(outs):
            if earlier:
                out[:unit, :] = earlier[q][...]
            out[out.shape[0] - unit :, :] = sent[q * unit : (q + 1) * unit]

    return body


def by_distance(bufs, order):
    return [bufs[0], *(bufs[1 + order.index(q)] for q in range(1, len(bufs)))]


def one_col(bufs, at, deep):
    return jnp.concatenate([r[at * deep : (at + 1) * deep, :] for r in bufs], 0)


def spread(outs, at, deep, value):
    for q, out in enumerate(outs):
        out[at * deep : (at + 1) * deep, :] = value[q * deep : (q + 1) * deep]


def columns(chips, rows, cols):
    narrow = jnp.bfloat16
    deep = 2 * rows

    def body(*refs):
        bufs, rest = by_distance(refs[:chips], FIRST_ORDER), refs[chips:]
        up_ref, down_ref, perm_up_ref, perm_down_ref = rest[:4]
        outs, rest = rest[4 : 4 + chips], rest[4 + chips :]
        activated_ref, grad_pre_ref, take_up_ref, take_down_ref = rest
        me = lax.axis_index("loop")
        size = chips * deep
        lead = lax.broadcasted_iota(jnp.int32, (size, size), 0)
        lane = lax.broadcasted_iota(jnp.int32, (size, size), 1)
        row = ((lead // rows) ^ me) * rows + lead % rows
        take_up_ref[...] = (perm_up_ref[...] == row).astype(narrow)
        take_down_ref[...] = dot(
            (lane == row).astype(narrow), (perm_down_ref[...] == lead).astype(narrow), 1, 1
        ).astype(narrow)
        for b in range(cols):
            span = slice(b * size, (b + 1) * size)
            up = dot(up_ref[span, :], take_up_ref[...], 1, 1).astype(narrow)
            down = dot(take_down_ref[...], down_ref[span, :]).astype(narrow)
            gelu_val, slope = gelu_parts(dot(up, one_col(bufs, b, deep)))
            activated = gelu_val.astype(narrow)
            activated_ref[span, :] = activated
            spread(outs, b, deep, dot(down, activated).astype(narrow))
            grad_act = dot(down, one_col(bufs, cols + b, deep), 0, 0)
            grad_pre = (grad_act * slope).astype(narrow)
            grad_pre_ref[span, :] = grad_pre
            spread(outs, cols + b, deep, dot(up, grad_pre, 0, 0).astype(narrow))

    return body


def column_grads(chips, rows, cols):
    narrow = jnp.bfloat16
    deep = 2 * rows

    def body(*refs):
        bufs = by_distance(refs[:chips], FIRST_ORDER)
        activated_ref, grad_pre_ref, take_up_ref, take_down_ref, out_ref = refs[chips:]
        size = chips * deep
        for b in range(cols):
            span = slice(b * size, (b + 1) * size)
            hid = one_col(bufs, b, deep)
            grad = one_col(bufs, cols + b, deep)
            g_up = dot(grad_pre_ref[span, :], hid, 1, 1).astype(narrow)
            g_down = dot(grad, activated_ref[span, :], 1, 1).astype(narrow)
            out_ref[span, :] = dot(g_up, take_up_ref[...]).astype(narrow)
            out_ref[cols * size + b * size : cols * size + (b + 1) * size, :] = dot(
                take_down_ref[...], g_down, 0, 0
            ).astype(narrow)

    return body


def row_grads(chips, rows, cols, half):
    narrow = jnp.bfloat16

    def body(*refs):
        bufs = by_distance(refs[:chips], BACK_ORDER)
        tok_ref, x_ref, cot_ref, d_ref, order_ref = refs[chips : chips + 5]
        grads_ref, back_ref, grad_ref = refs[-3:]
        parity = lax.axis_index("loop") % 2
        pair_blocks = tok_ref.shape[0] // half
        unit = 2 * rows * cols
        jobs = ((1, grad_ref, tok_ref, x_ref), (0, back_ref, cot_ref, d_ref))
        for at, (job, grid_ref, own_ref, other_ref) in enumerate(jobs):
            sent = one_col(bufs, job, unit)
            grid_ref[...] = dot(order_ref[...], sent).astype(narrow)
            high = grid_ref.shape[0] // pair_blocks
            grads = []
            for place, block in enumerate(pair_blocks_of(parity, pair_blocks)):
                part = slice(place * high, (place + 1) * high)
                features = block_rows(own_ref, other_ref, block * half, half)
                grads.append(dot(grid_ref[part, :], features, 1, 1))
            both = own_first(jnp.concatenate(grads, 0), parity).astype(narrow)
            size = both.shape[0] // 2
            for turn in range(2):
                start = (2 * turn + at) * size
                grads_ref[start : start + size, :] = both[turn * size : (turn + 1) * size]

    return body


def row_outputs(half):
    def body(*refs):
        jobs, col_refs, (*kept_refs, sent_ref, sum_ref) = (refs[:3], refs[3:6]), refs[6:8], refs[8:]
        add(*col_refs, sum_ref)
        parity = lax.axis_index("loop") % 2
        for at, (grid_ref, own_ref, weights_ref) in enumerate(jobs):
            kept_ref, features = kept_refs[at], own_ref.shape[0]
            pair_blocks = own_ref.shape[0] // half
            high = weights_ref.shape[0] // pair_blocks
            for place, block in enumerate(pair_blocks_of(parity, pair_blocks)):
                part = slice(place * high, (place + 1) * high)
                span = pl.ds(pl.multiple_of(block * half, half), half)
                branch = dot(weights_ref[part, :], grid_ref[part, :], 0, 0)
                kept_ref[span, :] = own_ref[span, :].astype(jnp.float32) + branch[:half]
                span = pl.ds(pl.multiple_of(at * features + block * half, half), half)
                sent_ref[span, :] = branch[half:].astype(jnp.bfloat16)

    return body


def add_partner(mixed_ref, grad_ref, got_ref, _, mixed_out, grad_out, done_ref):
    size = mixed_ref.shape[0]
    for at, (kept, out) in enumerate(((mixed_ref, mixed_out), (grad_ref, grad_out))):
        got = got_ref[at * size : (at + 1) * size, :].astype(jnp.float32)
        out[...] = (kept[...] + got).astype(out.dtype)
    done_ref[...] = jnp.zeros_like(done_ref)


def add(left_ref, right_ref, out_ref):
    total = left_ref[...].astype(jnp.float32) + right_ref[...].astype(jnp.float32)
    out_ref[...] = total.astype(out_ref.dtype)


def add_halves(left_ref, right_ref, kept_ref, leave_ref):
    size = kept_ref.shape[0]
    for at, out in enumerate((kept_ref, leave_ref)):
        span = slice(at * size, (at + 1) * size)
        total = left_ref[span, :].astype(jnp.float32) + right_ref[span, :].astype(jnp.float32)
        out[...] = total.astype(out.dtype)


def total_grads(scale):
    def body(*refs):
        parts, place_ref, outs = refs[:4], refs[4], refs[-2:]
        size = parts[0].shape[0] // 2
        near, far = place_ref[:, :size], place_ref[:, size:]
        place = jnp.concatenate([near, near, far, far], 1)
        for at, out in enumerate(outs):
            span = slice(at * size, (at + 1) * size)
            out[...] = dot(place, jnp.concatenate([r[span, :] for r in parts], 0)) * scale

    return body


def total_col_grads(scale):
    def body(sum_ref, got_ref, up_ref, down_ref, done_ref):
        done_ref[...] = jnp.zeros_like(done_ref)
        size = up_ref.shape[0]
        for at, out in enumerate((up_ref, down_ref)):
            span = slice(at * size, (at + 1) * size)
            both = sum_ref[span, :].astype(jnp.float32) + got_ref[span, :].astype(jnp.float32)
            out[...] = both * scale

    return body


def exchange(bufs, axis, order):
    pairs = {q: [(s, s ^ (2 * q)) for s in range(2 * len(bufs))] for q in order}
    return [bufs[0]] + [lax.ppermute(bufs[q], axis, pairs[q]) for q in order]


def shards(tokens, cotangent, up_first, up_second, down_first, down_second, perm_up, perm_down):
    narrow = jnp.bfloat16
    wide = jnp.float32
    loops, dps = lax.axis_size("loop"), lax.axis_size("dp")
    feature_rows, toks = tokens.shape
    rows, all_cols, block = up_first.shape
    cols, size = up_second.shape[:2]
    half = block // 2
    pair_blocks = feature_rows // half
    if loops != 8 or dps != 4 or rows % 16 or pair_blocks % 2 or 2 * rows * cols * loops // 2 % (16 * pair_blocks):
        return plain_shards(
            tokens, cotangent, up_first, up_second, down_first, down_second, perm_up, perm_down
        )
    chips = loops // 2

    def struct(lead, width, dtype=narrow):
        return jax.ShapeDtypeStruct((lead, width), dtype)

    up_rows = up_first.reshape(rows * all_cols, block)
    down_rows = down_second.reshape(rows * all_cols, block)
    grid_rows = 2 * rows * chips * cols
    half_buf = struct(2 * rows * cols, toks)
    buf = struct(4 * rows * cols, toks)
    grid = struct(grid_rows, toks)
    half_grid = struct(grid_rows // 2, toks)
    taken = struct(grid_rows, block)
    full = struct(feature_rows, toks)
    take, order, order_back, place = call(
        tables(chips, rows, cols),
        [struct(rows * all_cols, rows * chips * cols)] + [struct(grid_rows, grid_rows)] * 3,
        micros=4,
    )
    other_x = from_partner(tokens, "loop", 0)
    other_up = from_partner(up_rows, "loop", 0)
    other_down = from_partner(down_rows, "loop", 0)
    leaving, other_up, other_down = lax.optimization_barrier((cotangent, other_up, other_down))
    other_d = from_partner(leaving, "loop", 0)

    def rows_out(out, *args):
        return call(
            first_rows(chips, rows, cols, half),
            [out] * chips + [taken],
            *args,
            scratch=[pltpu.VMEM(grid.shape, narrow)],
        )

    *sent, up_taken = rows_out(half_buf, tokens, other_x, up_rows, other_up, take, order)
    *sent, down_taken = rows_out(
        buf, cotangent, other_d, down_rows, other_down, take, order, *sent
    )
    cells = exchange(sent, "loop", FIRST_ORDER)
    square = struct(cols * size, size)
    *sent, activated, grad_pre, take_up, take_down = call(
        columns(chips, rows, cols),
        [buf] * chips + [grid] * 2 + [struct(size, size)] * 2,
        *cells,
        up_second.reshape(square.shape),
        down_first.reshape(square.shape),
        perm_up.reshape(1, size),
        perm_down.reshape(1, size),
    )
    back = exchange(sent, "loop", BACK_ORDER)
    (col_grads,) = call(
        column_grads(chips, rows, cols),
        [struct(2 * cols * size, size)],
        *cells,
        activated,
        grad_pre,
        take_up,
        take_down,
    )

    def over_dp(value, apart):
        return lax.ppermute(value, "dp", [(s, s ^ apart) for s in range(dps)])

    sums, back_rows, grad_rows = call(
        row_grads(chips, rows, cols, half),
        [struct(2 * grid_rows, block), grid, grid],
        *back,
        tokens,
        other_x,
        cotangent,
        other_d,
        order_back,
        col_grads,
    )
    sums_got = over_dp(sums, ROW_APART[0])
    partial = struct(feature_rows, toks, wide)
    both = struct(2 * feature_rows, toks)
    mixed, grad_tokens, branches, col_sum = call(
        row_outputs(half),
        [partial, partial, both, struct(*col_grads.shape)],
        back_rows,
        tokens,
        down_taken,
        grad_rows,
        cotangent,
        up_taken,
        col_grads,
        over_dp(col_grads, COL_APART[0]),
    )
    kept, leaving = call(add_halves, [taken, taken], sums, sums_got)

    def to_partner(value, apart):
        pairs = [(s, s ^ (apart * loops + 1)) for s in range(dps * loops)]
        return lax.ppermute(value, ("dp", "loop"), pairs)

    parts = (kept, over_dp(kept, ROW_APART[1]), to_partner(leaving, ROW_APART[1]), from_partner(leaving, "loop", 0))
    scale = 1.0 / math.sqrt(dps * toks)
    token = struct(8, 128, wide)
    g_up_second, g_down_first, done = call(
        total_col_grads(scale),
        [struct(*square.shape, wide)] * 2 + [token],
        col_sum,
        over_dp(col_sum, COL_APART[1]),
        to_hbm=2,
        micros=COL_MICROS,
    )
    mixed, grad_tokens, done = call(
        add_partner,
        [full] * 2 + [token],
        mixed,
        grad_tokens,
        from_partner(branches, "loop", 0),
        done,
        to_hbm=2,
    )
    g_up_first, g_down_second = call(
        total_grads(scale),
        [struct(rows * all_cols, block, wide)] * 2,
        *parts,
        place,
        done,
        to_hbm=2,
    )
    return (
        mixed,
        grad_tokens,
        g_up_first.reshape(up_first.shape),
        g_up_second.reshape(up_second.shape),
        g_down_first.reshape(down_first.shape),
        g_down_second.reshape(down_second.shape),
    )


def solution(mesh):
    in_specs = (
        P("loop", "dp"),
        P("loop", "dp"),
        P("loop", None, None),
        P("loop", None, None),
        P("loop", None, None),
        P("loop", None, None),
        P(),
        P(),
    )
    out_specs = (
        P("loop", "dp"),
        P("loop", "dp"),
        P("loop", None, None),
        P("loop", None, None),
        P("loop", None, None),
        P("loop", None, None),
    )
    return jax.shard_map(shards, mesh=mesh, in_specs=in_specs, out_specs=out_specs, check_vma=False)
```

```python
import math

import jax
import jax.numpy as jnp
from jax import lax
from jax.experimental import pallas as pl
from jax.experimental.pallas import tpu as pltpu
from jax.sharding import PartitionSpec as P


def from_partner(value, axis, apart):
    mask = 2**apart
    pairs = [(source, source ^ mask) for source in range(lax.axis_size(axis))]
    return lax.ppermute(value, axis, pairs)


def gelu_parts(pre_act):
    cumul = 0.5 * (1.0 + jax.scipy.special.erf(pre_act * (1.0 / math.sqrt(2.0))))
    slope = cumul + pre_act * jnp.exp(-0.5 * pre_act * pre_act) * (1.0 / math.sqrt(2.0 * math.pi))
    return (pre_act * cumul, slope)


def inverse_of(permute):
    return (
        jnp.zeros(permute.shape, jnp.int32)
        .at[permute]
        .set(jnp.arange(permute.shape[0], dtype=jnp.int32))
    )


def pair_total(contrib, half_width, parity):
    pair_blocks = contrib.shape[0]
    tok_count = contrib.shape[2]
    leaving = lax.dynamic_slice_in_dim(contrib, (1 - parity) * half_width, half_width, 1)
    other = from_partner(leaving.astype(jnp.bfloat16), "loop", 0).astype(leaving.dtype)
    mine = lax.dynamic_slice_in_dim(contrib, parity * half_width, half_width, 1) + other
    return mine.reshape(pair_blocks * half_width, tok_count)


def plain_shards(tokens, cotangent, up_first, up_second, down_first, down_second, perm_up, perm_down):
    wide = jnp.float32
    narrow = jnp.bfloat16
    feature_rows = tokens.shape[0]
    tok_count = tokens.shape[1]
    local_rows = up_first.shape[0]
    block = up_first.shape[2]
    half_width = block // 2
    pair_blocks = 2 * feature_rows // block
    group = 2 * local_rows // pair_blocks
    parity = lax.axis_index("loop") % 2
    other_x, other_d = from_partner((tokens, cotangent), "loop", 0)
    low_x = jnp.where(parity == 0, tokens, other_x)
    high_x = jnp.where(parity == 0, other_x, tokens)
    low_d = jnp.where(parity == 0, cotangent, other_d)
    high_d = jnp.where(parity == 0, other_d, cotangent)
    x_blocks = jnp.concatenate(
        [
            low_x.reshape(pair_blocks, half_width, tok_count),
            high_x.reshape(pair_blocks, half_width, tok_count),
        ],
        1,
    )
    d_blocks = jnp.concatenate(
        [
            low_d.reshape(pair_blocks, half_width, tok_count),
            high_d.reshape(pair_blocks, half_width, tok_count),
        ],
        1,
    )
    row_block = (parity * local_rows + jnp.arange(local_rows, dtype=jnp.int32)) // group
    picker = row_block[:, None] == jnp.arange(pair_blocks, dtype=jnp.int32)[None, :]
    picker_narrow = picker.astype(narrow)
    picker_wide = picker.astype(wide)
    x_rows = jnp.einsum("am,mit->ait", picker_narrow, x_blocks, preferred_element_type=wide).astype(
        narrow
    )
    d_rows = jnp.einsum("am,mit->ait", picker_narrow, d_blocks, preferred_element_type=wide).astype(
        narrow
    )
    inverse_up = inverse_of(perm_up)
    inverse_down = inverse_of(perm_down)
    hidden_one = jnp.einsum("abi,ait->abt", up_first, x_rows, preferred_element_type=wide).astype(
        narrow
    )
    permuted = jnp.take(
        lax.all_to_all(hidden_one, "loop", split_axis=1, concat_axis=0, tiled=True), perm_up, axis=0
    )
    pre_act = jnp.einsum("boa,abt->bot", up_second, permuted, preferred_element_type=wide)
    gelu_val, slope = gelu_parts(pre_act)
    activated = gelu_val.astype(narrow)
    mixed_cols = jnp.einsum(
        "bpo,bot->pbt", down_first, activated, preferred_element_type=wide
    ).astype(narrow)
    leaving = jnp.take(mixed_cols, perm_down, axis=0)
    back_rows = lax.all_to_all(leaving, "loop", split_axis=0, concat_axis=1, tiled=True)
    back_rows, permuted, activated, slope = (back_rows, permuted, activated, slope)
    out_rows = jnp.einsum("abo,abt->aot", down_second, back_rows, preferred_element_type=wide)
    out_contrib = jnp.einsum("am,aot->mot", picker_wide, out_rows, precision=lax.Precision.HIGHEST)
    branch_out = pair_total(out_contrib, half_width, parity)
    mixed = (tokens.astype(wide) + branch_out).astype(narrow)
    scale = 1.0 / math.sqrt(lax.axis_size("dp") * tok_count)
    grad_rows = jnp.einsum("abo,aot->abt", down_second, d_rows, preferred_element_type=wide).astype(
        narrow
    )
    g_down_second = jnp.einsum("abt,aot->abo", back_rows, d_rows, preferred_element_type=wide)
    grad_cols = lax.all_to_all(grad_rows, "loop", split_axis=1, concat_axis=0, tiled=True)
    grad_mixed = jnp.take(grad_cols, inverse_down, axis=0)
    grad_act = jnp.einsum("bpo,pbt->bot", down_first, grad_mixed, preferred_element_type=wide)
    g_down_first = jnp.einsum("pbt,bot->bpo", grad_mixed, activated, preferred_element_type=wide)
    grad_pre = (grad_act * slope).astype(narrow)
    g_up_second = jnp.einsum("bot,abt->boa", grad_pre, permuted, preferred_element_type=wide)
    grad_perm = jnp.einsum("boa,bot->abt", up_second, grad_pre, preferred_element_type=wide).astype(
        narrow
    )
    grad_recv = jnp.take(grad_perm, inverse_up, axis=0)
    grad_hidden = lax.all_to_all(grad_recv, "loop", split_axis=0, concat_axis=1, tiled=True)
    g_up_first = jnp.einsum("abt,ait->abi", grad_hidden, x_rows, preferred_element_type=wide)
    g_up_first, g_up_second, g_down_first, g_down_second = (
        lax.psum(g_up_first.astype(jnp.bfloat16), "dp").astype(jnp.float32),
        lax.psum(g_up_second.astype(jnp.bfloat16), "dp").astype(jnp.float32),
        lax.psum(g_down_first.astype(jnp.bfloat16), "dp").astype(jnp.float32),
        lax.psum(g_down_second.astype(jnp.bfloat16), "dp").astype(jnp.float32),
    )
    grad_rows_in = jnp.einsum("abi,abt->ait", up_first, grad_hidden, preferred_element_type=wide)
    grad_contrib = jnp.einsum(
        "am,ait->mit", picker_wide, grad_rows_in, precision=lax.Precision.HIGHEST
    )
    grad_branch = pair_total(grad_contrib, half_width, parity)
    grad_tokens = (cotangent.astype(wide) + grad_branch).astype(narrow)
    return (
        mixed,
        grad_tokens,
        g_up_first * scale,
        g_up_second * scale,
        g_down_first * scale,
        g_down_second * scale,
    )


VMEM_LIMIT = 16 * 2**20
COL_MICROS = 28
FIRST_ORDER = (1, 2, 3)
BACK_ORDER = (2, 1, 3)
COL_APART = (2, 1)
ROW_APART = (2, 1)


def dot(left, right, left_dim=1, right_dim=0):
    return lax.dot_general(
        left, right, (((left_dim,), (right_dim,)), ((), ())), preferred_element_type=jnp.float32
    )


def call(body, outs, *args, scratch=(), micros=0.01, to_hbm=0, aliases=()):
    whole = pl.BlockSpec(memory_space=pltpu.VMEM)
    return pl.pallas_call(
        body,
        out_shape=outs,
        in_specs=[whole] * len(args),
        out_specs=[pl.BlockSpec()] * to_hbm + [whole] * (len(outs) - to_hbm),
        scratch_shapes=list(scratch),
        input_output_aliases=dict(aliases),
        compiler_params=pltpu.CompilerParams(vmem_limit_bytes=VMEM_LIMIT),
        cost_estimate=pl.CostEstimate(
            flops=int(micros * 1e9), bytes_accessed=int(micros * 3e6), transcendentals=0
        ),
    )(*args)


def own_first(weights, parity):
    half = weights.shape[1] // 2
    return jnp.where(parity == 0, weights, pltpu.roll(weights, half, 1))


def one_hot(rows, cols, at):
    lead = lax.broadcasted_iota(jnp.int32, (rows, cols), 0)
    lane = lax.broadcasted_iota(jnp.int32, (rows, cols), 1)
    return at(lead, lane).astype(jnp.bfloat16)


def pair_cols(me, chips, rows, cols, turn):
    mine = chips * cols
    every = 2 * mine

    def at(lead, lane):
        chip = (me // 2) ^ ((lane // cols) % chips)
        col = (2 * chip + ((me % 2) ^ turn)) * cols + lane % cols
        return lead == (lane // mine) * every + col

    return one_hot(rows * every, rows * mine, at)


def sent_order(chips, rows, cols, sent_dim):
    def at(lead, lane):
        sent, kept = (lead, lane) if sent_dim == 0 else (lane, lead)
        q, rest = sent // (cols * 2 * rows), sent % (cols * 2 * rows)
        b, row = rest // (2 * rows), rest % (2 * rows)
        return kept == row * (chips * cols) + q * cols + b

    size = 2 * rows * chips * cols
    return one_hot(size, size, at)


def block_rows(own_ref, other_ref, start, half):
    span = pl.ds(pl.multiple_of(start, half), half)
    return jnp.concatenate([own_ref[span, :], other_ref[span, :]], 0)


def pair_blocks_of(parity, pair_blocks):
    local = pair_blocks // 2
    return [(parity if at < local else 1 - parity) * local + at % local for at in range(pair_blocks)]


def tables(chips, rows, cols):
    def body(take_ref, order_ref, back_ref, place_ref):
        me = lax.axis_index("loop")
        places = [pair_cols(me, chips, rows, cols, turn) for turn in (0, 1)]
        take_ref[...] = places[0]
        order_ref[...] = sent_order(chips, rows, cols, 0)
        back_ref[...] = sent_order(chips, rows, cols, 1)
        place_ref[...] = jnp.concatenate(places, 1)

    return body


def take_weights(take_ref, weight_refs, parity, out_ref):
    taken = [own_first(dot(take_ref[...], ref[...], 0, 0), parity) for ref in weight_refs]
    out_ref[...] = jnp.concatenate(taken, 0).astype(out_ref.dtype)


def send_rows(own_ref, other_ref, taken_ref, order_ref, grid_ref, outs, at, half, parity):
    pair_blocks = own_ref.shape[0] // half
    high = taken_ref.shape[0] // pair_blocks
    for place, block in enumerate(pair_blocks_of(parity, pair_blocks)):
        part = slice(place * high, (place + 1) * high)
        features = block_rows(own_ref, other_ref, block * half, half)
        grid_ref[part, :] = dot(taken_ref[part, :], features).astype(grid_ref.dtype)
    sent = dot(order_ref[...], grid_ref[...]).astype(grid_ref.dtype)
    unit = sent.shape[0] // len(outs)
    for q, out in enumerate(outs):
        out[at * unit : (at + 1) * unit, :] = sent[q * unit : (q + 1) * unit]


def token_rows(chips, half):
    def body(*refs):
        own_ref, other_ref, *weights, take_ref, order_ref = refs[:8]
        outs, (up_ref, down_ref, grid_ref) = refs[8 : 8 + chips], refs[8 + chips :]
        parity = lax.axis_index("loop") % 2
        take_weights(take_ref, weights[:2], parity, up_ref)
        send_rows(own_ref, other_ref, up_ref, order_ref, grid_ref, outs, 0, half, parity)
        take_weights(take_ref, weights[2:], parity, down_ref)

    return body


def cotangent_rows(chips, half):
    def body(*refs):
        own_ref, other_ref, down_ref, order_ref = refs[:4]
        earlier, outs, grid_ref = refs[4 : 4 + chips], refs[4 + chips : -1], refs[-1]
        for out, ref in zip(outs, earlier, strict=True):
            out[: ref.shape[0], :] = ref[...]
        parity = lax.axis_index("loop") % 2
        send_rows(own_ref, other_ref, down_ref, order_ref, grid_ref, outs, 1, half, parity)

    return body


def by_distance(bufs, order):
    return [bufs[0], *(bufs[1 + order.index(q)] for q in range(1, len(bufs)))]


def one_col(bufs, at, deep):
    return jnp.concatenate([r[at * deep : (at + 1) * deep, :] for r in bufs], 0)


def spread(outs, at, deep, value):
    for q, out in enumerate(outs):
        out[at * deep : (at + 1) * deep, :] = value[q * deep : (q + 1) * deep]


def column_weights(rows, cols):
    narrow = jnp.bfloat16

    def body(up_ref, down_ref, perm_up_ref, perm_down_ref, *outs):
        up_out, down_out, take_up_ref, take_down_ref = outs
        me = lax.axis_index("loop")
        size = take_up_ref.shape[0]
        lead = lax.broadcasted_iota(jnp.int32, (size, size), 0)
        lane = lax.broadcasted_iota(jnp.int32, (size, size), 1)
        row = ((lead // rows) ^ me) * rows + lead % rows
        take_up_ref[...] = (perm_up_ref[...] == row).astype(narrow)
        take_down_ref[...] = dot(
            (lane == row).astype(narrow), (perm_down_ref[...] == lead).astype(narrow), 1, 1
        ).astype(narrow)
        for b in range(cols):
            span = slice(b * size, (b + 1) * size)
            up_out[span, :] = dot(up_ref[span, :], take_up_ref[...], 1, 1).astype(narrow)
            down_out[span, :] = dot(take_down_ref[...], down_ref[span, :]).astype(narrow)

    return body


def columns(chips, rows, cols):
    narrow = jnp.bfloat16
    deep = 2 * rows

    def body(*refs):
        bufs, (up_ref, down_ref) = by_distance(refs[:chips], FIRST_ORDER), refs[chips : chips + 2]
        outs, (activated_ref, grad_pre_ref) = refs[chips + 2 : -2], refs[-2:]
        size = chips * deep
        for b in range(cols):
            span = slice(b * size, (b + 1) * size)
            up, down = up_ref[span, :], down_ref[span, :]
            gelu_val, slope = gelu_parts(dot(up, one_col(bufs, b, deep)))
            activated = gelu_val.astype(narrow)
            activated_ref[span, :] = activated
            spread(outs, b, deep, dot(down, activated).astype(narrow))
            grad_act = dot(down, one_col(bufs, cols + b, deep), 0, 0)
            grad_pre = (grad_act * slope).astype(narrow)
            grad_pre_ref[span, :] = grad_pre
            spread(outs, cols + b, deep, dot(up, grad_pre, 0, 0).astype(narrow))

    return body


def column_grads(chips, rows, cols):
    narrow = jnp.bfloat16
    deep = 2 * rows

    def body(*refs):
        bufs = by_distance(refs[:chips], FIRST_ORDER)
        activated_ref, grad_pre_ref, take_up_ref, take_down_ref, out_ref = refs[chips:]
        size = chips * deep
        for b in range(cols):
            span = slice(b * size, (b + 1) * size)
            hid = one_col(bufs, b, deep)
            grad = one_col(bufs, cols + b, deep)
            g_up = dot(grad_pre_ref[span, :], hid, 1, 1).astype(narrow)
            g_down = dot(grad, activated_ref[span, :], 1, 1).astype(narrow)
            out_ref[span, :] = dot(g_up, take_up_ref[...]).astype(narrow)
            out_ref[cols * size + b * size : cols * size + (b + 1) * size, :] = dot(
                take_down_ref[...], g_down, 0, 0
            ).astype(narrow)

    return body


def row_grads(chips, rows, cols, half):
    narrow = jnp.bfloat16

    def body(*refs):
        bufs = by_distance(refs[:chips], BACK_ORDER)
        tok_ref, x_ref, cot_ref, d_ref, order_ref = refs[chips : chips + 5]
        grads_ref, back_ref, grad_ref = refs[-3:]
        parity = lax.axis_index("loop") % 2
        pair_blocks = tok_ref.shape[0] // half
        unit = 2 * rows * cols
        jobs = ((1, grad_ref, tok_ref, x_ref), (0, back_ref, cot_ref, d_ref))
        for at, (job, grid_ref, own_ref, other_ref) in enumerate(jobs):
            sent = one_col(bufs, job, unit)
            grid_ref[...] = dot(order_ref[...], sent).astype(narrow)
            high = grid_ref.shape[0] // pair_blocks
            grads = []
            for place, block in enumerate(pair_blocks_of(parity, pair_blocks)):
                part = slice(place * high, (place + 1) * high)
                features = block_rows(own_ref, other_ref, block * half, half)
                grads.append(dot(grid_ref[part, :], features, 1, 1))
            both = own_first(jnp.concatenate(grads, 0), parity).astype(narrow)
            size = both.shape[0] // 2
            for turn in range(2):
                start = (2 * turn + at) * size
                grads_ref[start : start + size, :] = both[turn * size : (turn + 1) * size]

    return body


def row_outputs(half):
    def body(*refs):
        jobs, col_refs, (*kept_refs, sent_ref, sum_ref) = (refs[:3], refs[3:6]), refs[6:8], refs[8:]
        add(*col_refs, sum_ref)
        parity = lax.axis_index("loop") % 2
        for at, (grid_ref, own_ref, weights_ref) in enumerate(jobs):
            kept_ref, features = kept_refs[at], own_ref.shape[0]
            pair_blocks = own_ref.shape[0] // half
            high = weights_ref.shape[0] // pair_blocks
            for place, block in enumerate(pair_blocks_of(parity, pair_blocks)):
                part = slice(place * high, (place + 1) * high)
                span = pl.ds(pl.multiple_of(block * half, half), half)
                branch = dot(weights_ref[part, :], grid_ref[part, :], 0, 0)
                kept_ref[span, :] = own_ref[span, :].astype(jnp.float32) + branch[:half]
                span = pl.ds(pl.multiple_of(at * features + block * half, half), half)
                sent_ref[span, :] = branch[half:].astype(jnp.bfloat16)

    return body


def add_partner(mixed_ref, grad_ref, got_ref, _, mixed_out, grad_out, done_ref):
    size = mixed_ref.shape[0]
    for at, (kept, out) in enumerate(((mixed_ref, mixed_out), (grad_ref, grad_out))):
        got = got_ref[at * size : (at + 1) * size, :].astype(jnp.float32)
        out[...] = (kept[...] + got).astype(out.dtype)
    done_ref[...] = jnp.zeros_like(done_ref)


def add(left_ref, right_ref, out_ref):
    total = left_ref[...].astype(jnp.float32) + right_ref[...].astype(jnp.float32)
    out_ref[...] = total.astype(out_ref.dtype)


def add_halves(left_ref, right_ref, kept_ref, *leave_refs):
    size = kept_ref.shape[0]
    for at, outs in enumerate(((kept_ref, leave_refs[0]), leave_refs[1:])):
        span = slice(at * size, (at + 1) * size)
        total = left_ref[span, :].astype(jnp.float32) + right_ref[span, :].astype(jnp.float32)
        for out in outs:
            out[...] = total.astype(out.dtype)


def total_grads(scale):
    def body(*refs):
        parts, place_ref, outs = [refs[at] for at in (0, 2, 1, 3)], refs[4], refs[-2:]
        size = parts[0].shape[0] // 2
        near, far = place_ref[:, :size], place_ref[:, size:]
        place = jnp.concatenate([near, near, far, far], 1)
        for at, out in enumerate(outs):
            span = slice(at * size, (at + 1) * size)
            out[...] = dot(place, jnp.concatenate([r[span, :] for r in parts], 0)) * scale

    return body


def total_col_grads(scale):
    def body(sum_ref, got_ref, up_ref, down_ref, done_ref):
        done_ref[...] = jnp.zeros_like(done_ref)
        size = up_ref.shape[0]
        for at, out in enumerate((up_ref, down_ref)):
            span = slice(at * size, (at + 1) * size)
            both = sum_ref[span, :].astype(jnp.float32) + got_ref[span, :].astype(jnp.float32)
            out[...] = both * scale

    return body


def exchange(bufs, axis, order):
    pairs = {q: [(s, s ^ (2 * q)) for s in range(2 * len(bufs))] for q in order}
    return [bufs[0]] + [lax.ppermute(bufs[q], axis, pairs[q]) for q in order]


def shards(tokens, cotangent, up_first, up_second, down_first, down_second, perm_up, perm_down):
    narrow = jnp.bfloat16
    wide = jnp.float32
    loops, dps = lax.axis_size("loop"), lax.axis_size("dp")
    feature_rows, toks = tokens.shape
    rows, all_cols, block = up_first.shape
    cols, size = up_second.shape[:2]
    half = block // 2
    pair_blocks = feature_rows // half
    if loops != 8 or dps != 4 or rows % 16 or pair_blocks % 2 or 2 * rows * cols * loops // 2 % (16 * pair_blocks):
        return plain_shards(
            tokens, cotangent, up_first, up_second, down_first, down_second, perm_up, perm_down
        )
    chips = loops // 2

    def struct(lead, width, dtype=narrow):
        return jax.ShapeDtypeStruct((lead, width), dtype)

    up_rows = up_first.reshape(rows * all_cols, block)
    down_rows = down_second.reshape(rows * all_cols, block)
    grid_rows = 2 * rows * chips * cols
    half_buf = struct(2 * rows * cols, toks)
    buf = struct(4 * rows * cols, toks)
    grid = struct(grid_rows, toks)
    half_grid = struct(grid_rows // 2, toks)
    taken = struct(grid_rows, block)
    full = struct(feature_rows, toks)
    take, order, order_back, place = call(
        tables(chips, rows, cols),
        [struct(rows * all_cols, rows * chips * cols)] + [struct(grid_rows, grid_rows)] * 3,
        micros=4,
    )
    other_x = from_partner(tokens, "loop", 0)
    other_up = from_partner(up_rows, "loop", 0)
    other_down = from_partner(down_rows, "loop", 0)
    leaving, other_up, other_down = lax.optimization_barrier((cotangent, other_up, other_down))
    other_d = from_partner(leaving, "loop", 0)

    *sent, up_taken, down_taken = call(
        token_rows(chips, half),
        [half_buf] * chips + [taken] * 2,
        tokens,
        other_x,
        up_rows,
        other_up,
        down_rows,
        other_down,
        take,
        order,
        scratch=[pltpu.VMEM(grid.shape, narrow)],
    )
    sent = call(
        cotangent_rows(chips, half),
        [buf] * chips,
        cotangent,
        other_d,
        down_taken,
        order,
        *sent,
        scratch=[pltpu.VMEM(grid.shape, narrow)],
    )
    cells = exchange(sent, "loop", FIRST_ORDER)
    square = struct(cols * size, size)
    up_cols, down_cols, take_up, take_down = call(
        column_weights(rows, cols),
        [square] * 2 + [struct(size, size)] * 2,
        up_second.reshape(square.shape),
        down_first.reshape(square.shape),
        perm_up.reshape(1, size),
        perm_down.reshape(1, size),
        micros=2,
    )
    *sent, activated, grad_pre = call(
        columns(chips, rows, cols),
        [buf] * chips + [grid] * 2,
        *cells,
        up_cols,
        down_cols,
    )
    back = exchange(sent, "loop", BACK_ORDER)
    (col_grads,) = call(
        column_grads(chips, rows, cols),
        [struct(2 * cols * size, size)],
        *cells,
        activated,
        grad_pre,
        take_up,
        take_down,
    )

    def over_dp(value, apart):
        return lax.ppermute(value, "dp", [(s, s ^ apart) for s in range(dps)])

    sums, back_rows, grad_rows = call(
        row_grads(chips, rows, cols, half),
        [struct(2 * grid_rows, block), grid, grid],
        *back,
        tokens,
        other_x,
        cotangent,
        other_d,
        order_back,
        col_grads,
    )
    sums_got = over_dp(sums, ROW_APART[0])
    partial = struct(feature_rows, toks, wide)
    both = struct(2 * feature_rows, toks)
    mixed, grad_tokens, branches, col_sum = call(
        row_outputs(half),
        [partial, partial, both, struct(*col_grads.shape)],
        back_rows,
        tokens,
        down_taken,
        grad_rows,
        cotangent,
        up_taken,
        col_grads,
        over_dp(col_grads, COL_APART[0]),
    )
    kept, to_next, to_other, to_core = call(add_halves, [taken] * 4, sums, sums_got)

    def to_partner(value, apart):
        pairs = [(s, s ^ (apart * loops + 1)) for s in range(dps * loops)]
        return lax.ppermute(value, ("dp", "loop"), pairs)

    got = {}
    got['c'] = to_partner(to_other, ROW_APART[1])
    got['z'] = over_dp(to_next, ROW_APART[1])
    got['p'] = from_partner(to_core, "loop", 0)
    parts = (kept, got['c'], got['z'], got['p'])
    scale = 1.0 / math.sqrt(dps * toks)
    token = struct(8, 128, wide)
    g_up_second, g_down_first, done = call(
        total_col_grads(scale),
        [struct(*square.shape, wide)] * 2 + [token],
        col_sum,
        over_dp(col_sum, COL_APART[1]),
        to_hbm=2,
        micros=COL_MICROS,
    )
    mixed, grad_tokens, done = call(
        add_partner,
        [full] * 2 + [token],
        mixed,
        grad_tokens,
        from_partner(branches, "loop", 0),
        done,
        to_hbm=2,
    )
    g_up_first, g_down_second = call(
        total_grads(scale),
        [struct(rows * all_cols, block, wide)] * 2,
        *parts,
        place,
        done,
        to_hbm=2,
    )
    return (
        mixed,
        grad_tokens,
        g_up_first.reshape(up_first.shape),
        g_up_second.reshape(up_second.shape),
        g_down_first.reshape(down_first.shape),
        g_down_second.reshape(down_second.shape),
    )


def solution(mesh):
    in_specs = (
        P("loop", "dp"),
        P("loop", "dp"),
        P("loop", None, None),
        P("loop", None, None),
        P("loop", None, None),
        P("loop", None, None),
        P(),
        P(),
    )
    out_specs = (
        P("loop", "dp"),
        P("loop", "dp"),
        P("loop", None, None),
        P("loop", None, None),
        P("loop", None, None),
        P("loop", None, None),
    )
    return jax.shard_map(shards, mesh=mesh, in_specs=in_specs, out_specs=out_specs, check_vma=False)
```

```python
import math

import jax
import jax.numpy as jnp
from jax import lax
from jax.experimental import pallas as pl
from jax.experimental.pallas import tpu as pltpu
from jax.sharding import PartitionSpec as P


def from_partner(value, axis, apart):
    mask = 2**apart
    pairs = [(source, source ^ mask) for source in range(lax.axis_size(axis))]
    return lax.ppermute(value, axis, pairs)


def gelu_parts(pre_act):
    cumul = 0.5 * (1.0 + jax.scipy.special.erf(pre_act * (1.0 / math.sqrt(2.0))))
    slope = cumul + pre_act * jnp.exp(-0.5 * pre_act * pre_act) * (1.0 / math.sqrt(2.0 * math.pi))
    return (pre_act * cumul, slope)


def inverse_of(permute):
    return (
        jnp.zeros(permute.shape, jnp.int32)
        .at[permute]
        .set(jnp.arange(permute.shape[0], dtype=jnp.int32))
    )


def pair_total(contrib, half_width, parity):
    pair_blocks = contrib.shape[0]
    tok_count = contrib.shape[2]
    leaving = lax.dynamic_slice_in_dim(contrib, (1 - parity) * half_width, half_width, 1)
    other = from_partner(leaving.astype(jnp.bfloat16), "loop", 0).astype(leaving.dtype)
    mine = lax.dynamic_slice_in_dim(contrib, parity * half_width, half_width, 1) + other
    return mine.reshape(pair_blocks * half_width, tok_count)


def plain_shards(tokens, cotangent, up_first, up_second, down_first, down_second, perm_up, perm_down):
    wide = jnp.float32
    narrow = jnp.bfloat16
    feature_rows = tokens.shape[0]
    tok_count = tokens.shape[1]
    local_rows = up_first.shape[0]
    block = up_first.shape[2]
    half_width = block // 2
    pair_blocks = 2 * feature_rows // block
    group = 2 * local_rows // pair_blocks
    parity = lax.axis_index("loop") % 2
    other_x, other_d = from_partner((tokens, cotangent), "loop", 0)
    low_x = jnp.where(parity == 0, tokens, other_x)
    high_x = jnp.where(parity == 0, other_x, tokens)
    low_d = jnp.where(parity == 0, cotangent, other_d)
    high_d = jnp.where(parity == 0, other_d, cotangent)
    x_blocks = jnp.concatenate(
        [
            low_x.reshape(pair_blocks, half_width, tok_count),
            high_x.reshape(pair_blocks, half_width, tok_count),
        ],
        1,
    )
    d_blocks = jnp.concatenate(
        [
            low_d.reshape(pair_blocks, half_width, tok_count),
            high_d.reshape(pair_blocks, half_width, tok_count),
        ],
        1,
    )
    row_block = (parity * local_rows + jnp.arange(local_rows, dtype=jnp.int32)) // group
    picker = row_block[:, None] == jnp.arange(pair_blocks, dtype=jnp.int32)[None, :]
    picker_narrow = picker.astype(narrow)
    picker_wide = picker.astype(wide)
    x_rows = jnp.einsum("am,mit->ait", picker_narrow, x_blocks, preferred_element_type=wide).astype(
        narrow
    )
    d_rows = jnp.einsum("am,mit->ait", picker_narrow, d_blocks, preferred_element_type=wide).astype(
        narrow
    )
    inverse_up = inverse_of(perm_up)
    inverse_down = inverse_of(perm_down)
    hidden_one = jnp.einsum("abi,ait->abt", up_first, x_rows, preferred_element_type=wide).astype(
        narrow
    )
    permuted = jnp.take(
        lax.all_to_all(hidden_one, "loop", split_axis=1, concat_axis=0, tiled=True), perm_up, axis=0
    )
    pre_act = jnp.einsum("boa,abt->bot", up_second, permuted, preferred_element_type=wide)
    gelu_val, slope = gelu_parts(pre_act)
    activated = gelu_val.astype(narrow)
    mixed_cols = jnp.einsum(
        "bpo,bot->pbt", down_first, activated, preferred_element_type=wide
    ).astype(narrow)
    leaving = jnp.take(mixed_cols, perm_down, axis=0)
    back_rows = lax.all_to_all(leaving, "loop", split_axis=0, concat_axis=1, tiled=True)
    back_rows, permuted, activated, slope = (back_rows, permuted, activated, slope)
    out_rows = jnp.einsum("abo,abt->aot", down_second, back_rows, preferred_element_type=wide)
    out_contrib = jnp.einsum("am,aot->mot", picker_wide, out_rows, precision=lax.Precision.HIGHEST)
    branch_out = pair_total(out_contrib, half_width, parity)
    mixed = (tokens.astype(wide) + branch_out).astype(narrow)
    scale = 1.0 / math.sqrt(lax.axis_size("dp") * tok_count)
    grad_rows = jnp.einsum("abo,aot->abt", down_second, d_rows, preferred_element_type=wide).astype(
        narrow
    )
    g_down_second = jnp.einsum("abt,aot->abo", back_rows, d_rows, preferred_element_type=wide)
    grad_cols = lax.all_to_all(grad_rows, "loop", split_axis=1, concat_axis=0, tiled=True)
    grad_mixed = jnp.take(grad_cols, inverse_down, axis=0)
    grad_act = jnp.einsum("bpo,pbt->bot", down_first, grad_mixed, preferred_element_type=wide)
    g_down_first = jnp.einsum("pbt,bot->bpo", grad_mixed, activated, preferred_element_type=wide)
    grad_pre = (grad_act * slope).astype(narrow)
    g_up_second = jnp.einsum("bot,abt->boa", grad_pre, permuted, preferred_element_type=wide)
    grad_perm = jnp.einsum("boa,bot->abt", up_second, grad_pre, preferred_element_type=wide).astype(
        narrow
    )
    grad_recv = jnp.take(grad_perm, inverse_up, axis=0)
    grad_hidden = lax.all_to_all(grad_recv, "loop", split_axis=0, concat_axis=1, tiled=True)
    g_up_first = jnp.einsum("abt,ait->abi", grad_hidden, x_rows, preferred_element_type=wide)
    g_up_first, g_up_second, g_down_first, g_down_second = (
        lax.psum(g_up_first.astype(jnp.bfloat16), "dp").astype(jnp.float32),
        lax.psum(g_up_second.astype(jnp.bfloat16), "dp").astype(jnp.float32),
        lax.psum(g_down_first.astype(jnp.bfloat16), "dp").astype(jnp.float32),
        lax.psum(g_down_second.astype(jnp.bfloat16), "dp").astype(jnp.float32),
    )
    grad_rows_in = jnp.einsum("abi,abt->ait", up_first, grad_hidden, preferred_element_type=wide)
    grad_contrib = jnp.einsum(
        "am,ait->mit", picker_wide, grad_rows_in, precision=lax.Precision.HIGHEST
    )
    grad_branch = pair_total(grad_contrib, half_width, parity)
    grad_tokens = (cotangent.astype(wide) + grad_branch).astype(narrow)
    return (
        mixed,
        grad_tokens,
        g_up_first * scale,
        g_up_second * scale,
        g_down_first * scale,
        g_down_second * scale,
    )


VMEM_LIMIT = 16 * 2**20
COL_MICROS = 28
FIRST_ORDER = (1, 2, 3)
BACK_ORDER = (2, 1, 3)
COL_APART = (2, 1)
ROW_APART = (2, 1)


def dot(left, right, left_dim=1, right_dim=0):
    return lax.dot_general(
        left, right, (((left_dim,), (right_dim,)), ((), ())), preferred_element_type=jnp.float32
    )


def call(body, outs, *args, scratch=(), micros=0.01, to_hbm=0, aliases=()):
    whole = pl.BlockSpec(memory_space=pltpu.VMEM)
    return pl.pallas_call(
        body,
        out_shape=outs,
        in_specs=[whole] * len(args),
        out_specs=[pl.BlockSpec()] * to_hbm + [whole] * (len(outs) - to_hbm),
        scratch_shapes=list(scratch),
        input_output_aliases=dict(aliases),
        compiler_params=pltpu.CompilerParams(vmem_limit_bytes=VMEM_LIMIT),
        cost_estimate=pl.CostEstimate(
            flops=int(micros * 1e9), bytes_accessed=int(micros * 3e6), transcendentals=0
        ),
    )(*args)


def own_first(weights, parity):
    half = weights.shape[1] // 2
    return jnp.where(parity == 0, weights, pltpu.roll(weights, half, 1))


def one_hot(rows, cols, at):
    lead = lax.broadcasted_iota(jnp.int32, (rows, cols), 0)
    lane = lax.broadcasted_iota(jnp.int32, (rows, cols), 1)
    return at(lead, lane).astype(jnp.bfloat16)


def pair_cols(me, chips, rows, cols, turn):
    mine = chips * cols
    every = 2 * mine

    def at(lead, lane):
        chip = (me // 2) ^ ((lane // cols) % chips)
        col = (2 * chip + ((me % 2) ^ turn)) * cols + lane % cols
        return lead == (lane // mine) * every + col

    return one_hot(rows * every, rows * mine, at)


def sent_order(chips, rows, cols, sent_dim):
    def at(lead, lane):
        sent, kept = (lead, lane) if sent_dim == 0 else (lane, lead)
        q, rest = sent // (cols * 2 * rows), sent % (cols * 2 * rows)
        b, row = rest // (2 * rows), rest % (2 * rows)
        return kept == row * (chips * cols) + q * cols + b

    size = 2 * rows * chips * cols
    return one_hot(size, size, at)


def block_rows(own_ref, other_ref, start, half):
    span = pl.ds(pl.multiple_of(start, half), half)
    return jnp.concatenate([own_ref[span, :], other_ref[span, :]], 0)


def pair_blocks_of(parity, pair_blocks):
    local = pair_blocks // 2
    return [(parity if at < local else 1 - parity) * local + at % local for at in range(pair_blocks)]


def tables(chips, rows, cols):
    def body(take_ref, order_ref, back_ref, place_ref):
        me = lax.axis_index("loop")
        places = [pair_cols(me, chips, rows, cols, turn) for turn in (0, 1)]
        take_ref[...] = places[0]
        order_ref[...] = sent_order(chips, rows, cols, 0)
        back_ref[...] = sent_order(chips, rows, cols, 1)
        place_ref[...] = jnp.concatenate(places, 1)

    return body


def take_weights(take_ref, weight_refs, parity, out_ref):
    taken = [own_first(dot(take_ref[...], ref[...], 0, 0), parity) for ref in weight_refs]
    out_ref[...] = jnp.concatenate(taken, 0).astype(out_ref.dtype)


def send_rows(own_ref, other_ref, taken_ref, order_ref, grid_ref, outs, at, half, parity):
    pair_blocks = own_ref.shape[0] // half
    high = taken_ref.shape[0] // pair_blocks
    for place, block in enumerate(pair_blocks_of(parity, pair_blocks)):
        part = slice(place * high, (place + 1) * high)
        features = block_rows(own_ref, other_ref, block * half, half)
        grid_ref[part, :] = dot(taken_ref[part, :], features).astype(grid_ref.dtype)
    sent = dot(order_ref[...], grid_ref[...]).astype(grid_ref.dtype)
    unit = sent.shape[0] // len(outs)
    for q, out in enumerate(outs):
        out[at * unit : (at + 1) * unit, :] = sent[q * unit : (q + 1) * unit]


def token_rows(chips, half):
    def body(*refs):
        own_ref, other_ref, *weights, take_ref, order_ref = refs[:8]
        outs, (up_ref, down_ref, grid_ref) = refs[8 : 8 + chips], refs[8 + chips :]
        parity = lax.axis_index("loop") % 2
        take_weights(take_ref, weights[:2], parity, up_ref)
        send_rows(own_ref, other_ref, up_ref, order_ref, grid_ref, outs, 0, half, parity)
        take_weights(take_ref, weights[2:], parity, down_ref)

    return body


def cotangent_rows(chips, half):
    def body(*refs):
        own_ref, other_ref, down_ref, order_ref = refs[:4]
        earlier, outs, grid_ref = refs[4 : 4 + chips], refs[4 + chips : -1], refs[-1]
        for out, ref in zip(outs, earlier, strict=True):
            out[: ref.shape[0], :] = ref[...]
        parity = lax.axis_index("loop") % 2
        send_rows(own_ref, other_ref, down_ref, order_ref, grid_ref, outs, 1, half, parity)

    return body


def turn_blocks(half):
    def body(own_ref, other_ref, _, out_ref):
        parity = lax.axis_index("loop") % 2
        pair_blocks = own_ref.shape[0] // half
        for at, block in enumerate(pair_blocks_of(parity, pair_blocks)):
            features = block_rows(own_ref, other_ref, block * half, half)
            out_ref[:, at * 2 * half : (at + 1) * 2 * half] = features.T

    return body


def by_distance(bufs, order):
    return [bufs[0], *(bufs[1 + order.index(q)] for q in range(1, len(bufs)))]


def one_col(bufs, at, deep):
    return jnp.concatenate([r[at * deep : (at + 1) * deep, :] for r in bufs], 0)


def spread(outs, at, deep, value):
    for q, out in enumerate(outs):
        out[at * deep : (at + 1) * deep, :] = value[q * deep : (q + 1) * deep]


def column_weights(rows, cols):
    narrow = jnp.bfloat16

    def body(up_ref, down_ref, perm_up_ref, perm_down_ref, _, *outs):
        up_out, up_turned, down_out, down_turned, take_up_ref, take_down_ref = outs
        me = lax.axis_index("loop")
        size = take_up_ref.shape[0]
        lead = lax.broadcasted_iota(jnp.int32, (size, size), 0)
        lane = lax.broadcasted_iota(jnp.int32, (size, size), 1)
        row = ((lead // rows) ^ me) * rows + lead % rows
        take_up_ref[...] = (perm_up_ref[...] == row).astype(narrow)
        take_down_ref[...] = dot(
            (lane == row).astype(narrow), (perm_down_ref[...] == lead).astype(narrow), 1, 1
        ).astype(narrow)
        for b in range(cols):
            span = slice(b * size, (b + 1) * size)
            up = dot(up_ref[span, :], take_up_ref[...], 1, 1)
            down = dot(take_down_ref[...], down_ref[span, :])
            up_out[span, :] = up.astype(narrow)
            up_turned[span, :] = up.T.astype(narrow)
            down_out[span, :] = down.astype(narrow)
            down_turned[span, :] = down.T.astype(narrow)

    return body


def columns(chips, rows, cols):
    narrow = jnp.bfloat16
    deep = 2 * rows

    def body(*refs):
        bufs, weights = by_distance(refs[:chips], FIRST_ORDER), refs[chips : chips + 4]
        outs, (activated_ref, grad_pre_ref) = refs[-chips - 2 : -2], refs[-2:]
        size = chips * deep
        for b in range(cols):
            span = slice(b * size, (b + 1) * size)
            up, up_turned, down, down_turned = (ref[span, :] for ref in weights)
            gelu_val, slope = gelu_parts(dot(up, one_col(bufs, b, deep)))
            activated = gelu_val.astype(narrow)
            activated_ref[span, :] = activated
            spread(outs, b, deep, dot(down, activated).astype(narrow))
            grad_act = dot(down_turned, one_col(bufs, cols + b, deep))
            grad_pre = (grad_act * slope).astype(narrow)
            grad_pre_ref[span, :] = grad_pre
            spread(outs, cols + b, deep, dot(up_turned, grad_pre).astype(narrow))

    return body


def column_grads(chips, rows, cols):
    narrow = jnp.bfloat16
    deep = 2 * rows

    def body(*refs):
        bufs = by_distance(refs[:chips], FIRST_ORDER)
        activated_ref, grad_pre_ref, out_ref = refs[chips:]
        size = chips * deep
        for b in range(cols):
            span = slice(b * size, (b + 1) * size)
            hid = one_col(bufs, b, deep)
            grad = one_col(bufs, cols + b, deep)
            g_up = dot(grad_pre_ref[span, :], hid, 1, 1).astype(narrow)
            g_down = dot(grad, activated_ref[span, :], 1, 1).astype(narrow)
            out_ref[span, :] = g_up
            out_ref[cols * size + b * size : cols * size + (b + 1) * size, :] = g_down

    return body


def row_grads(chips, rows, cols, half):
    narrow = jnp.bfloat16

    def body(*refs):
        bufs = by_distance(refs[:chips], BACK_ORDER)
        x_ref, d_ref, order_ref = refs[chips : chips + 3]
        grads_ref, back_ref, grad_ref = refs[-3:]
        parity = lax.axis_index("loop") % 2
        block = 2 * half
        unit = 2 * rows * cols
        pair_blocks = x_ref.shape[1] // block
        jobs = ((1, grad_ref, x_ref), (0, back_ref, d_ref))
        for at, (job, grid_ref, turned_ref) in enumerate(jobs):
            grid_ref[...] = dot(order_ref[...], one_col(bufs, job, unit)).astype(narrow)
            high = grid_ref.shape[0] // pair_blocks
            grads = []
            for place in range(0, pair_blocks, 2):
                both = dot(
                    grid_ref[place * high : (place + 2) * high, :],
                    turned_ref[:, place * block : (place + 2) * block],
                )
                grads += [both[:high, :block], both[high:, block:]]
            both = own_first(jnp.concatenate(grads, 0), parity).astype(narrow)
            size = both.shape[0] // 2
            for turn in range(2):
                start = (2 * turn + at) * size
                grads_ref[start : start + size, :] = both[turn * size : (turn + 1) * size]

    return body


def row_outputs(half):
    def body(*refs):
        jobs, col_refs, (*kept_refs, sent_ref, sum_ref) = (refs[:3], refs[3:6]), refs[6:8], refs[8:]
        add(*col_refs, sum_ref)
        parity = lax.axis_index("loop") % 2
        for at, (grid_ref, own_ref, weights_ref) in enumerate(jobs):
            kept_ref, features = kept_refs[at], own_ref.shape[0]
            pair_blocks = own_ref.shape[0] // half
            high = weights_ref.shape[0] // pair_blocks
            for place, block in enumerate(pair_blocks_of(parity, pair_blocks)):
                part = slice(place * high, (place + 1) * high)
                span = pl.ds(pl.multiple_of(block * half, half), half)
                branch = dot(weights_ref[part, :], grid_ref[part, :], 0, 0)
                kept_ref[span, :] = own_ref[span, :].astype(jnp.float32) + branch[:half]
                span = pl.ds(pl.multiple_of(at * features + block * half, half), half)
                sent_ref[span, :] = branch[half:].astype(jnp.bfloat16)

    return body


def add_partner(mixed_ref, grad_ref, got_ref, _, mixed_out, grad_out, done_ref):
    size = mixed_ref.shape[0]
    for at, (kept, out) in enumerate(((mixed_ref, mixed_out), (grad_ref, grad_out))):
        got = got_ref[at * size : (at + 1) * size, :].astype(jnp.float32)
        out[...] = (kept[...] + got).astype(out.dtype)
    done_ref[...] = jnp.zeros_like(done_ref)


def add(left_ref, right_ref, out_ref):
    total = left_ref[...].astype(jnp.float32) + right_ref[...].astype(jnp.float32)
    out_ref[...] = total.astype(out_ref.dtype)


def add_halves(left_ref, right_ref, kept_ref, *leave_refs):
    size = kept_ref.shape[0]
    for at, outs in enumerate(((kept_ref, leave_refs[0]), leave_refs[1:])):
        span = slice(at * size, (at + 1) * size)
        total = left_ref[span, :].astype(jnp.float32) + right_ref[span, :].astype(jnp.float32)
        for out in outs:
            out[...] = total.astype(out.dtype)


def total_grads(scale):
    def body(*refs):
        parts, place_ref, outs = [refs[at] for at in (0, 2, 1, 3)], refs[4], refs[-2:]
        size = parts[0].shape[0] // 2
        near, far = place_ref[:, :size], place_ref[:, size:]
        place = jnp.concatenate([near, near, far, far], 1)
        for at, out in enumerate(outs):
            span = slice(at * size, (at + 1) * size)
            out[...] = dot(place, jnp.concatenate([r[span, :] for r in parts], 0)) * scale

    return body


def total_col_grads(scale):
    def body(sum_ref, got_ref, take_up_ref, take_down_ref, up_ref, down_ref, done_ref):
        done_ref[...] = jnp.zeros_like(done_ref)
        size = take_up_ref.shape[0]
        count = up_ref.shape[0]
        for start in range(0, count, size):
            near = slice(start, start + size)
            far = slice(count + start, count + start + size)
            up = [dot(ref[near, :], take_up_ref[...]) for ref in (sum_ref, got_ref)]
            down = [dot(take_down_ref[...], ref[far, :], 0, 0) for ref in (sum_ref, got_ref)]
            up_ref[near, :] = (up[0] + up[1]) * scale
            down_ref[near, :] = (down[0] + down[1]) * scale

    return body


def exchange(bufs, axis, order):
    pairs = {q: [(s, s ^ (2 * q)) for s in range(2 * len(bufs))] for q in order}
    return [bufs[0]] + [lax.ppermute(bufs[q], axis, pairs[q]) for q in order]


def shards(tokens, cotangent, up_first, up_second, down_first, down_second, perm_up, perm_down):
    narrow = jnp.bfloat16
    wide = jnp.float32
    loops, dps = lax.axis_size("loop"), lax.axis_size("dp")
    feature_rows, toks = tokens.shape
    rows, all_cols, block = up_first.shape
    cols, size = up_second.shape[:2]
    half = block // 2
    pair_blocks = feature_rows // half
    if loops != 8 or dps != 4 or rows % 16 or pair_blocks % 2 or 2 * rows * cols * loops // 2 % (16 * pair_blocks):
        return plain_shards(
            tokens, cotangent, up_first, up_second, down_first, down_second, perm_up, perm_down
        )
    chips = loops // 2

    def struct(lead, width, dtype=narrow):
        return jax.ShapeDtypeStruct((lead, width), dtype)

    up_rows = up_first.reshape(rows * all_cols, block)
    down_rows = down_second.reshape(rows * all_cols, block)
    grid_rows = 2 * rows * chips * cols
    half_buf = struct(2 * rows * cols, toks)
    buf = struct(4 * rows * cols, toks)
    grid = struct(grid_rows, toks)
    half_grid = struct(grid_rows // 2, toks)
    taken = struct(grid_rows, block)
    full = struct(feature_rows, toks)
    take, order, order_back, place = call(
        tables(chips, rows, cols),
        [struct(rows * all_cols, rows * chips * cols)] + [struct(grid_rows, grid_rows)] * 3,
        micros=4,
    )
    other_x = from_partner(tokens, "loop", 0)
    other_up = from_partner(up_rows, "loop", 0)
    other_down = from_partner(down_rows, "loop", 0)
    leaving, other_up, other_down = lax.optimization_barrier((cotangent, other_up, other_down))
    other_d = from_partner(leaving, "loop", 0)

    *sent, up_taken, down_taken = call(
        token_rows(chips, half),
        [half_buf] * chips + [taken] * 2,
        tokens,
        other_x,
        up_rows,
        other_up,
        down_rows,
        other_down,
        take,
        order,
        scratch=[pltpu.VMEM(grid.shape, narrow)],
    )
    sent = call(
        cotangent_rows(chips, half),
        [buf] * chips,
        cotangent,
        other_d,
        down_taken,
        order,
        *sent,
        scratch=[pltpu.VMEM(grid.shape, narrow)],
    )
    cells = exchange(sent, "loop", FIRST_ORDER)
    square = struct(cols * size, size)
    *col_weights, take_up, take_down = call(
        column_weights(rows, cols),
        [square] * 4 + [struct(size, size)] * 2,
        up_second.reshape(square.shape),
        down_first.reshape(square.shape),
        perm_up.reshape(1, size),
        perm_down.reshape(1, size),
        sent[0],
        micros=2,
    )
    turned = struct(toks, 2 * feature_rows)
    (x_turned,) = call(turn_blocks(half), [turned], tokens, other_x, sent[0], micros=1)
    (d_turned,) = call(turn_blocks(half), [turned], cotangent, other_d, sent[0], micros=1)
    *sent, activated, grad_pre = call(
        columns(chips, rows, cols),
        [buf] * chips + [grid] * 2,
        *cells,
        *col_weights,
        x_turned,
        d_turned,
    )
    back = exchange(sent, "loop", BACK_ORDER)
    (col_grads,) = call(
        column_grads(chips, rows, cols),
        [struct(2 * cols * size, size)],
        *cells,
        activated,
        grad_pre,
    )

    def over_dp(value, apart):
        return lax.ppermute(value, "dp", [(s, s ^ apart) for s in range(dps)])

    sums, back_rows, grad_rows = call(
        row_grads(chips, rows, cols, half),
        [struct(2 * grid_rows, block), grid, grid],
        *back,
        x_turned,
        d_turned,
        order_back,
        col_grads,
    )
    sums_got = over_dp(sums, ROW_APART[0])
    partial = struct(feature_rows, toks, wide)
    both = struct(2 * feature_rows, toks)
    mixed, grad_tokens, branches, col_sum = call(
        row_outputs(half),
        [partial, partial, both, struct(*col_grads.shape)],
        back_rows,
        tokens,
        down_taken,
        grad_rows,
        cotangent,
        up_taken,
        col_grads,
        over_dp(col_grads, COL_APART[0]),
    )
    kept, to_next, to_other, to_core = call(add_halves, [taken] * 4, sums, sums_got)

    def to_partner(value, apart):
        pairs = [(s, s ^ (apart * loops + 1)) for s in range(dps * loops)]
        return lax.ppermute(value, ("dp", "loop"), pairs)

    got = {}
    got['c'] = to_partner(to_other, ROW_APART[1])
    got['z'] = over_dp(to_next, ROW_APART[1])
    got['p'] = from_partner(to_core, "loop", 0)
    parts = (kept, got['c'], got['z'], got['p'])
    scale = 1.0 / math.sqrt(dps * toks)
    token = struct(8, 128, wide)
    g_up_second, g_down_first, done = call(
        total_col_grads(scale),
        [struct(*square.shape, wide)] * 2 + [token],
        col_sum,
        over_dp(col_sum, COL_APART[1]),
        take_up,
        take_down,
        to_hbm=2,
        micros=COL_MICROS,
    )
    mixed, grad_tokens, done = call(
        add_partner,
        [full] * 2 + [token],
        mixed,
        grad_tokens,
        from_partner(branches, "loop", 0),
        done,
        to_hbm=2,
    )
    g_up_first, g_down_second = call(
        total_grads(scale),
        [struct(rows * all_cols, block, wide)] * 2,
        *parts,
        place,
        done,
        to_hbm=2,
    )
    return (
        mixed,
        grad_tokens,
        g_up_first.reshape(up_first.shape),
        g_up_second.reshape(up_second.shape),
        g_down_first.reshape(down_first.shape),
        g_down_second.reshape(down_second.shape),
    )


def solution(mesh):
    in_specs = (
        P("loop", "dp"),
        P("loop", "dp"),
        P("loop", None, None),
        P("loop", None, None),
        P("loop", None, None),
        P("loop", None, None),
        P(),
        P(),
    )
    out_specs = (
        P("loop", "dp"),
        P("loop", "dp"),
        P("loop", None, None),
        P("loop", None, None),
        P("loop", None, None),
        P("loop", None, None),
    )
    return jax.shard_map(shards, mesh=mesh, in_specs=in_specs, out_specs=out_specs, check_vma=False)
```

```python
import math

import jax
import jax.numpy as jnp
from jax import lax
from jax.experimental import pallas as pl
from jax.experimental.pallas import tpu as pltpu
from jax.sharding import PartitionSpec as P


def from_partner(value, axis, apart):
    mask = 2**apart
    pairs = [(source, source ^ mask) for source in range(lax.axis_size(axis))]
    return lax.ppermute(value, axis, pairs)


def gelu_parts(pre_act):
    cumul = 0.5 * (1.0 + jax.scipy.special.erf(pre_act * (1.0 / math.sqrt(2.0))))
    slope = cumul + pre_act * jnp.exp(-0.5 * pre_act * pre_act) * (1.0 / math.sqrt(2.0 * math.pi))
    return (pre_act * cumul, slope)


def inverse_of(permute):
    return (
        jnp.zeros(permute.shape, jnp.int32)
        .at[permute]
        .set(jnp.arange(permute.shape[0], dtype=jnp.int32))
    )


def pair_total(contrib, half_width, parity):
    pair_blocks = contrib.shape[0]
    tok_count = contrib.shape[2]
    leaving = lax.dynamic_slice_in_dim(contrib, (1 - parity) * half_width, half_width, 1)
    other = from_partner(leaving.astype(jnp.bfloat16), "loop", 0).astype(leaving.dtype)
    mine = lax.dynamic_slice_in_dim(contrib, parity * half_width, half_width, 1) + other
    return mine.reshape(pair_blocks * half_width, tok_count)


def plain_shards(tokens, cotangent, up_first, up_second, down_first, down_second, perm_up, perm_down):
    wide = jnp.float32
    narrow = jnp.bfloat16
    feature_rows = tokens.shape[0]
    tok_count = tokens.shape[1]
    local_rows = up_first.shape[0]
    block = up_first.shape[2]
    half_width = block // 2
    pair_blocks = 2 * feature_rows // block
    group = 2 * local_rows // pair_blocks
    parity = lax.axis_index("loop") % 2
    other_x, other_d = from_partner((tokens, cotangent), "loop", 0)
    low_x = jnp.where(parity == 0, tokens, other_x)
    high_x = jnp.where(parity == 0, other_x, tokens)
    low_d = jnp.where(parity == 0, cotangent, other_d)
    high_d = jnp.where(parity == 0, other_d, cotangent)
    x_blocks = jnp.concatenate(
        [
            low_x.reshape(pair_blocks, half_width, tok_count),
            high_x.reshape(pair_blocks, half_width, tok_count),
        ],
        1,
    )
    d_blocks = jnp.concatenate(
        [
            low_d.reshape(pair_blocks, half_width, tok_count),
            high_d.reshape(pair_blocks, half_width, tok_count),
        ],
        1,
    )
    row_block = (parity * local_rows + jnp.arange(local_rows, dtype=jnp.int32)) // group
    picker = row_block[:, None] == jnp.arange(pair_blocks, dtype=jnp.int32)[None, :]
    picker_narrow = picker.astype(narrow)
    picker_wide = picker.astype(wide)
    x_rows = jnp.einsum("am,mit->ait", picker_narrow, x_blocks, preferred_element_type=wide).astype(
        narrow
    )
    d_rows = jnp.einsum("am,mit->ait", picker_narrow, d_blocks, preferred_element_type=wide).astype(
        narrow
    )
    inverse_up = inverse_of(perm_up)
    inverse_down = inverse_of(perm_down)
    hidden_one = jnp.einsum("abi,ait->abt", up_first, x_rows, preferred_element_type=wide).astype(
        narrow
    )
    permuted = jnp.take(
        lax.all_to_all(hidden_one, "loop", split_axis=1, concat_axis=0, tiled=True), perm_up, axis=0
    )
    pre_act = jnp.einsum("boa,abt->bot", up_second, permuted, preferred_element_type=wide)
    gelu_val, slope = gelu_parts(pre_act)
    activated = gelu_val.astype(narrow)
    mixed_cols = jnp.einsum(
        "bpo,bot->pbt", down_first, activated, preferred_element_type=wide
    ).astype(narrow)
    leaving = jnp.take(mixed_cols, perm_down, axis=0)
    back_rows = lax.all_to_all(leaving, "loop", split_axis=0, concat_axis=1, tiled=True)
    back_rows, permuted, activated, slope = (back_rows, permuted, activated, slope)
    out_rows = jnp.einsum("abo,abt->aot", down_second, back_rows, preferred_element_type=wide)
    out_contrib = jnp.einsum("am,aot->mot", picker_wide, out_rows, precision=lax.Precision.HIGHEST)
    branch_out = pair_total(out_contrib, half_width, parity)
    mixed = (tokens.astype(wide) + branch_out).astype(narrow)
    scale = 1.0 / math.sqrt(lax.axis_size("dp") * tok_count)
    grad_rows = jnp.einsum("abo,aot->abt", down_second, d_rows, preferred_element_type=wide).astype(
        narrow
    )
    g_down_second = jnp.einsum("abt,aot->abo", back_rows, d_rows, preferred_element_type=wide)
    grad_cols = lax.all_to_all(grad_rows, "loop", split_axis=1, concat_axis=0, tiled=True)
    grad_mixed = jnp.take(grad_cols, inverse_down, axis=0)
    grad_act = jnp.einsum("bpo,pbt->bot", down_first, grad_mixed, preferred_element_type=wide)
    g_down_first = jnp.einsum("pbt,bot->bpo", grad_mixed, activated, preferred_element_type=wide)
    grad_pre = (grad_act * slope).astype(narrow)
    g_up_second = jnp.einsum("bot,abt->boa", grad_pre, permuted, preferred_element_type=wide)
    grad_perm = jnp.einsum("boa,bot->abt", up_second, grad_pre, preferred_element_type=wide).astype(
        narrow
    )
    grad_recv = jnp.take(grad_perm, inverse_up, axis=0)
    grad_hidden = lax.all_to_all(grad_recv, "loop", split_axis=0, concat_axis=1, tiled=True)
    g_up_first = jnp.einsum("abt,ait->abi", grad_hidden, x_rows, preferred_element_type=wide)
    g_up_first, g_up_second, g_down_first, g_down_second = (
        lax.psum(g_up_first.astype(jnp.bfloat16), "dp").astype(jnp.float32),
        lax.psum(g_up_second.astype(jnp.bfloat16), "dp").astype(jnp.float32),
        lax.psum(g_down_first.astype(jnp.bfloat16), "dp").astype(jnp.float32),
        lax.psum(g_down_second.astype(jnp.bfloat16), "dp").astype(jnp.float32),
    )
    grad_rows_in = jnp.einsum("abi,abt->ait", up_first, grad_hidden, preferred_element_type=wide)
    grad_contrib = jnp.einsum(
        "am,ait->mit", picker_wide, grad_rows_in, precision=lax.Precision.HIGHEST
    )
    grad_branch = pair_total(grad_contrib, half_width, parity)
    grad_tokens = (cotangent.astype(wide) + grad_branch).astype(narrow)
    return (
        mixed,
        grad_tokens,
        g_up_first * scale,
        g_up_second * scale,
        g_down_first * scale,
        g_down_second * scale,
    )


VMEM_LIMIT = 16 * 2**20
COL_MICROS = 28
FIRST_ORDER = (1, 2, 3)
BACK_ORDER = (1, 2, 3)
COL_APART = (2, 1)
ROW_APART = (2, 1)


def dot(left, right, left_dim=1, right_dim=0):
    return lax.dot_general(
        left, right, (((left_dim,), (right_dim,)), ((), ())), preferred_element_type=jnp.float32
    )


def call(body, outs, *args, scratch=(), micros=0.01, to_hbm=0, aliases=()):
    whole = pl.BlockSpec(memory_space=pltpu.VMEM)
    return pl.pallas_call(
        body,
        out_shape=outs,
        in_specs=[whole] * len(args),
        out_specs=[pl.BlockSpec()] * to_hbm + [whole] * (len(outs) - to_hbm),
        scratch_shapes=list(scratch),
        input_output_aliases=dict(aliases),
        compiler_params=pltpu.CompilerParams(vmem_limit_bytes=VMEM_LIMIT),
        cost_estimate=pl.CostEstimate(
            flops=int(micros * 1e9), bytes_accessed=int(micros * 3e6), transcendentals=0
        ),
    )(*args)


def own_first(weights, parity):
    half = weights.shape[1] // 2
    return jnp.where(parity == 0, weights, pltpu.roll(weights, half, 1))


def one_hot(rows, cols, at):
    lead = lax.broadcasted_iota(jnp.int32, (rows, cols), 0)
    lane = lax.broadcasted_iota(jnp.int32, (rows, cols), 1)
    return at(lead, lane).astype(jnp.bfloat16)


def pair_cols(me, chips, rows, cols, turn):
    mine = chips * cols
    every = 2 * mine

    def at(lead, lane):
        chip = (me // 2) ^ ((lane // cols) % chips)
        col = (2 * chip + ((me % 2) ^ turn)) * cols + lane % cols
        return lead == (lane // mine) * every + col

    return one_hot(rows * every, rows * mine, at)


def sent_order(chips, rows, cols, sent_dim):
    def at(lead, lane):
        sent, kept = (lead, lane) if sent_dim == 0 else (lane, lead)
        q, rest = sent // (cols * 2 * rows), sent % (cols * 2 * rows)
        b, row = rest // (2 * rows), rest % (2 * rows)
        return kept == row * (chips * cols) + q * cols + b

    size = 2 * rows * chips * cols
    return one_hot(size, size, at)


def block_rows(own_ref, other_ref, start, half):
    span = pl.ds(pl.multiple_of(start, half), half)
    return jnp.concatenate([own_ref[span, :], other_ref[span, :]], 0)


def pair_blocks_of(parity, pair_blocks):
    local = pair_blocks // 2
    return [(parity if at < local else 1 - parity) * local + at % local for at in range(pair_blocks)]


def tables(chips, rows, cols):
    def body(take_ref, order_ref, back_ref, place_ref):
        me = lax.axis_index("loop")
        places = [pair_cols(me, chips, rows, cols, turn) for turn in (0, 1)]
        take_ref[...] = places[0]
        order_ref[...] = sent_order(chips, rows, cols, 0)
        back_ref[...] = sent_order(chips, rows, cols, 1)
        place_ref[...] = jnp.concatenate(places, 1)

    return body


def take_weights(take_ref, weight_refs, parity, out_ref):
    taken = [own_first(dot(take_ref[...], ref[...], 0, 0), parity) for ref in weight_refs]
    out_ref[...] = jnp.concatenate(taken, 0).astype(out_ref.dtype)


def send_rows(own_ref, other_ref, taken_ref, order_ref, grid_ref, outs, at, half, parity):
    pair_blocks = own_ref.shape[0] // half
    high = taken_ref.shape[0] // pair_blocks
    for place, block in enumerate(pair_blocks_of(parity, pair_blocks)):
        part = slice(place * high, (place + 1) * high)
        features = block_rows(own_ref, other_ref, block * half, half)
        grid_ref[part, :] = dot(taken_ref[part, :], features).astype(grid_ref.dtype)
    sent = dot(order_ref[...], grid_ref[...]).astype(grid_ref.dtype)
    unit = sent.shape[0] // len(outs)
    for q, out in enumerate(outs):
        out[at * unit : (at + 1) * unit, :] = sent[q * unit : (q + 1) * unit]


def token_rows(chips, half):
    def body(*refs):
        own_ref, other_ref, *weights, take_ref, order_ref = refs[:8]
        outs, (up_ref, down_ref, grid_ref) = refs[8 : 8 + chips], refs[8 + chips :]
        parity = lax.axis_index("loop") % 2
        take_weights(take_ref, weights[:2], parity, up_ref)
        send_rows(own_ref, other_ref, up_ref, order_ref, grid_ref, outs, 0, half, parity)
        take_weights(take_ref, weights[2:], parity, down_ref)

    return body


def cotangent_rows(chips, half):
    def body(*refs):
        own_ref, other_ref, down_ref, order_ref = refs[:4]
        earlier, outs, grid_ref = refs[4 : 4 + chips], refs[4 + chips : -1], refs[-1]
        for out, ref in zip(outs, earlier, strict=True):
            out[: ref.shape[0], :] = ref[...]
        parity = lax.axis_index("loop") % 2
        send_rows(own_ref, other_ref, down_ref, order_ref, grid_ref, outs, 1, half, parity)

    return body


def turn_blocks(half):
    def body(own_ref, other_ref, _, out_ref):
        parity = lax.axis_index("loop") % 2
        pair_blocks = own_ref.shape[0] // half
        for at, block in enumerate(pair_blocks_of(parity, pair_blocks)):
            features = block_rows(own_ref, other_ref, block * half, half)
            out_ref[:, at * 2 * half : (at + 1) * 2 * half] = features.T

    return body


def by_distance(bufs, order):
    return [bufs[0], *(bufs[1 + order.index(q)] for q in range(1, len(bufs)))]


def one_col(bufs, at, deep):
    return jnp.concatenate([r[at * deep : (at + 1) * deep, :] for r in bufs], 0)


def spread(outs, at, deep, value):
    for q, out in enumerate(outs):
        out[at * deep : (at + 1) * deep, :] = value[q * deep : (q + 1) * deep]


def column_weights(rows, cols):
    narrow = jnp.bfloat16

    def body(up_ref, down_ref, perm_up_ref, perm_down_ref, _, *outs):
        up_out, up_turned, down_out, down_turned, take_up_ref, take_down_ref = outs
        me = lax.axis_index("loop")
        size = take_up_ref.shape[0]
        lead = lax.broadcasted_iota(jnp.int32, (size, size), 0)
        lane = lax.broadcasted_iota(jnp.int32, (size, size), 1)
        row = ((lead // rows) ^ me) * rows + lead % rows
        take_up_ref[...] = (perm_up_ref[...] == row).astype(narrow)
        take_down_ref[...] = dot(
            (lane == row).astype(narrow), (perm_down_ref[...] == lead).astype(narrow), 1, 1
        ).astype(narrow)
        for b in range(cols):
            span = slice(b * size, (b + 1) * size)
            up = dot(up_ref[span, :], take_up_ref[...], 1, 1)
            down = dot(take_down_ref[...], down_ref[span, :])
            up_out[span, :] = up.astype(narrow)
            up_turned[span, :] = up.T.astype(narrow)
            down_out[span, :] = down.astype(narrow)
            down_turned[span, :] = down.T.astype(narrow)

    return body


def columns(chips, rows, cols):
    narrow = jnp.bfloat16
    deep = 2 * rows

    def body(*refs):
        bufs, weights = by_distance(refs[:chips], FIRST_ORDER), refs[chips : chips + 4]
        outs, (activated_ref, grad_pre_ref) = refs[-chips - 2 : -2], refs[-2:]
        size = chips * deep
        for b in range(cols):
            span = slice(b * size, (b + 1) * size)
            up, up_turned, down, down_turned = (ref[span, :] for ref in weights)
            gelu_val, slope = gelu_parts(dot(up, one_col(bufs, b, deep)))
            activated = gelu_val.astype(narrow)
            activated_ref[span, :] = activated
            spread(outs, b, deep, dot(down, activated).astype(narrow))
            grad_act = dot(down_turned, one_col(bufs, cols + b, deep))
            grad_pre = (grad_act * slope).astype(narrow)
            grad_pre_ref[span, :] = grad_pre
            spread(outs, cols + b, deep, dot(up_turned, grad_pre).astype(narrow))

    return body


def column_grads(chips, rows, cols):
    narrow = jnp.bfloat16
    deep = 2 * rows

    def body(*refs):
        bufs = by_distance(refs[:chips], FIRST_ORDER)
        activated_ref, grad_pre_ref, out_ref = refs[chips:]
        size = chips * deep
        for b in range(cols):
            span = slice(b * size, (b + 1) * size)
            hid = one_col(bufs, b, deep)
            grad = one_col(bufs, cols + b, deep)
            g_up = dot(grad_pre_ref[span, :], hid, 1, 1).astype(narrow)
            g_down = dot(grad, activated_ref[span, :], 1, 1).astype(narrow)
            out_ref[span, :] = g_up
            out_ref[cols * size + b * size : cols * size + (b + 1) * size, :] = g_down

    return body


def row_grads(chips, rows, cols, half):
    narrow = jnp.bfloat16

    def body(*refs):
        bufs = by_distance(refs[:chips], BACK_ORDER)
        x_ref, d_ref, order_ref = refs[chips : chips + 3]
        grads_ref, back_ref, grad_ref = refs[-3:]
        parity = lax.axis_index("loop") % 2
        block = 2 * half
        unit = 2 * rows * cols
        pair_blocks = x_ref.shape[1] // block
        jobs = ((1, grad_ref, x_ref), (0, back_ref, d_ref))
        for at, (job, grid_ref, turned_ref) in enumerate(jobs):
            grid_ref[...] = dot(order_ref[...], one_col(bufs, job, unit)).astype(narrow)
            high = grid_ref.shape[0] // pair_blocks
            grads = []
            for place in range(0, pair_blocks, 2):
                both = dot(
                    grid_ref[place * high : (place + 2) * high, :],
                    turned_ref[:, place * block : (place + 2) * block],
                )
                grads += [both[:high, :block], both[high:, block:]]
            both = own_first(jnp.concatenate(grads, 0), parity).astype(narrow)
            size = both.shape[0] // 2
            for turn in range(2):
                start = (2 * turn + at) * size
                grads_ref[start : start + size, :] = both[turn * size : (turn + 1) * size]

    return body


def row_outputs(half):
    def body(*refs):
        jobs, col_refs, (*kept_refs, sent_ref, sum_ref) = (refs[:3], refs[3:6]), refs[6:8], refs[8:]
        add(*col_refs, sum_ref)
        parity = lax.axis_index("loop") % 2
        for at, (grid_ref, own_ref, weights_ref) in enumerate(jobs):
            kept_ref, features = kept_refs[at], own_ref.shape[0]
            pair_blocks = own_ref.shape[0] // half
            high = weights_ref.shape[0] // pair_blocks
            for place, block in enumerate(pair_blocks_of(parity, pair_blocks)):
                part = slice(place * high, (place + 1) * high)
                span = pl.ds(pl.multiple_of(block * half, half), half)
                branch = dot(weights_ref[part, :], grid_ref[part, :], 0, 0)
                kept_ref[span, :] = own_ref[span, :].astype(jnp.float32) + branch[:half]
                span = pl.ds(pl.multiple_of(at * features + block * half, half), half)
                sent_ref[span, :] = branch[half:].astype(jnp.bfloat16)

    return body


def add_partner(mixed_ref, grad_ref, got_ref, _, mixed_out, grad_out, done_ref):
    size = mixed_ref.shape[0]
    for at, (kept, out) in enumerate(((mixed_ref, mixed_out), (grad_ref, grad_out))):
        got = got_ref[at * size : (at + 1) * size, :].astype(jnp.float32)
        out[...] = (kept[...] + got).astype(out.dtype)
    done_ref[...] = jnp.zeros_like(done_ref)


def add(left_ref, right_ref, out_ref):
    total = left_ref[...].astype(jnp.float32) + right_ref[...].astype(jnp.float32)
    out_ref[...] = total.astype(out_ref.dtype)


def add_halves(left_ref, right_ref, kept_ref, *leave_refs):
    size = kept_ref.shape[0]
    for at, outs in enumerate(((kept_ref, leave_refs[0]), leave_refs[1:])):
        span = slice(at * size, (at + 1) * size)
        total = left_ref[span, :].astype(jnp.float32) + right_ref[span, :].astype(jnp.float32)
        for out in outs:
            out[...] = total.astype(out.dtype)


def total_grads(scale):
    def body(*refs):
        parts, place_ref, outs = [refs[at] for at in (0, 2, 1, 3)], refs[4], refs[-2:]
        size = parts[0].shape[0] // 2
        near, far = place_ref[:, :size], place_ref[:, size:]
        place = jnp.concatenate([near, near, far, far], 1)
        for at, out in enumerate(outs):
            span = slice(at * size, (at + 1) * size)
            out[...] = dot(place, jnp.concatenate([r[span, :] for r in parts], 0)) * scale

    return body


def total_col_grads(scale):
    def body(sum_ref, got_ref, take_up_ref, take_down_ref, up_ref, down_ref, done_ref):
        done_ref[...] = jnp.zeros_like(done_ref)
        size = take_up_ref.shape[0]
        count = up_ref.shape[0]
        for start in range(0, count, size):
            near = slice(start, start + size)
            far = slice(count + start, count + start + size)
            up = [dot(ref[near, :], take_up_ref[...]) for ref in (sum_ref, got_ref)]
            down = [dot(take_down_ref[...], ref[far, :], 0, 0) for ref in (sum_ref, got_ref)]
            up_ref[near, :] = (up[0] + up[1]) * scale
            down_ref[near, :] = (down[0] + down[1]) * scale

    return body


def exchange(bufs, axis, order):
    pairs = {q: [(s, s ^ (2 * q)) for s in range(2 * len(bufs))] for q in order}
    return [bufs[0]] + [lax.ppermute(bufs[q], axis, pairs[q]) for q in order]


def shards(tokens, cotangent, up_first, up_second, down_first, down_second, perm_up, perm_down):
    narrow = jnp.bfloat16
    wide = jnp.float32
    loops, dps = lax.axis_size("loop"), lax.axis_size("dp")
    feature_rows, toks = tokens.shape
    rows, all_cols, block = up_first.shape
    cols, size = up_second.shape[:2]
    half = block // 2
    pair_blocks = feature_rows // half
    if loops != 8 or dps != 4 or rows % 16 or pair_blocks % 2 or 2 * rows * cols * loops // 2 % (16 * pair_blocks):
        return plain_shards(
            tokens, cotangent, up_first, up_second, down_first, down_second, perm_up, perm_down
        )
    chips = loops // 2

    def struct(lead, width, dtype=narrow):
        return jax.ShapeDtypeStruct((lead, width), dtype)

    up_rows = up_first.reshape(rows * all_cols, block)
    down_rows = down_second.reshape(rows * all_cols, block)
    grid_rows = 2 * rows * chips * cols
    half_buf = struct(2 * rows * cols, toks)
    buf = struct(4 * rows * cols, toks)
    grid = struct(grid_rows, toks)
    half_grid = struct(grid_rows // 2, toks)
    taken = struct(grid_rows, block)
    full = struct(feature_rows, toks)
    take, order, order_back, place = call(
        tables(chips, rows, cols),
        [struct(rows * all_cols, rows * chips * cols)] + [struct(grid_rows, grid_rows)] * 3,
        micros=4,
    )
    other_x = from_partner(tokens, "loop", 0)
    other_up = from_partner(up_rows, "loop", 0)
    other_down = from_partner(down_rows, "loop", 0)
    leaving, other_up, other_down = lax.optimization_barrier((cotangent, other_up, other_down))
    other_d = from_partner(leaving, "loop", 0)

    *sent, up_taken, down_taken = call(
        token_rows(chips, half),
        [half_buf] * chips + [taken] * 2,
        tokens,
        other_x,
        up_rows,
        other_up,
        down_rows,
        other_down,
        take,
        order,
        scratch=[pltpu.VMEM(grid.shape, narrow)],
    )
    sent = call(
        cotangent_rows(chips, half),
        [buf] * chips,
        cotangent,
        other_d,
        down_taken,
        order,
        *sent,
        scratch=[pltpu.VMEM(grid.shape, narrow)],
    )
    cells = exchange(sent, "loop", FIRST_ORDER)
    square = struct(cols * size, size)
    *col_weights, take_up, take_down = call(
        column_weights(rows, cols),
        [square] * 4 + [struct(size, size)] * 2,
        up_second.reshape(square.shape),
        down_first.reshape(square.shape),
        perm_up.reshape(1, size),
        perm_down.reshape(1, size),
        sent[0],
        micros=2,
    )
    turned = struct(toks, 2 * feature_rows)
    (x_turned,) = call(turn_blocks(half), [turned], tokens, other_x, sent[0], micros=1)
    (d_turned,) = call(turn_blocks(half), [turned], cotangent, other_d, sent[0], micros=1)
    *sent, activated, grad_pre = call(
        columns(chips, rows, cols),
        [buf] * chips + [grid] * 2,
        *cells,
        *col_weights,
        x_turned,
        d_turned,
    )
    back = exchange(sent, "loop", BACK_ORDER)
    (col_grads,) = call(
        column_grads(chips, rows, cols),
        [struct(2 * cols * size, size)],
        *cells,
        activated,
        grad_pre,
    )

    def over_dp(value, apart):
        return lax.ppermute(value, "dp", [(s, s ^ apart) for s in range(dps)])

    sums, back_rows, grad_rows = call(
        row_grads(chips, rows, cols, half),
        [struct(2 * grid_rows, block), grid, grid],
        *back,
        x_turned,
        d_turned,
        order_back,
        col_grads,
    )
    sums_got = over_dp(sums, ROW_APART[0])
    partial = struct(feature_rows, toks, wide)
    both = struct(2 * feature_rows, toks)
    mixed, grad_tokens, branches, col_sum = call(
        row_outputs(half),
        [partial, partial, both, struct(*col_grads.shape)],
        back_rows,
        tokens,
        down_taken,
        grad_rows,
        cotangent,
        up_taken,
        col_grads,
        over_dp(col_grads, COL_APART[0]),
    )
    kept, to_next, to_other, to_core = call(add_halves, [taken] * 4, sums, sums_got)

    def to_partner(value, apart):
        pairs = [(s, s ^ (apart * loops + 1)) for s in range(dps * loops)]
        return lax.ppermute(value, ("dp", "loop"), pairs)

    got = {}
    got['c'] = to_partner(to_other, ROW_APART[1])
    got['z'] = over_dp(to_next, ROW_APART[1])
    got['p'] = from_partner(to_core, "loop", 0)
    parts = (kept, got['c'], got['z'], got['p'])
    scale = 1.0 / math.sqrt(dps * toks)
    token = struct(8, 128, wide)
    g_up_second, g_down_first, done = call(
        total_col_grads(scale),
        [struct(*square.shape, wide)] * 2 + [token],
        col_sum,
        over_dp(col_sum, COL_APART[1]),
        take_up,
        take_down,
        to_hbm=2,
        micros=COL_MICROS,
    )
    mixed, grad_tokens, done = call(
        add_partner,
        [full] * 2 + [token],
        mixed,
        grad_tokens,
        from_partner(branches, "loop", 0),
        done,
        to_hbm=2,
    )
    g_up_first, g_down_second = call(
        total_grads(scale),
        [struct(rows * all_cols, block, wide)] * 2,
        *parts,
        place,
        done,
        to_hbm=2,
    )
    return (
        mixed,
        grad_tokens,
        g_up_first.reshape(up_first.shape),
        g_up_second.reshape(up_second.shape),
        g_down_first.reshape(down_first.shape),
        g_down_second.reshape(down_second.shape),
    )


def solution(mesh):
    in_specs = (
        P("loop", "dp"),
        P("loop", "dp"),
        P("loop", None, None),
        P("loop", None, None),
        P("loop", None, None),
        P("loop", None, None),
        P(),
        P(),
    )
    out_specs = (
        P("loop", "dp"),
        P("loop", "dp"),
        P("loop", None, None),
        P("loop", None, None),
        P("loop", None, None),
        P("loop", None, None),
    )
    return jax.shard_map(shards, mesh=mesh, in_specs=in_specs, out_specs=out_specs, check_vma=False)
```

```python
import math

import jax
import jax.numpy as jnp
from jax import lax
from jax.experimental import pallas as pl
from jax.experimental.pallas import tpu as pltpu
from jax.sharding import PartitionSpec as P


def from_partner(value, axis, apart):
    mask = 2**apart
    pairs = [(source, source ^ mask) for source in range(lax.axis_size(axis))]
    return lax.ppermute(value, axis, pairs)


def gelu_parts(pre_act):
    cumul = 0.5 * (1.0 + jax.scipy.special.erf(pre_act * (1.0 / math.sqrt(2.0))))
    slope = cumul + pre_act * jnp.exp(-0.5 * pre_act * pre_act) * (1.0 / math.sqrt(2.0 * math.pi))
    return (pre_act * cumul, slope)


def inverse_of(permute):
    return (
        jnp.zeros(permute.shape, jnp.int32)
        .at[permute]
        .set(jnp.arange(permute.shape[0], dtype=jnp.int32))
    )


def pair_total(contrib, half_width, parity):
    pair_blocks = contrib.shape[0]
    tok_count = contrib.shape[2]
    leaving = lax.dynamic_slice_in_dim(contrib, (1 - parity) * half_width, half_width, 1)
    other = from_partner(leaving.astype(jnp.bfloat16), "loop", 0).astype(leaving.dtype)
    mine = lax.dynamic_slice_in_dim(contrib, parity * half_width, half_width, 1) + other
    return mine.reshape(pair_blocks * half_width, tok_count)


def plain_shards(tokens, cotangent, up_first, up_second, down_first, down_second, perm_up, perm_down):
    wide = jnp.float32
    narrow = jnp.bfloat16
    feature_rows = tokens.shape[0]
    tok_count = tokens.shape[1]
    local_rows = up_first.shape[0]
    block = up_first.shape[2]
    half_width = block // 2
    pair_blocks = 2 * feature_rows // block
    group = 2 * local_rows // pair_blocks
    parity = lax.axis_index("loop") % 2
    other_x, other_d = from_partner((tokens, cotangent), "loop", 0)
    low_x = jnp.where(parity == 0, tokens, other_x)
    high_x = jnp.where(parity == 0, other_x, tokens)
    low_d = jnp.where(parity == 0, cotangent, other_d)
    high_d = jnp.where(parity == 0, other_d, cotangent)
    x_blocks = jnp.concatenate(
        [
            low_x.reshape(pair_blocks, half_width, tok_count),
            high_x.reshape(pair_blocks, half_width, tok_count),
        ],
        1,
    )
    d_blocks = jnp.concatenate(
        [
            low_d.reshape(pair_blocks, half_width, tok_count),
            high_d.reshape(pair_blocks, half_width, tok_count),
        ],
        1,
    )
    row_block = (parity * local_rows + jnp.arange(local_rows, dtype=jnp.int32)) // group
    picker = row_block[:, None] == jnp.arange(pair_blocks, dtype=jnp.int32)[None, :]
    picker_narrow = picker.astype(narrow)
    picker_wide = picker.astype(wide)
    x_rows = jnp.einsum("am,mit->ait", picker_narrow, x_blocks, preferred_element_type=wide).astype(
        narrow
    )
    d_rows = jnp.einsum("am,mit->ait", picker_narrow, d_blocks, preferred_element_type=wide).astype(
        narrow
    )
    inverse_up = inverse_of(perm_up)
    inverse_down = inverse_of(perm_down)
    hidden_one = jnp.einsum("abi,ait->abt", up_first, x_rows, preferred_element_type=wide).astype(
        narrow
    )
    permuted = jnp.take(
        lax.all_to_all(hidden_one, "loop", split_axis=1, concat_axis=0, tiled=True), perm_up, axis=0
    )
    pre_act = jnp.einsum("boa,abt->bot", up_second, permuted, preferred_element_type=wide)
    gelu_val, slope = gelu_parts(pre_act)
    activated = gelu_val.astype(narrow)
    mixed_cols = jnp.einsum(
        "bpo,bot->pbt", down_first, activated, preferred_element_type=wide
    ).astype(narrow)
    leaving = jnp.take(mixed_cols, perm_down, axis=0)
    back_rows = lax.all_to_all(leaving, "loop", split_axis=0, concat_axis=1, tiled=True)
    back_rows, permuted, activated, slope = (back_rows, permuted, activated, slope)
    out_rows = jnp.einsum("abo,abt->aot", down_second, back_rows, preferred_element_type=wide)
    out_contrib = jnp.einsum("am,aot->mot", picker_wide, out_rows, precision=lax.Precision.HIGHEST)
    branch_out = pair_total(out_contrib, half_width, parity)
    mixed = (tokens.astype(wide) + branch_out).astype(narrow)
    scale = 1.0 / math.sqrt(lax.axis_size("dp") * tok_count)
    grad_rows = jnp.einsum("abo,aot->abt", down_second, d_rows, preferred_element_type=wide).astype(
        narrow
    )
    g_down_second = jnp.einsum("abt,aot->abo", back_rows, d_rows, preferred_element_type=wide)
    grad_cols = lax.all_to_all(grad_rows, "loop", split_axis=1, concat_axis=0, tiled=True)
    grad_mixed = jnp.take(grad_cols, inverse_down, axis=0)
    grad_act = jnp.einsum("bpo,pbt->bot", down_first, grad_mixed, preferred_element_type=wide)
    g_down_first = jnp.einsum("pbt,bot->bpo", grad_mixed, activated, preferred_element_type=wide)
    grad_pre = (grad_act * slope).astype(narrow)
    g_up_second = jnp.einsum("bot,abt->boa", grad_pre, permuted, preferred_element_type=wide)
    grad_perm = jnp.einsum("boa,bot->abt", up_second, grad_pre, preferred_element_type=wide).astype(
        narrow
    )
    grad_recv = jnp.take(grad_perm, inverse_up, axis=0)
    grad_hidden = lax.all_to_all(grad_recv, "loop", split_axis=0, concat_axis=1, tiled=True)
    g_up_first = jnp.einsum("abt,ait->abi", grad_hidden, x_rows, preferred_element_type=wide)
    g_up_first, g_up_second, g_down_first, g_down_second = (
        lax.psum(g_up_first.astype(jnp.bfloat16), "dp").astype(jnp.float32),
        lax.psum(g_up_second.astype(jnp.bfloat16), "dp").astype(jnp.float32),
        lax.psum(g_down_first.astype(jnp.bfloat16), "dp").astype(jnp.float32),
        lax.psum(g_down_second.astype(jnp.bfloat16), "dp").astype(jnp.float32),
    )
    grad_rows_in = jnp.einsum("abi,abt->ait", up_first, grad_hidden, preferred_element_type=wide)
    grad_contrib = jnp.einsum(
        "am,ait->mit", picker_wide, grad_rows_in, precision=lax.Precision.HIGHEST
    )
    grad_branch = pair_total(grad_contrib, half_width, parity)
    grad_tokens = (cotangent.astype(wide) + grad_branch).astype(narrow)
    return (
        mixed,
        grad_tokens,
        g_up_first * scale,
        g_up_second * scale,
        g_down_first * scale,
        g_down_second * scale,
    )


VMEM_LIMIT = 16 * 2**20
COL_MICROS = 28
FIRST_ORDER = (1, 2, 3)
BACK_ORDER = (1, 2, 3)
COL_APART = (2, 1)
ROW_APART = (2, 1)


def dot(left, right, left_dim=1, right_dim=0):
    return lax.dot_general(
        left, right, (((left_dim,), (right_dim,)), ((), ())), preferred_element_type=jnp.float32
    )


def call(body, outs, *args, scratch=(), micros=0.01, to_hbm=0, aliases=()):
    whole = pl.BlockSpec(memory_space=pltpu.VMEM)
    return pl.pallas_call(
        body,
        out_shape=outs,
        in_specs=[whole] * len(args),
        out_specs=[pl.BlockSpec()] * to_hbm + [whole] * (len(outs) - to_hbm),
        scratch_shapes=list(scratch),
        input_output_aliases=dict(aliases),
        compiler_params=pltpu.CompilerParams(vmem_limit_bytes=VMEM_LIMIT),
        cost_estimate=pl.CostEstimate(
            flops=int(micros * 1e9), bytes_accessed=int(micros * 3e6), transcendentals=0
        ),
    )(*args)


def own_first(weights, parity):
    half = weights.shape[1] // 2
    return jnp.where(parity == 0, weights, pltpu.roll(weights, half, 1))


def one_hot(rows, cols, at):
    lead = lax.broadcasted_iota(jnp.int32, (rows, cols), 0)
    lane = lax.broadcasted_iota(jnp.int32, (rows, cols), 1)
    return at(lead, lane).astype(jnp.bfloat16)


def pair_cols(me, chips, rows, cols, turn):
    mine = chips * cols
    every = 2 * mine

    def at(lead, lane):
        chip = (me // 2) ^ ((lane // cols) % chips)
        col = (2 * chip + ((me % 2) ^ turn)) * cols + lane % cols
        return lead == (lane // mine) * every + col

    return one_hot(rows * every, rows * mine, at)


def sent_order(chips, rows, cols, sent_dim):
    def at(lead, lane):
        sent, kept = (lead, lane) if sent_dim == 0 else (lane, lead)
        q, rest = sent // (cols * 2 * rows), sent % (cols * 2 * rows)
        b, row = rest // (2 * rows), rest % (2 * rows)
        return kept == row * (chips * cols) + q * cols + b

    size = 2 * rows * chips * cols
    return one_hot(size, size, at)


def block_rows(own_ref, other_ref, start, half):
    span = pl.ds(pl.multiple_of(start, half), half)
    return jnp.concatenate([own_ref[span, :], other_ref[span, :]], 0)


def pair_blocks_of(parity, pair_blocks):
    local = pair_blocks // 2
    return [(parity if at < local else 1 - parity) * local + at % local for at in range(pair_blocks)]


def tables(chips, rows, cols):
    def body(take_ref, order_ref, back_ref, place_ref):
        me = lax.axis_index("loop")
        places = [pair_cols(me, chips, rows, cols, turn) for turn in (0, 1)]
        take_ref[...] = places[0]
        order_ref[...] = sent_order(chips, rows, cols, 0)
        back_ref[...] = sent_order(chips, rows, cols, 1)
        place_ref[...] = jnp.concatenate(places, 1)

    return body


def take_weights(take_ref, weight_refs, parity, out_ref):
    taken = [own_first(dot(take_ref[...], ref[...], 0, 0), parity) for ref in weight_refs]
    out_ref[...] = jnp.concatenate(taken, 0).astype(out_ref.dtype)


def send_rows(own_ref, other_ref, taken_ref, order_ref, grid_ref, outs, at, half, parity):
    pair_blocks = own_ref.shape[0] // half
    high = taken_ref.shape[0] // pair_blocks
    for place, block in enumerate(pair_blocks_of(parity, pair_blocks)):
        part = slice(place * high, (place + 1) * high)
        features = block_rows(own_ref, other_ref, block * half, half)
        grid_ref[part, :] = dot(taken_ref[part, :], features).astype(grid_ref.dtype)
    sent = dot(order_ref[...], grid_ref[...]).astype(grid_ref.dtype)
    unit = sent.shape[0] // len(outs)
    for q, out in enumerate(outs):
        out[at * unit : (at + 1) * unit, :] = sent[q * unit : (q + 1) * unit]


def token_rows(chips, half):
    def body(*refs):
        own_ref, other_ref, *weights, take_ref, order_ref = refs[:8]
        outs, (up_ref, down_ref, grid_ref) = refs[8 : 8 + chips], refs[8 + chips :]
        parity = lax.axis_index("loop") % 2
        take_weights(take_ref, weights[:2], parity, up_ref)
        send_rows(own_ref, other_ref, up_ref, order_ref, grid_ref, outs, 0, half, parity)
        take_weights(take_ref, weights[2:], parity, down_ref)

    return body


def cotangent_rows(chips, half):
    def body(*refs):
        own_ref, other_ref, down_ref, order_ref = refs[:4]
        earlier, outs, grid_ref = refs[4 : 4 + chips], refs[4 + chips : -1], refs[-1]
        for out, ref in zip(outs, earlier, strict=True):
            out[: ref.shape[0], :] = ref[...]
        parity = lax.axis_index("loop") % 2
        send_rows(own_ref, other_ref, down_ref, order_ref, grid_ref, outs, 1, half, parity)

    return body


def turn_blocks(half):
    def body(own_ref, other_ref, _, out_ref):
        parity = lax.axis_index("loop") % 2
        pair_blocks = own_ref.shape[0] // half
        for at, block in enumerate(pair_blocks_of(parity, pair_blocks)):
            features = block_rows(own_ref, other_ref, block * half, half)
            out_ref[:, at * 2 * half : (at + 1) * 2 * half] = features.T

    return body


def by_distance(bufs, order):
    return [bufs[0], *(bufs[1 + order.index(q)] for q in range(1, len(bufs)))]


def one_col(bufs, at, deep):
    return jnp.concatenate([r[at * deep : (at + 1) * deep, :] for r in bufs], 0)


def spread(outs, at, deep, value):
    for q, out in enumerate(outs):
        out[at * deep : (at + 1) * deep, :] = value[q * deep : (q + 1) * deep]


def column_weights(rows, cols):
    narrow = jnp.bfloat16

    def body(up_ref, down_ref, perm_up_ref, perm_down_ref, _, *outs):
        up_out, up_turned, down_out, down_turned, take_up_ref, take_down_ref = outs
        me = lax.axis_index("loop")
        size = take_up_ref.shape[0]
        lead = lax.broadcasted_iota(jnp.int32, (size, size), 0)
        lane = lax.broadcasted_iota(jnp.int32, (size, size), 1)
        row = ((lead // rows) ^ me) * rows + lead % rows
        take_up_ref[...] = (perm_up_ref[...] == row).astype(narrow)
        take_down_ref[...] = dot(
            (lane == row).astype(narrow), (perm_down_ref[...] == lead).astype(narrow), 1, 1
        ).astype(narrow)
        for b in range(cols):
            span = slice(b * size, (b + 1) * size)
            up = dot(up_ref[span, :], take_up_ref[...], 1, 1)
            down = dot(take_down_ref[...], down_ref[span, :])
            up_out[span, :] = up.astype(narrow)
            up_turned[span, :] = up.T.astype(narrow)
            down_out[span, :] = down.astype(narrow)
            down_turned[span, :] = down.T.astype(narrow)

    return body


def columns(chips, rows, cols):
    narrow = jnp.bfloat16
    deep = 2 * rows

    def body(*refs):
        bufs, weights = by_distance(refs[:chips], FIRST_ORDER), refs[chips : chips + 4]
        outs, (activated_ref, grad_pre_ref) = refs[-chips - 2 : -2], refs[-2:]
        size = chips * deep
        for b in range(cols):
            span = slice(b * size, (b + 1) * size)
            up, up_turned, down, down_turned = (ref[span, :] for ref in weights)
            gelu_val, slope = gelu_parts(dot(up, one_col(bufs, b, deep)))
            activated = gelu_val.astype(narrow)
            activated_ref[span, :] = activated
            spread(outs, b, deep, dot(down, activated).astype(narrow))
            grad_act = dot(down_turned, one_col(bufs, cols + b, deep))
            grad_pre = (grad_act * slope).astype(narrow)
            grad_pre_ref[span, :] = grad_pre
            spread(outs, cols + b, deep, dot(up_turned, grad_pre).astype(narrow))

    return body


def column_grads(chips, rows, cols):
    narrow = jnp.bfloat16
    deep = 2 * rows

    def body(*refs):
        bufs = by_distance(refs[:chips], FIRST_ORDER)
        activated_ref, grad_pre_ref, out_ref = refs[chips:]
        size = chips * deep
        for b in range(cols):
            span = slice(b * size, (b + 1) * size)
            hid = one_col(bufs, b, deep)
            grad = one_col(bufs, cols + b, deep)
            g_up = dot(grad_pre_ref[span, :], hid, 1, 1).astype(narrow)
            g_down = dot(grad, activated_ref[span, :], 1, 1).astype(narrow)
            out_ref[span, :] = g_up
            out_ref[cols * size + b * size : cols * size + (b + 1) * size, :] = g_down

    return body


def row_grads(chips, rows, cols, half):
    narrow = jnp.bfloat16

    def body(*refs):
        bufs = by_distance(refs[:chips], BACK_ORDER)
        x_ref, d_ref, order_ref = refs[chips : chips + 3]
        grads_ref, back_ref, grad_ref = refs[-3:]
        parity = lax.axis_index("loop") % 2
        block = 2 * half
        unit = 2 * rows * cols
        pair_blocks = x_ref.shape[1] // block
        jobs = ((1, grad_ref, x_ref), (0, back_ref, d_ref))
        for at, (job, grid_ref, turned_ref) in enumerate(jobs):
            grid_ref[...] = dot(order_ref[...], one_col(bufs, job, unit)).astype(narrow)
            high = grid_ref.shape[0] // pair_blocks
            grads = []
            for place in range(0, pair_blocks, 2):
                both = dot(
                    grid_ref[place * high : (place + 2) * high, :],
                    turned_ref[:, place * block : (place + 2) * block],
                )
                grads += [both[:high, :block], both[high:, block:]]
            both = own_first(jnp.concatenate(grads, 0), parity).astype(narrow)
            size = both.shape[0] // 2
            for turn in range(2):
                start = (2 * turn + at) * size
                grads_ref[start : start + size, :] = both[turn * size : (turn + 1) * size]

    return body


def row_outputs(half):
    def body(*refs):
        jobs, col_refs, (*kept_refs, sent_ref, sum_ref) = (refs[:3], refs[3:6]), refs[6:8], refs[8:]
        add(*col_refs, sum_ref)
        parity = lax.axis_index("loop") % 2
        for at, (grid_ref, own_ref, weights_ref) in enumerate(jobs):
            kept_ref, features = kept_refs[at], own_ref.shape[0]
            pair_blocks = own_ref.shape[0] // half
            high = weights_ref.shape[0] // pair_blocks
            for place, block in enumerate(pair_blocks_of(parity, pair_blocks)):
                part = slice(place * high, (place + 1) * high)
                span = pl.ds(pl.multiple_of(block * half, half), half)
                branch = dot(weights_ref[part, :], grid_ref[part, :], 0, 0)
                kept_ref[span, :] = own_ref[span, :].astype(jnp.float32) + branch[:half]
                span = pl.ds(pl.multiple_of(at * features + block * half, half), half)
                sent_ref[span, :] = branch[half:].astype(jnp.bfloat16)

    return body


def add_partner(mixed_ref, grad_ref, got_ref, _, mixed_out, grad_out, done_ref):
    size = mixed_ref.shape[0]
    for at, (kept, out) in enumerate(((mixed_ref, mixed_out), (grad_ref, grad_out))):
        got = got_ref[at * size : (at + 1) * size, :].astype(jnp.float32)
        out[...] = (kept[...] + got).astype(out.dtype)
    done_ref[...] = jnp.zeros_like(done_ref)


def add(left_ref, right_ref, out_ref):
    total = left_ref[...].astype(jnp.float32) + right_ref[...].astype(jnp.float32)
    out_ref[...] = total.astype(out_ref.dtype)


def add_halves(left_ref, right_ref, kept_ref, *leave_refs):
    size = kept_ref.shape[0]
    for at, outs in enumerate(((kept_ref, leave_refs[0]), leave_refs[1:])):
        span = slice(at * size, (at + 1) * size)
        total = left_ref[span, :].astype(jnp.float32) + right_ref[span, :].astype(jnp.float32)
        for out in outs:
            out[...] = total.astype(out.dtype)


def place_parts(near_ref, far_ref, place_ref, at):
    size = near_ref.shape[0] // 2
    span = slice(at * size, (at + 1) * size)
    return dot(place_ref[...], jnp.concatenate([near_ref[span, :], far_ref[span, :]], 0))


def chip_grads(near_ref, far_ref, place_ref, out_ref):
    size = out_ref.shape[0] // 2
    for at in range(2):
        out_ref[at * size : (at + 1) * size, :] = place_parts(near_ref, far_ref, place_ref, at)


def total_grads(scale):
    def body(chip_ref, near_ref, far_ref, place_ref, _, *outs):
        size = outs[0].shape[0]
        for at, out in enumerate(outs):
            chip = chip_ref[at * size : (at + 1) * size, :]
            out[...] = (chip + place_parts(near_ref, far_ref, place_ref, at)) * scale

    return body


def total_col_grads(scale):
    def body(sum_ref, got_ref, take_up_ref, take_down_ref, up_ref, down_ref, done_ref):
        done_ref[...] = jnp.zeros_like(done_ref)
        size = take_up_ref.shape[0]
        count = up_ref.shape[0]
        for start in range(0, count, size):
            near = slice(start, start + size)
            far = slice(count + start, count + start + size)
            up = [dot(ref[near, :], take_up_ref[...]) for ref in (sum_ref, got_ref)]
            down = [dot(take_down_ref[...], ref[far, :], 0, 0) for ref in (sum_ref, got_ref)]
            up_ref[near, :] = (up[0] + up[1]) * scale
            down_ref[near, :] = (down[0] + down[1]) * scale

    return body


def exchange(bufs, axis, order):
    pairs = {q: [(s, s ^ (2 * q)) for s in range(2 * len(bufs))] for q in order}
    return [bufs[0]] + [lax.ppermute(bufs[q], axis, pairs[q]) for q in order]


def shards(tokens, cotangent, up_first, up_second, down_first, down_second, perm_up, perm_down):
    narrow = jnp.bfloat16
    wide = jnp.float32
    loops, dps = lax.axis_size("loop"), lax.axis_size("dp")
    feature_rows, toks = tokens.shape
    rows, all_cols, block = up_first.shape
    cols, size = up_second.shape[:2]
    half = block // 2
    pair_blocks = feature_rows // half
    if loops != 8 or dps != 4 or rows % 16 or pair_blocks % 2 or 2 * rows * cols * loops // 2 % (16 * pair_blocks):
        return plain_shards(
            tokens, cotangent, up_first, up_second, down_first, down_second, perm_up, perm_down
        )
    chips = loops // 2

    def struct(lead, width, dtype=narrow):
        return jax.ShapeDtypeStruct((lead, width), dtype)

    up_rows = up_first.reshape(rows * all_cols, block)
    down_rows = down_second.reshape(rows * all_cols, block)
    grid_rows = 2 * rows * chips * cols
    half_buf = struct(2 * rows * cols, toks)
    buf = struct(4 * rows * cols, toks)
    grid = struct(grid_rows, toks)
    half_grid = struct(grid_rows // 2, toks)
    taken = struct(grid_rows, block)
    full = struct(feature_rows, toks)
    take, order, order_back, place = call(
        tables(chips, rows, cols),
        [struct(rows * all_cols, rows * chips * cols)] + [struct(grid_rows, grid_rows)] * 3,
        micros=4,
    )
    other_x = from_partner(tokens, "loop", 0)
    other_up = from_partner(up_rows, "loop", 0)
    other_down = from_partner(down_rows, "loop", 0)
    leaving, other_up, other_down = lax.optimization_barrier((cotangent, other_up, other_down))
    other_d = from_partner(leaving, "loop", 0)

    *sent, up_taken, down_taken = call(
        token_rows(chips, half),
        [half_buf] * chips + [taken] * 2,
        tokens,
        other_x,
        up_rows,
        other_up,
        down_rows,
        other_down,
        take,
        order,
        scratch=[pltpu.VMEM(grid.shape, narrow)],
    )
    sent = call(
        cotangent_rows(chips, half),
        [buf] * chips,
        cotangent,
        other_d,
        down_taken,
        order,
        *sent,
        scratch=[pltpu.VMEM(grid.shape, narrow)],
    )
    cells = exchange(sent, "loop", FIRST_ORDER)
    square = struct(cols * size, size)
    *col_weights, take_up, take_down = call(
        column_weights(rows, cols),
        [square] * 4 + [struct(size, size)] * 2,
        up_second.reshape(square.shape),
        down_first.reshape(square.shape),
        perm_up.reshape(1, size),
        perm_down.reshape(1, size),
        sent[0],
        micros=2,
    )
    turned = struct(toks, 2 * feature_rows)
    (x_turned,) = call(turn_blocks(half), [turned], tokens, other_x, sent[0], micros=1)
    (d_turned,) = call(turn_blocks(half), [turned], cotangent, other_d, sent[0], micros=1)
    *sent, activated, grad_pre = call(
        columns(chips, rows, cols),
        [buf] * chips + [grid] * 2,
        *cells,
        *col_weights,
        x_turned,
        d_turned,
    )
    back = exchange(sent, "loop", BACK_ORDER)
    (col_grads,) = call(
        column_grads(chips, rows, cols),
        [struct(2 * cols * size, size)],
        *cells,
        activated,
        grad_pre,
    )

    def over_dp(value, apart):
        return lax.ppermute(value, "dp", [(s, s ^ apart) for s in range(dps)])

    sums, back_rows, grad_rows = call(
        row_grads(chips, rows, cols, half),
        [struct(2 * grid_rows, block), grid, grid],
        *back,
        x_turned,
        d_turned,
        order_back,
        col_grads,
    )
    sums_got = over_dp(sums, ROW_APART[0])
    partial = struct(feature_rows, toks, wide)
    both = struct(2 * feature_rows, toks)
    mixed, grad_tokens, branches, col_sum = call(
        row_outputs(half),
        [partial, partial, both, struct(*col_grads.shape)],
        back_rows,
        tokens,
        down_taken,
        grad_rows,
        cotangent,
        up_taken,
        col_grads,
        over_dp(col_grads, COL_APART[0]),
    )
    kept, to_next, to_other, to_core = call(add_halves, [taken] * 4, sums, sums_got)

    def to_partner(value, apart):
        pairs = [(s, s ^ (apart * loops + 1)) for s in range(dps * loops)]
        return lax.ppermute(value, ("dp", "loop"), pairs)

    got = {}
    got['c'] = to_partner(to_other, ROW_APART[1])
    got['z'] = over_dp(to_next, ROW_APART[1])
    got['p'] = from_partner(to_core, "loop", 0)
    (chip,) = call(
        chip_grads, [struct(2 * rows * all_cols, block, wide)], kept, got['p'], place
    )
    scale = 1.0 / math.sqrt(dps * toks)
    token = struct(8, 128, wide)
    g_up_second, g_down_first, done = call(
        total_col_grads(scale),
        [struct(*square.shape, wide)] * 2 + [token],
        col_sum,
        over_dp(col_sum, COL_APART[1]),
        take_up,
        take_down,
        to_hbm=2,
        micros=COL_MICROS,
    )
    mixed, grad_tokens, done = call(
        add_partner,
        [full] * 2 + [token],
        mixed,
        grad_tokens,
        from_partner(branches, "loop", 0),
        done,
        to_hbm=2,
    )
    g_up_first, g_down_second = call(
        total_grads(scale),
        [struct(rows * all_cols, block, wide)] * 2,
        chip,
        got['z'],
        got['c'],
        place,
        done,
        to_hbm=2,
    )
    return (
        mixed,
        grad_tokens,
        g_up_first.reshape(up_first.shape),
        g_up_second.reshape(up_second.shape),
        g_down_first.reshape(down_first.shape),
        g_down_second.reshape(down_second.shape),
    )


def solution(mesh):
    in_specs = (
        P("loop", "dp"),
        P("loop", "dp"),
        P("loop", None, None),
        P("loop", None, None),
        P("loop", None, None),
        P("loop", None, None),
        P(),
        P(),
    )
    out_specs = (
        P("loop", "dp"),
        P("loop", "dp"),
        P("loop", None, None),
        P("loop", None, None),
        P("loop", None, None),
        P("loop", None, None),
    )
    return jax.shard_map(shards, mesh=mesh, in_specs=in_specs, out_specs=out_specs, check_vma=False)
```
